128 devices in a mesh: batch: 32 (over x_hi, z, y), stream: 4 (over x_lo, core).
Axes of the slice: x: 4 (x_hi: 2, x_lo: 2; x = x_hi * 2 + x_lo), y: 4, z: 4, core: 2. Of those that a mesh axis runs over, the one named last changes fastest.
Arguments:
- tokens: bfloat16 [128, 256, 768], P('batch', 'stream'), may hold values from -6 to 6
- timestep: float32 [128], P('batch'), may hold values from 0 to 1000
- src_len: int32 [128], P('batch'), may hold values from 1 to 128, as said below
- total_len: int32 [128], P('batch'), may hold values from 2 to 256, as said below
- time_in: bfloat16 [128, 512], P(('batch', 'stream')), may hold values from -0.5 to 0.5
- time_bias: bfloat16 [512], P(('batch', 'stream')), may hold values from -3 to 3
- time_out: bfloat16 [512, 768], P(('batch', 'stream')), may hold values from -0.25 to 0.25
- qkv_weight: bfloat16 [2, 768, 2304], P(None, ('batch', 'stream')), may hold values from -0.21875 to 0.21875
- out_weight: bfloat16 [2, 768, 768], P(None, ('batch', 'stream')), may hold values from -2.5 to 2.5
- norm1_gain: bfloat16 [2, 768], P(None, ('batch', 'stream')), may hold values from 0.5 to 1.5
- norm1_bias: bfloat16 [2, 768], P(None, ('batch', 'stream')), may hold values from -2 to 2
- ffn_in: bfloat16 [2, 768, 3072], P(None, ('batch', 'stream')), may hold values from -0.21875 to 0.21875
- ffn_bias: bfloat16 [2, 3072], P(None, ('batch', 'stream')), may hold values from -2 to 2
- ffn_out: bfloat16 [2, 3072, 768], P(None, ('batch', 'stream')), may hold values from -0.109375 to 0.109375
- norm2_gain: bfloat16 [2, 768], P(None, ('batch', 'stream')), may hold values from 0.5 to 1.5
- norm2_bias: bfloat16 [2, 768], P(None, ('batch', 'stream')), may hold values from -2 to 2
- cotangent: bfloat16 [128, 256, 768], P('batch', 'stream'), may hold values from -6 to 6
Outputs:
- output: bfloat16 [128, 256, 768], P('batch', 'stream')
- grad_tokens: float32 [128, 256, 768], P('batch', 'stream')
- grad_time_in: float32 [128, 512], P(('batch', 'stream'))
- grad_time_bias: float32 [512], P(('batch', 'stream'))
- grad_time_out: float32 [512, 768], P(('batch', 'stream'))
- grad_qkv_weight: float32 [2, 768, 2304], P(None, ('batch', 'stream'))
- grad_out_weight: float32 [2, 768, 768], P(None, ('batch', 'stream'))
- grad_norm1_gain: float32 [2, 768], P(None, ('batch', 'stream'))
- grad_norm1_bias: float32 [2, 768], P(None, ('batch', 'stream'))
- grad_ffn_in: float32 [2, 768, 3072], P(None, ('batch', 'stream'))
- grad_ffn_bias: float32 [2, 3072], P(None, ('batch', 'stream'))
- grad_ffn_out: float32 [2, 3072, 768], P(None, ('batch', 'stream'))
- grad_norm2_gain: float32 [2, 768], P(None, ('batch', 'stream'))
- grad_norm2_bias: float32 [2, 768], P(None, ('batch', 'stream'))
The draws below stay inside these ranges and needn't reach their ends.
Inputs may be any that keep to these rules, and one draw needn't show every extreme that they name: total_len - src_len lies in 1 to 128; among the 4 sequences of each index of batch, one has src_len = 128. Among the 4 sequences of each index of batch, one has total_len = 256.
All inputs are finite; a program needn't handle non-finite values.
Results may differ from the reference program's by a relative error of at most 0.02.
Values may be sent and summed in bfloat16 or wider, within the bound.
A program may use at most 256 MiB of HBM per device.

```python
import math
import jax
import jax.numpy as jnp
from jax import lax

D = 768
HEADS = 12
FF = 3072
TIME_FREQ = 128
TIME_HID = 512
LAYERS = 2
SEG = 64
SEQ_DEV = 4
SEQS = 128
SLOT = 256


def lengths_pair(key):
    source_key, target_key, pick_key = jax.random.split(key, 3)
    source = jax.random.randint(source_key, (SEQS,), 1, 2 * SEG + 1)
    target = jax.random.randint(target_key, (SEQS,), 1, 2 * SEG + 1)
    chosen = jax.random.randint(pick_key, (SEQS // SEQ_DEV, 1), 0, SEQ_DEV)
    full_pick = (jnp.arange(SEQ_DEV)[None, :] == chosen).reshape(SEQS)
    source = jnp.where(full_pick, 2 * SEG, source)
    target = jnp.where(full_pick, 2 * SEG, target)
    return (source.astype(jnp.int32), (source + target).astype(jnp.int32))


def draw_src_len(key, part):
    return lengths_pair(key)[0]


def draw_total_len(key, part):
    return lengths_pair(key)[1]


def levels(stream_key, extent, cuts, least, largest):
    level = 1.0
    for axis_at, parts in cuts:
        draws = jax.random.uniform(jax.random.fold_in(jax.random.fold_in(stream_key, 6), axis_at), (parts,), jnp.float32, least / len(cuts), largest / len(cuts))
        level = level * jnp.repeat(jnp.exp(draws), extent[axis_at] // parts).reshape((-1,) + (1,) * (len(extent) - 1 - axis_at))
    return level


def gaussian(own_key, shape, scale, most, pieces=(), kind=jnp.bfloat16):
    loudness = levels(own_key, shape, pieces, -0.22, 0.18) if pieces else 1.0
    array = jax.random.normal(own_key, shape, jnp.float32) * scale * loudness
    return jnp.minimum(jnp.maximum(array, -most), most).astype(kind)


def setup_inputs(seed: int = 0) -> dict:
    arg_keys = jax.random.split(jax.random.key(seed), 18)
    return {
        "tokens": gaussian(arg_keys[0], (SEQS, SLOT, D), 1.0, 6.0, ((0, 32), (1, 4))),
        "timestep": jnp.clip(1000.0 * jax.random.uniform(arg_keys[1], (SEQS,), jnp.float32) ** levels(arg_keys[1], (SEQS,), ((0, 32),), -0.2, 0.2), 0.0, 1000.0),
        "src_len": draw_src_len(jax.random.fold_in(arg_keys[17], 71), 0),
        "total_len": draw_total_len(jax.random.fold_in(arg_keys[17], 71), 0),
        "time_in": gaussian(arg_keys[4], (TIME_FREQ, TIME_HID), TIME_FREQ ** -0.5, 0.5, ((0, 128),)),
        "time_bias": gaussian(arg_keys[5], (TIME_HID,), 0.5, 3.0, ((0, 128),)),
        "time_out": gaussian(arg_keys[6], (TIME_HID, D), TIME_HID ** -0.5, 0.25, ((0, 128),)),
        "qkv_weight": gaussian(arg_keys[7], (LAYERS, D, 3 * D), D ** -0.5, 0.21875, ((1, 128),)),
        "out_weight": gaussian(arg_keys[8], (LAYERS, D, D), (max(D // 128, 1)) ** -0.5, 2.5, ((1, 128),)),
        "norm1_gain": jnp.clip(1.0 + 0.1 * jax.random.normal(arg_keys[9], (LAYERS, D), jnp.float32), 0.5, 1.5).astype(jnp.bfloat16),
        "norm1_bias": gaussian(arg_keys[10], (LAYERS, D), 0.3, 2.0, ((1, 128),)),
        "ffn_in": gaussian(arg_keys[11], (LAYERS, D, FF), D ** -0.5, 0.21875, ((1, 128),)),
        "ffn_bias": gaussian(arg_keys[12], (LAYERS, FF), 0.3, 2.0, ((1, 128),)),
        "ffn_out": gaussian(arg_keys[13], (LAYERS, FF, D), FF ** -0.5, 0.109375, ((1, 128),)),
        "norm2_gain": jnp.clip(1.0 + 0.1 * jax.random.normal(arg_keys[14], (LAYERS, D), jnp.float32), 0.5, 1.5).astype(jnp.bfloat16),
        "norm2_bias": gaussian(arg_keys[15], (LAYERS, D), 0.3, 2.0, ((1, 128),)),
        "cotangent": gaussian(arg_keys[16], (SEQS, SLOT, D), 1.0, 6.0, ((0, 32), (1, 4))),
    }


@jax.custom_vjp
def low(v):
    return lax.optimization_barrier(v.astype(jnp.bfloat16)).astype(jnp.float32)

@jax.custom_vjp
def low_back(v):
    return v

def low_keep(v):
    return (low(v), None)

def low_pass(kept, grad):
    return (grad,)

def back_keep(v):
    return (v, None)

def back_low(kept, grad):
    return (low(grad),)
low.defvjp(low_keep, low_pass)
low_back.defvjp(back_keep, back_low)
EPS = 1e-05
highest = lax.Precision.HIGHEST

def matmul(left, right):
    return jnp.dot(left, right, precision=highest)

def sinusoid(timestep, feature_count):
    half_width = feature_count // 2
    frequency = jnp.exp(-math.log(10000.0) * jnp.arange(half_width).astype(timestep.dtype) / half_width)
    angles = timestep[:, None] * frequency[None, :]
    return jnp.concatenate([jnp.sin(angles), jnp.cos(angles)], axis=1)

def key_valid(key_rows, source_len, whole_len, half_slot):
    source_side = key_rows[None, :] < source_len[:, None]
    target_side = key_rows[None, :] - half_slot < (whole_len - source_len)[:, None]
    return jnp.where(key_rows[None, :] < half_slot, source_side, target_side)

def layer_norm(values, norm_gain, norm_shift):
    center = values - lax.optimization_barrier(jnp.mean(values, axis=-1, keepdims=True))
    spread = lax.optimization_barrier(jnp.mean(center * center, axis=-1, keepdims=True))
    return center * lax.rsqrt(spread + EPS) * norm_gain + norm_shift

def value_grad_low(values):
    return low(low_back(values))

def layer_apply(hidden_state, key_mask, layer_weights):
    qkv_w, out_w, gain_one, shift_one, in_w, in_bias, out_ffn, gain_two, shift_two = layer_weights
    group_count, slot_count, model_width = hidden_state.shape
    head_size = model_width // HEADS
    projected = value_grad_low(matmul(low(hidden_state), qkv_w))
    queries = projected[..., :model_width].reshape(group_count, slot_count, HEADS, head_size)
    key_split = projected[..., model_width:2 * model_width].reshape(group_count, slot_count, HEADS, head_size)
    value_split = projected[..., 2 * model_width:].reshape(group_count, slot_count, HEADS, head_size)
    scores = jnp.einsum('gqhd,gkhd->ghqk', queries, key_split, precision=highest) * head_size ** (-0.5)
    scores = low_back(scores)
    full_mask = key_mask[:, None, None, :]
    masked = jnp.where(full_mask, scores, -1e+30)
    row_max = lax.optimization_barrier(jnp.max(masked, axis=-1, keepdims=True))
    exp_scores = jnp.where(full_mask, jnp.exp(masked - row_max), 0.0)
    soft_low = low(exp_scores / lax.optimization_barrier(jnp.sum(exp_scores, axis=-1, keepdims=True)))
    mixed_heads = jnp.einsum('ghqk,gkhd->gqhd', soft_low, value_split, precision=highest)
    mixed_heads = value_grad_low(mixed_heads.reshape(group_count, slot_count, model_width))
    attended = low_back(matmul(mixed_heads, out_w))
    first_norm = layer_norm(hidden_state + attended, gain_one, shift_one)
    ffn_pre = low_back(matmul(low(first_norm), in_w) + in_bias)
    act_low = low(jax.nn.gelu(ffn_pre, approximate=False))
    branch = low_back(matmul(act_low, out_ffn))
    return layer_norm(first_norm + branch, gain_two, shift_two)

def group_apply(params, inputs):
    token_rows, step_values, source_len, whole_len = inputs
    time_w_in, time_b, time_w_out = (params[0], params[1], params[2])
    emb_low = low(sinusoid(step_values, TIME_FREQ))
    time_act = jax.nn.silu(matmul(emb_low, time_w_in) + time_b)
    temb = matmul(low(time_act), time_w_out)
    hidden_state = token_rows + temb[:, None, :]
    key_mask = key_valid(jnp.arange(SLOT, dtype=jnp.int32), source_len, whole_len, SLOT // 2)
    for layer_index in range(LAYERS):
        layer_weights = tuple((member[layer_index] for member in params[3:]))
        hidden_state = layer_apply(hidden_state, key_mask, layer_weights)
    return hidden_state

def reference(tokens, timestep, src_len, total_len, time_in, time_bias, time_out, qkv_weight, out_weight, norm1_gain, norm1_bias, ffn_in, ffn_bias, ffn_out, norm2_gain, norm2_bias, cotangent):
    params = tuple((member.astype(jnp.float32) for member in (time_in, time_bias, time_out, qkv_weight, out_weight, norm1_gain, norm1_bias, ffn_in, ffn_bias, ffn_out, norm2_gain, norm2_bias)))
    tokens_f = tokens.astype(jnp.float32)
    group_size = math.gcd(SEQS, max(1, 4096 // SLOT))
    group_count = SEQS // group_size

    def forward(param_set, token_values):
        inputs = (token_values.reshape(group_count, group_size, SLOT, D), timestep.reshape(group_count, group_size), src_len.reshape(group_count, group_size), total_len.reshape(group_count, group_size))
        results = lax.map(jax.checkpoint(lambda piece: group_apply(param_set, piece)), inputs)
        return results.reshape(SEQS, SLOT, D)
    final, pullback = jax.vjp(forward, params, tokens_f)
    param_grads, grad_tokens = pullback(cotangent.astype(jnp.float32))
    return (final.astype(jnp.bfloat16), grad_tokens, param_grads[0], param_grads[1], param_grads[2], param_grads[3], param_grads[4], param_grads[5], param_grads[6], param_grads[7], param_grads[8], param_grads[9], param_grads[10], param_grads[11])
```

```python
from functools import partial
import math

import jax
import jax.numpy as jnp
from jax import lax
from jax.experimental import pallas as pl
from jax.experimental.pallas import tpu as pltpu
from jax.sharding import PartitionSpec as P

F32, BF16 = jnp.float32, jnp.bfloat16
EPS = 1e-05
NN = (((1,), (0,)), ((), ()))
NT = (((1,), (1,)), ((), ()))
TN = (((0,), (0,)), ((), ()))
VMEM_BYTES = 60 * 1024 * 1024
PART_AXES = ("zyx", "xzy", "yxz")


def dot(left, right, dims=NN):
    return lax.dot_general(left, right, dims, preferred_element_type=F32)


def place(part, core, x, y, z, k):
    at = {"x": x, "y": y, "z": z}
    return (core,) + tuple(at[name] for name in PART_AXES[part]) + (k,)


def split_tile(tile):
    return lax.div(tile, 4), lax.rem(lax.div(tile, 2), 2), lax.rem(tile, 2)


GROUPS = [(x_hi, z, y_hi) for x_hi in range(2) for z in range(4) for y_hi in range(2)]


def read_tile(weights, part, tile):
    k, y_lo, x_lo = split_tile(tile)
    return jnp.concatenate(
        [
            jnp.concatenate(
                [
                    weights[(part,) + place(part, core, 2 * x_hi + x_lo, 2 * y_hi + y_lo, z, k)]
                    for x_hi, z, y_hi in GROUPS
                ],
                axis=0,
            )
            for core in range(2)
        ],
        axis=1,
    )


def write_tile(grads, part, tile, values):
    k, y_lo, x_lo = split_tile(tile)
    for at, (x_hi, z, y_hi) in enumerate(GROUPS):
        for core in range(2):
            grads[(part,) + place(part, core, 2 * x_hi + x_lo, 2 * y_hi + y_lo, z, k)] = values[
                48 * at : 48 * at + 48, 128 * core : 128 * core + 128
            ]


def read_rows(weights, step, columns):
    x_hi, z = lax.div(step, 4), lax.rem(step, 4)
    return jnp.concatenate(
        [
            jnp.concatenate(
                [
                    weights[(2,) + place(2, column // 3, 2 * x_hi + x_lo, y, z, column % 3)]
                    for y in range(4)
                    for x_lo in range(2)
                ],
                axis=0,
            )
            for column in columns
        ],
        axis=1,
    )


def write_rows(grads, step, values):
    x_hi, z = lax.div(step, 4), lax.rem(step, 4)
    for y in range(4):
        for x_lo in range(2):
            at = 48 * (2 * y + x_lo)
            for column in range(6):
                grads[(2,) + place(2, column // 3, 2 * x_hi + x_lo, y, z, column % 3)] = values[
                    at : at + 48, 128 * column : 128 * column + 128
                ]


def chunks_of(ref, first, count):
    return jnp.concatenate([ref[first + at] for at in range(count)], axis=1)


def normalize(values):
    center = values - jnp.mean(values, axis=-1, keepdims=True)
    scale = lax.rsqrt(jnp.mean(center * center, axis=-1, keepdims=True) + EPS)
    return center * scale, scale


def normalize_back(grad, gain, normal, scale):
    grad_normal = grad * gain
    mean_one = jnp.mean(grad_normal, axis=-1, keepdims=True)
    mean_two = jnp.mean(grad_normal * normal, axis=-1, keepdims=True)
    return scale * (grad_normal - mean_one - normal * mean_two)


def half_masks():
    lane = lax.broadcasted_iota(jnp.int32, (1, 128), 1)
    first = jnp.where(lane < 64, 1.0, 0.0)
    return first.astype(BF16), (1.0 - first).astype(BF16)


def load_weights(layer, weights_hbm, weights, sems):
    copies = [
        pltpu.make_async_copy(weights_hbm.at[part, layer], weights.at[part], sems.at[part])
        for part in range(3)
    ]
    for copy in copies:
        copy.start()
    return copies


def forward_kernel(
    layer,
    lens,
    x_ref,
    norms,
    bias,
    weights_hbm,
    y_ref,
    proj,
    soft,
    mixed,
    normal1,
    scale1,
    first_low,
    act,
    slope,
    normal2,
    scale2,
    weights,
    acc,
    sems,
):
    copies = load_weights(layer, weights_hbm, weights, sems)
    x_low = x_ref[...].astype(BF16)
    copies[0].wait()

    def project(tile, carry):
        out = dot(x_low, read_tile(weights, 0, tile)).astype(BF16)
        proj[2 * tile] = out[:, :128]
        proj[2 * tile + 1] = out[:, 128:]
        return carry

    lax.fori_loop(0, 9, project, 0)

    key_at = lax.broadcasted_iota(jnp.int32, (1, 256), 1)
    bound = jnp.where(key_at < 128, lens[0], 128 + lens[1] - lens[0])
    shut = jnp.where(key_at < bound, 0.0, -1e30)
    low_half = lax.broadcasted_iota(jnp.int32, (256, 128), 1) < 64
    halves = half_masks()

    def attend(pair, carry):
        queries = proj[pair] * jnp.asarray(0.125, BF16)
        keys = proj[6 + pair]
        values = proj[12 + pair]
        outs = []
        for side in range(2):
            scores = dot(queries * halves[side], keys, NT) + shut
            top = jnp.max(scores, axis=-1, keepdims=True)
            exps = jnp.exp(scores - top)
            low = (exps * (1.0 / jnp.sum(exps, axis=-1, keepdims=True))).astype(BF16)
            soft[2 * pair + side] = low
            outs.append(dot(low, values))
        mixed[pair] = jnp.where(low_half, outs[0], outs[1]).astype(BF16)
        return carry

    lax.fori_loop(0, 6, attend, 0)

    mixed_all = chunks_of(mixed, 0, 6)
    for tile in range(3):
        acc[:, 256 * tile : 256 * tile + 256] = dot(mixed_all, read_tile(weights, 0, 9 + tile))
    normal, scale = normalize(x_ref[...] + acc[...])
    normal1[...] = normal
    scale1[...] = scale
    first = normal * norms[0:1, :] + norms[1:2, :]
    acc[...] = first
    first_low[...] = first.astype(BF16)
    copies[1].wait()

    def feed(tile, carry):
        columns = pl.ds(pl.multiple_of(256 * tile, 256), 256)
        pre = dot(first_low[...], read_tile(weights, 1, tile)) + bias[0:1, columns]
        cdf = 0.5 * (1.0 + lax.erf(pre * math.sqrt(0.5)))
        out = (pre * cdf).astype(BF16)
        grad = (cdf + pre * (jnp.exp(-0.5 * pre * pre) * (1.0 / math.sqrt(2 * math.pi)))).astype(BF16)
        act[2 * tile] = out[:, :128]
        act[2 * tile + 1] = out[:, 128:]
        slope[2 * tile] = grad[:, :128]
        slope[2 * tile + 1] = grad[:, 128:]
        return carry

    lax.fori_loop(0, 12, feed, 0)
    copies[2].wait()

    def unfeed(step, carry):
        rows = chunks_of(act, 3 * step, 3)
        acc[...] += dot(rows, read_rows(weights, step, range(6)))
        return carry

    lax.fori_loop(0, 8, unfeed, 0)
    normal, scale = normalize(acc[...])
    normal2[...] = normal
    scale2[...] = scale
    y_ref[...] = normal * norms[2:3, :] + norms[3:4, :]


SAVED = (
    ((18, 256, 128), BF16),
    ((12, 256, 256), BF16),
    ((6, 256, 128), BF16),
    ((256, 768), F32),
    ((256, 1), F32),
    ((256, 768), BF16),
    ((24, 256, 128), BF16),
    ((24, 256, 128), BF16),
    ((256, 768), F32),
    ((256, 1), F32),
)
PART = (2, 4, 4, 4, 3, 48, 128)


def forward(layer, lens, x, norms, bias, weights, interpret=False):
    vmem, anywhere = pl.BlockSpec(memory_space=pltpu.VMEM), pl.BlockSpec(memory_space=pl.ANY)
    return pl.pallas_call(
        partial(forward_kernel, layer),
        out_shape=[jax.ShapeDtypeStruct((256, 768), F32)]
        + [jax.ShapeDtypeStruct(shape, kind) for shape, kind in SAVED],
        in_specs=[pl.BlockSpec(memory_space=pltpu.SMEM), vmem, vmem, vmem, anywhere],
        out_specs=[vmem] * (1 + len(SAVED)),
        scratch_shapes=[
            pltpu.VMEM((3,) + PART, BF16),
            pltpu.VMEM((256, 768), F32),
            pltpu.SemaphoreType.DMA((3,)),
        ],
        compiler_params=pltpu.CompilerParams(vmem_limit_bytes=VMEM_BYTES),
        interpret=interpret,
        name="forward",
    )(lens, x, norms, bias, weights)


def backward_kernel(
    layer,
    grad_ref,
    x_ref,
    norms,
    proj,
    soft,
    mixed,
    normal1,
    scale1,
    first_low,
    act,
    slope,
    normal2,
    scale2,
    weights_hbm,
    grad_x,
    grads_hbm,
    grad_norms,
    grad_bias,
    weights,
    grads,
    acc,
    grad_pre,
    grad_proj,
    grad_mixed,
    sems,
    out_sems,
):
    copies = load_weights(layer, weights_hbm, weights, sems)
    sends = [
        pltpu.make_async_copy(grads.at[part], grads_hbm.at[part], out_sems.at[part])
        for part in range(3)
    ]
    grad = grad_ref[...]
    normal = normal2[...]
    grad_norms[2:3, :] = jnp.sum(grad * normal, axis=0, keepdims=True)
    grad_norms[3:4, :] = jnp.sum(grad, axis=0, keepdims=True)
    acc[...] = normalize_back(grad, norms[2:3, :], normal, scale2[...])
    branch = acc[...].astype(BF16)
    copies[2].wait()

    def unfeed(step, carry):
        grad_act = dot(branch, read_rows(weights, step, range(6)), NT)
        pre_low = (grad_act * chunks_of(slope, 3 * step, 3).astype(F32)).astype(BF16)
        for at in range(3):
            grad_pre[3 * step + at] = pre_low[:, 128 * at : 128 * at + 128]
            chunk_sum = jnp.sum(pre_low[:, 128 * at : 128 * at + 128].astype(F32), axis=0, keepdims=True)
            grad_bias[pl.ds(3 * step + at, 1), :] = chunk_sum
        rows = chunks_of(act, 3 * step, 3)
        write_rows(grads, step, dot(rows, branch, TN).astype(BF16))
        return carry

    lax.fori_loop(0, 8, unfeed, 0)
    sends[2].start()
    copies[1].wait()

    def feed(tile, carry):
        pre_low = chunks_of(grad_pre, 2 * tile, 2)
        acc[...] += dot(pre_low, read_tile(weights, 1, tile), NT)
        write_tile(grads, 1, tile, dot(first_low[...], pre_low, TN).astype(BF16))
        return carry

    lax.fori_loop(0, 12, feed, 0)
    sends[1].start()

    grad = acc[...]
    normal = normal1[...]
    grad_norms[0:1, :] = jnp.sum(grad * normal, axis=0, keepdims=True)
    grad_norms[1:2, :] = jnp.sum(grad, axis=0, keepdims=True)
    grad_norms[4:8, :] = jnp.zeros((4, 768), F32)
    acc[...] = normalize_back(grad, norms[0:1, :], normal, scale1[...])
    attended = acc[...].astype(BF16)
    copies[0].wait()
    mixed_all = chunks_of(mixed, 0, 6)
    total = jnp.zeros((256, 768), F32)
    for tile in range(3):
        part_low = attended[:, 256 * tile : 256 * tile + 256]
        total += dot(part_low, read_tile(weights, 0, 9 + tile), NT)
        write_tile(grads, 0, 9 + tile, dot(mixed_all, part_low, TN).astype(BF16))
    for chunk in range(6):
        grad_mixed[chunk] = total[:, 128 * chunk : 128 * chunk + 128].astype(BF16)

    low_half = lax.broadcasted_iota(jnp.int32, (256, 128), 1) < 64
    halves = half_masks()

    def attend(pair, carry):
        queries, keys, values = proj[pair], proj[6 + pair], proj[12 + pair]
        back = grad_mixed[pair]
        grads_q, grads_k, grads_v = [], [], []
        for side in range(2):
            low = soft[2 * pair + side]
            weight = low.astype(F32)
            grad_soft = dot(back * halves[side], values, NT)
            inner = jnp.sum(weight * grad_soft, axis=-1, keepdims=True)
            grad_score = (weight * (grad_soft - inner) * 0.125).astype(BF16)
            grads_q.append(dot(grad_score, keys))
            grads_k.append(dot(grad_score, queries, TN))
            grads_v.append(dot(low, back, TN))
        for first, both in ((0, grads_q), (6, grads_k), (12, grads_v)):
            grad_proj[first + pair] = jnp.where(low_half, both[0], both[1]).astype(BF16)
        return carry

    lax.fori_loop(0, 6, attend, 0)
    x_low = x_ref[...].astype(BF16)

    def project(tile, carry):
        pair = chunks_of(grad_proj, 2 * tile, 2)
        acc[...] += dot(pair, read_tile(weights, 0, tile), NT)
        write_tile(grads, 0, tile, dot(x_low, pair, TN).astype(BF16))
        return carry

    lax.fori_loop(0, 9, project, 0)
    sends[0].start()
    grad_x[...] = acc[...]
    for send in sends:
        send.wait()


def backward(layer, grad, x, norms, saved, weights, interpret=False):
    vmem, anywhere = pl.BlockSpec(memory_space=pltpu.VMEM), pl.BlockSpec(memory_space=pl.ANY)
    return pl.pallas_call(
        partial(backward_kernel, layer),
        out_shape=[
            jax.ShapeDtypeStruct((256, 768), F32),
            jax.ShapeDtypeStruct((3,) + PART, BF16),
            jax.ShapeDtypeStruct((8, 768), F32),
            jax.ShapeDtypeStruct((24, 128), F32),
        ],
        in_specs=[vmem] * (3 + len(SAVED)) + [anywhere],
        out_specs=[vmem, anywhere, vmem, vmem],
        scratch_shapes=[
            pltpu.VMEM((3,) + PART, BF16),
            pltpu.VMEM((3,) + PART, BF16),
            pltpu.VMEM((256, 768), F32),
            pltpu.VMEM((24, 256, 128), BF16),
            pltpu.VMEM((18, 256, 128), BF16),
            pltpu.VMEM((6, 256, 128), BF16),
            pltpu.SemaphoreType.DMA((3,)),
            pltpu.SemaphoreType.DMA((3,)),
        ],
        compiler_params=pltpu.CompilerParams(vmem_limit_bytes=VMEM_BYTES),
        interpret=interpret,
        name="backward",
    )(grad, x, norms, *saved, weights)


MESH = pl.DeviceIdType.MESH
LINKS = 17


def here():
    batch, stream = lax.axis_index("batch"), lax.axis_index("stream")
    return {
        "x": 2 * lax.div(batch, 16) + lax.div(stream, 2),
        "y": lax.rem(batch, 4),
        "z": lax.rem(lax.div(batch, 4), 4),
        "core": lax.rem(stream, 2),
    }


def device(at):
    return (
        lax.div(at["x"], 2) * 16 + at["z"] * 4 + at["y"],
        lax.rem(at["x"], 2) * 2 + at["core"],
    )


def moved(at, axis, by):
    return {**at, axis: lax.rem(at[axis] + by + 4, 4)}


def flipped(at, flip_y, flip_x, flip_core):
    new = dict(at)
    if flip_y:
        new["y"] = at["y"] + 1 - 2 * lax.rem(at["y"], 2)
    if flip_x:
        new["x"] = at["x"] + 1 - 2 * lax.rem(at["x"], 2)
    if flip_core:
        new["core"] = 1 - at["core"]
    return new


def member(at):
    return lax.rem(at["y"], 2) * 4 + lax.rem(at["x"], 2) * 2 + at["core"]


def stream_of(at):
    return lax.rem(at["x"], 2) * 2 + at["core"]


FLIPS = [(flip // 4, flip // 2 % 2, flip % 2) for flip in range(1, 8)]


def greet(at):
    partners = [flipped(at, *flip) for flip in FLIPS]
    partners += [moved(at, "z", 1), moved(at, "z", -1)]
    partners += [moved(at, axis, 2 * lax.rem(at[axis], 2) - 1) for axis in "xy"]
    barrier = pltpu.get_barrier_semaphore()
    for partner in partners:
        pl.semaphore_signal(barrier, inc=1, device_id=device(partner), device_id_type=MESH)
    pl.semaphore_wait(barrier, len(partners))


def remote(src, dst, send_sem, recv_sem, to):
    return pltpu.make_async_remote_copy(
        src_ref=src,
        dst_ref=dst,
        send_sem=send_sem,
        recv_sem=recv_sem,
        device_id=device(to),
        device_id_type=MESH,
    )


class Spread:
    def __init__(self, number, base, own, axes, at, sems, cut):
        self.base, self.own, self.at, self.cut = base.at[at["core"]], own, at, cut
        self.axes = axes[::-1]
        self.place = [at[axis] for axis in axes]
        self.send_sems, self.recv_sems, self.local_sem = sems
        self.number, self.copies = number, {}

    def block(self, phase, by):
        c, b, a = self.place
        turn = lambda index: lax.rem(index + by + 4, 4)
        if phase == 0:
            return self.base.at[c, b, turn(a)]
        if phase == 1:
            return self.base.at[c, turn(b)]
        return self.base.at[turn(c)]

    def half(self, phase, ref, second):
        cut, size = (self.cut, ref.shape[0]) if phase == 0 else (2, 4)
        return ref.at[pl.ds(cut, size - cut)] if second else ref.at[pl.ds(0, cut)]

    def send(self, slot, src, dst, to):
        copy = remote(
            src, dst, self.send_sems.at[self.number, slot], self.recv_sems.at[self.number, slot], to
        )
        copy.start()
        self.copies[slot] = copy

    def out(self, phase):
        axis = self.axes[phase]
        mine = self.block(phase, 0)
        src = self.own if phase == 0 else mine
        self.send(4 * phase, src, mine, moved(self.at, axis, 1))
        self.send(4 * phase + 1, src, mine, moved(self.at, axis, -1))

    def share(self, slot, ref):
        self.send(slot, ref, ref, flipped(self.at, 0, 0, 1))

    def forward(self, phase):
        axis = self.axes[phase]
        for side, by in ((0, -1), (1, 1)):
            self.copies[4 * phase + side].wait_recv()
            came = self.block(phase, by)
            piece = self.half(phase, came, side == 1)
            self.send(4 * phase + 2 + side, piece, piece, moved(self.at, axis, -by))
            if phase == 2:
                self.share(13 + side, came)

    def close(self, phase):
        for side in range(2):
            self.copies[4 * phase + 2 + side].wait_recv()
            if phase == 2:
                piece = self.half(phase, self.block(phase, 2), side == 1)
                self.share(15 + side, piece)

    def step(self, turn):
        if turn == 0:
            self.keep = pltpu.make_async_copy(
                self.own, self.block(0, 0), self.local_sem.at[self.number]
            )
            self.keep.start()
            self.out(0)
        elif turn == 2:
            self.close(0)
            self.keep.wait()
            self.out(1)
        elif turn == 4:
            self.close(1)
            self.out(2)
            self.share(12, self.block(2, 0))
        elif turn == 6:
            self.close(2)
        elif turn in (1, 3, 5):
            self.forward(turn // 2)

    def finish(self):
        for slot, copy in self.copies.items():
            copy.wait_send()
            if slot >= 12:
                copy.wait_recv()


def gather_kernel(
    qkv,
    out_w,
    ffn_in,
    ffn_out,
    time_in,
    time_out,
    small,
    tokens,
    cotangent,
    weights,
    extra,
    tokens_all,
    cotangent_all,
    send_a,
    recv_a,
    send_b,
    recv_b,
    rows,
    rows_b,
    units,
    unit_extra,
    send_sems,
    recv_sems,
    local_sems,
    first_send,
    first_recv,
    token_send,
    token_recv,
    token_local,
):
    at = here()
    mine, core = member(at), at["core"]
    my_stream = stream_of(at)
    greet(at)
    token_copies = []
    for number, (src, dst) in enumerate(((tokens, tokens_all), (cotangent, cotangent_all))):
        to_rows = dst.at[pl.ds(pl.multiple_of(64 * my_stream, 64), 64)]
        keep = pltpu.make_async_copy(src.at[my_stream], to_rows, token_local.at[number])
        keep.start()
        token_copies.append(keep)
        for flip in range(1, 4):
            to = flipped(at, 0, flip // 2, flip % 2)
            sems = token_send.at[number, flip - 1], token_recv.at[number, flip - 1]
            copy = remote(src.at[stream_of(to)], to_rows, *sems, to)
            copy.start()
            token_copies.append(copy)

    for to in range(8):
        for layer in range(2):
            for k in range(6):
                chunk = to + 8 * (k % 3)
                if k >= 3:
                    piece = ffn_in[layer, :, 128 * chunk : 128 * chunk + 128]
                elif chunk < 18:
                    piece = qkv[layer, :, 128 * chunk : 128 * chunk + 128]
                else:
                    piece = out_w[layer, :, 128 * (chunk - 18) : 128 * (chunk - 18) + 128]
                send_a[to, 6 * layer + k, 0:6, :] = piece.astype(F32)
        send_a[to, 12] = jnp.zeros((8, 128), F32)
        if to < 6:
            send_a[to, 12, 0:4, :] = time_out[:, 128 * to : 128 * to + 128].astype(F32)
        elif to == 6:
            for chunk in range(4):
                send_a[to, 12, chunk : chunk + 1, :] = time_in[
                    :, 128 * chunk : 128 * chunk + 128
                ].astype(F32)
        else:
            send_a[to, 12, 0:1, :] = small[...]
    for layer in range(2):
        for k in range(3):
            column = pl.multiple_of(128 * (3 * (1 - core) + k), 128)
            send_b[layer, k] = ffn_out[layer, :, pl.ds(column, 128)].astype(F32)
    first = []
    for number, flip in enumerate(FLIPS):
        to = flipped(at, *flip)
        copy = remote(
            send_a.at[member(to)], recv_a.at[mine], first_send.at[number], first_recv.at[number], to
        )
        copy.start()
        first.append(copy)
    copy = remote(send_b, recv_b, first_send.at[7], first_recv.at[7], flipped(at, 0, 0, 1))
    copy.start()
    first.append(copy)
    recv_a[mine] = send_a[mine]
    for copy in first:
        copy.wait_recv()

    streams = []
    for layer in range(2):
        for part in range(3):
            for k in range(3):
                if part < 2:
                    for frm in range(8):
                        rows[6 * frm : 6 * frm + 6, :] = recv_a[
                            frm, 6 * layer + 3 * part + k, 0:6, :
                        ]
                    units[part, layer, k] = rows[...].astype(BF16)
                else:
                    column = pl.multiple_of(128 * (3 * core + k), 128)
                    rows_b[core] = ffn_out[layer, :, pl.ds(column, 128)].astype(F32)
                    rows_b[1 - core] = recv_b[layer, k]
                    units[part, layer, k, 0:48, :] = rows_b[...].reshape(48, 128).astype(BF16)
            streams.append(
                Spread(
                    3 * layer + part,
                    weights.at[part, layer],
                    units.at[part, layer],
                    PART_AXES[part],
                    at,
                    (send_sems, recv_sems, local_sems),
                    2,
                )
            )
            if layer == 0:
                streams[-1].step(0)
        if layer == 0:
            for frm in range(8):
                rows[4 * frm : 4 * frm + 4, :] = recv_a[frm, 12, 0:4, :]
            unit_extra[...] = rows[0:32, :].astype(BF16)
            streams.append(
                Spread(6, extra, unit_extra, "zyx", at, (send_sems, recv_sems, local_sems), 16)
            )
            streams[-1].step(0)
    for turn in range(1, 9):
        for number, stream in enumerate(streams):
            stream.step(turn - (2 if number > 3 else 0))
    for stream in streams:
        stream.finish()
    for copy in first:
        copy.wait_send()
    for copy in token_copies:
        copy.wait()


def gather(qkv, out_w, ffn_in, ffn_out, time_in, time_out, small, tokens, cotangent):
    vmem, anywhere = pl.BlockSpec(memory_space=pltpu.VMEM), pl.BlockSpec(memory_space=pl.ANY)
    dma = pltpu.SemaphoreType.DMA
    return pl.pallas_call(
        gather_kernel,
        out_shape=[
            jax.ShapeDtypeStruct((3, 2) + PART, BF16),
            jax.ShapeDtypeStruct((2, 4, 4, 4, 32, 128), BF16),
            jax.ShapeDtypeStruct((256, 768), BF16),
            jax.ShapeDtypeStruct((256, 768), BF16),
        ],
        in_specs=[vmem] * 7 + [anywhere] * 2,
        out_specs=[anywhere] * 4,
        scratch_shapes=[
            pltpu.VMEM((8, 13, 8, 128), F32),
            pltpu.VMEM((8, 13, 8, 128), F32),
            pltpu.VMEM((2, 3, 24, 128), F32),
            pltpu.VMEM((2, 3, 24, 128), F32),
            pltpu.VMEM((48, 128), F32),
            pltpu.VMEM((2, 24, 128), F32),
            pltpu.VMEM((3, 2, 3, 48, 128), BF16),
            pltpu.VMEM((32, 128), BF16),
            dma((7, LINKS)),
            dma((7, LINKS)),
            dma((7,)),
            dma((8,)),
            dma((8,)),
            dma((2, 3)),
            dma((2, 3)),
            dma((2,)),
        ],
        compiler_params=pltpu.CompilerParams(
            collective_id=1, has_side_effects=True, vmem_limit_bytes=VMEM_BYTES
        ),
        name="gather_weights",
    )(qkv, out_w, ffn_in, ffn_out, time_in, time_out, small, tokens, cotangent)


class Reduce:
    def __init__(self, number, grads, own, twin, halves, fulls, axes, at, sems, cut):
        self.grads, self.own, self.twin, self.at, self.cut = grads, own, twin, at, cut
        self.halves, self.fulls = halves, fulls
        self.axes = axes
        self.place = [at[axis] for axis in axes]
        self.send_sems, self.recv_sems, self.local_sem = sems
        self.number, self.copies = number, {}

    def send(self, slot, src, dst, to):
        copy = remote(
            src, dst, self.send_sems.at[self.number, slot], self.recv_sems.at[self.number, slot], to
        )
        copy.start()
        self.copies[slot] = copy

    def turn(self, phase, by):
        return lax.rem(self.place[phase] + by + 4, 4)

    def load(self):
        core = self.at["core"]
        self.keep = pltpu.make_async_copy(self.grads.at[core], self.own, self.local_sem.at[self.number])
        self.keep.start()

    def trade(self, slot, by):
        plane = self.turn(0, by)
        self.send(
            12 + slot,
            self.grads.at[1 - self.at["core"], plane],
            self.twin.at[plane],
            flipped(self.at, 0, 0, 1),
        )

    def meet(self, slot, by):
        self.copies[12 + slot].wait_recv()
        plane = self.turn(0, by)

        def add(line, carry):
            self.own[plane, line] = self.own[plane, line] + self.twin[plane, line]
            return carry

        lax.fori_loop(0, 4, add, 0)

    def block(self, phase, by):
        at = self.turn(phase, by)
        if phase == 0:
            return (at,)
        if phase == 1:
            return (self.place[0], at)
        return (self.place[0], self.place[1], at)

    def cuts(self, phase):
        if phase < 2:
            return (0, 2), (2, 2)
        size = self.own.shape[3]
        return (0, self.cut), (self.cut, size - self.cut)

    def begin(self, phase):
        opposite = self.block(phase, 2)
        for side, by in ((0, 1), (1, -1)):
            start, size = self.cuts(phase)[side]
            self.send(
                4 * phase + side,
                self.own.at[opposite + (pl.ds(start, size),)],
                self.halves[phase][side],
                moved(self.at, self.axes[phase], by),
            )

    def add_piece(self, index, start, size, piece):
        def add(line, carry):
            self.own[index + (start + line,)] = self.own[index + (start + line,)] + piece[line]
            return carry

        if len(index) < 3:
            lax.fori_loop(0, size, add, 0)
        else:
            rows = index + (pl.ds(start, size),)
            self.own[rows] = self.own[rows] + piece[...]

    def pass_on(self, phase):
        for side, by in ((0, 1), (1, -1)):
            self.copies[4 * phase + side].wait_recv()
            start, size = self.cuts(phase)[side]
            block = self.block(phase, by)
            self.add_piece(block, start, size, self.halves[phase][side])
            self.send(
                4 * phase + 2 + side,
                self.own.at[block],
                self.fulls[phase].at[side],
                moved(self.at, self.axes[phase], by),
            )

    def settle(self, phase, result=None):
        for side in range(2):
            self.copies[4 * phase + 2 + side].wait_recv()
        block = self.block(phase, 0)
        full = self.fulls[phase]
        if phase == 2:
            result[...] = (
                self.own[block].astype(F32) + full[0].astype(F32) + full[1].astype(F32)
            )
            return

        def add(line, carry):
            index = block + (line,)
            total = self.own[index].astype(F32) + full[0, line].astype(F32)
            self.own[index] = (total + full[1, line].astype(F32)).astype(BF16)
            return carry

        lax.fori_loop(0, 4, add, 0)

    def step(self, turn, result):
        if turn == 0:
            self.keep.wait()
            self.meet(0, 2)
            self.begin(0)
        elif turn == 1:
            self.meet(1, 1)
            self.meet(2, -1)
            self.pass_on(0)
        elif turn == 2:
            self.meet(3, 0)
            self.settle(0)
            self.begin(1)
        elif turn == 3:
            self.pass_on(1)
        elif turn == 4:
            self.settle(1)
            self.begin(2)
        elif turn == 5:
            self.pass_on(2)
        elif turn == 6:
            self.settle(2, result)

    def finish(self):
        for copy in self.copies.values():
            copy.wait_send()


def scatter_kernel(
    grads,
    extra,
    output,
    grad_x,
    got_a,
    got_b,
    kept_b,
    output_part,
    grad_part,
    own,
    twin,
    half_0,
    full_0,
    half_1,
    full_1,
    half_2,
    full_2,
    own_x,
    twin_x,
    half_0x,
    full_0x,
    half_1x,
    full_1x,
    half_2x,
    full_2x,
    result,
    result_x,
    send_a,
    send_b,
    send_sems,
    recv_sems,
    local_sems,
    first_send,
    first_recv,
    token_send,
    token_recv,
    token_local,
):
    at = here()
    mine, core = member(at), at["core"]
    my_stream = stream_of(at)
    sems = (send_sems, recv_sems, local_sems)
    streams, results = [], []
    for layer in (1, 0):
        for part in range(3):
            where = (part, layer)
            streams.append(
                Reduce(
                    3 * layer + part,
                    grads[layer].at[part],
                    own.at[where],
                    twin.at[where],
                    [
                        (half_0.at[where + (0,)], half_0.at[where + (1,)]),
                        (half_1.at[where + (0,)], half_1.at[where + (1,)]),
                        (half_2.at[where + (pl.ds(0, 2),)], half_2.at[where + (pl.ds(2, 1),)]),
                    ],
                    [full_0.at[where], full_1.at[where], full_2.at[where]],
                    PART_AXES[part],
                    at,
                    sems,
                    2,
                )
            )
            results.append(result.at[where])
    streams.append(
        Reduce(
            6,
            extra,
            own_x,
            twin_x,
            [
                (half_0x.at[0], half_0x.at[1]),
                (half_1x.at[0], half_1x.at[1]),
                (half_2x.at[pl.ds(0, 16)], half_2x.at[pl.ds(16, 16)]),
            ],
            [full_0x, full_1x, full_2x],
            "zyx",
            at,
            sems,
            16,
        )
    )
    results.append(result_x)
    for stream in streams:
        stream.load()
    greet(at)
    for slot, by in enumerate((2, 1, -1, 0)):
        for stream in streams:
            stream.trade(slot, by)
    token_copies = []
    for number, (src, dst) in enumerate(((output, output_part), (grad_x, grad_part))):
        rows = lambda stream: src.at[pl.ds(pl.multiple_of(64 * stream, 64), 64)]
        keep = pltpu.make_async_copy(rows(my_stream), dst.at[my_stream], token_local.at[number])
        keep.start()
        token_copies.append(keep)
        for flip in range(1, 4):
            to = flipped(at, 0, flip // 2, flip % 2)
            sems = token_send.at[number, flip - 1], token_recv.at[number, flip - 1]
            copy = remote(rows(stream_of(to)), dst.at[my_stream], *sems, to)
            copy.start()
            token_copies.append(copy)
    for turn in range(7):
        for stream, into in zip(streams, results):
            stream.step(turn, into)
    for to in range(8):
        for layer in range(2):
            for k in range(6):
                send_a[to, 6 * layer + k, 0:6, :] = result[k // 3, layer, k % 3, 6 * to : 6 * to + 6, :]
        send_a[to, 12, 0:4, :] = result_x[4 * to : 4 * to + 4, :]
    there = pl.ds(pl.multiple_of(24 * (1 - core), 8), 24)
    near = pl.ds(pl.multiple_of(24 * core, 8), 24)
    for layer in range(2):
        for k in range(3):
            send_b[layer, k] = result[2, layer, k, there, :]
            kept_b[layer, k] = result[2, layer, k, near, :]
    first = []
    for number, flip in enumerate(FLIPS):
        to = flipped(at, *flip)
        copy = remote(
            send_a.at[member(to)], got_a.at[mine], first_send.at[number], first_recv.at[number], to
        )
        copy.start()
        first.append(copy)
    copy = remote(send_b, got_b, first_send.at[7], first_recv.at[7], flipped(at, 0, 0, 1))
    copy.start()
    first.append(copy)
    got_a[mine] = send_a[mine]
    for stream in streams:
        stream.finish()
    for copy in first + token_copies:
        copy.wait()


def scatter(grads0, grads1, extra, output, grad_x):
    vmem, anywhere = pl.BlockSpec(memory_space=pltpu.VMEM), pl.BlockSpec(memory_space=pl.ANY)
    dma = pltpu.SemaphoreType.DMA
    block = (3, 48, 128)
    scratch = []
    for lead, unit, in (((3, 2), block), ((), (32, 128))):
        scratch += [
            pltpu.VMEM(lead + shape + unit, BF16)
            for shape in ((4, 4, 4), (4, 4, 4), (2, 2, 4), (2, 4, 4), (2, 2), (2, 4), (), (2,))
        ]

    def kernel(grads0, grads1, *rest):
        scatter_kernel((grads0, grads1), *rest)

    return pl.pallas_call(
        kernel,
        out_shape=[
            jax.ShapeDtypeStruct((8, 13, 8, 128), F32),
            jax.ShapeDtypeStruct((2, 3, 24, 128), F32),
            jax.ShapeDtypeStruct((2, 3, 24, 128), F32),
            jax.ShapeDtypeStruct((4, 64, 768), BF16),
            jax.ShapeDtypeStruct((4, 64, 768), BF16),
        ],
        in_specs=[anywhere] * 5,
        out_specs=[vmem] * 3 + [anywhere] * 2,
        scratch_shapes=scratch
        + [
            pltpu.VMEM((3, 2) + block, F32),
            pltpu.VMEM((32, 128), F32),
            pltpu.VMEM((8, 13, 8, 128), F32),
            pltpu.VMEM((2, 3, 24, 128), F32),
            dma((7, 16)),
            dma((7, 16)),
            dma((7,)),
            dma((8,)),
            dma((8,)),
            dma((2, 3)),
            dma((2, 3)),
            dma((2,)),
        ],
        compiler_params=pltpu.CompilerParams(
            collective_id=2, has_side_effects=True, vmem_limit_bytes=VMEM_BYTES
        ),
        name="scatter_grads",
    )(grads0, grads1, extra, output, grad_x)


def finish_kernel(
    got_a, got_b, kept_b, output, grad, out, grad_x, g_tin, g_tout, g_small, g_qkv, g_out, g_in, g_ffn
):
    core = lax.rem(lax.axis_index("stream"), 2)
    out[...] = output[...]
    grad_x[...] = grad[...].astype(F32)
    for frm in range(8):
        for layer in range(2):
            for k in range(6):
                chunk = frm + 8 * (k % 3)
                piece = got_a[frm, 6 * layer + k, 0:6, :]
                if k >= 3:
                    g_in[layer, :, 128 * chunk : 128 * chunk + 128] = piece
                elif chunk < 18:
                    g_qkv[layer, :, 128 * chunk : 128 * chunk + 128] = piece
                else:
                    g_out[layer, :, 128 * (chunk - 18) : 128 * (chunk - 18) + 128] = piece
        if frm < 6:
            g_tout[:, 128 * frm : 128 * frm + 128] = got_a[frm, 12, 0:4, :]
        elif frm == 6:
            for chunk in range(4):
                g_tin[:, 128 * chunk : 128 * chunk + 128] = got_a[frm, 12, chunk : chunk + 1, :]
        else:
            g_small[...] = got_a[frm, 12, 0:1, :]
    for layer in range(2):
        for k in range(3):
            near = pl.ds(pl.multiple_of(128 * (3 * core + k), 128), 128)
            there = pl.ds(pl.multiple_of(128 * (3 * (1 - core) + k), 128), 128)
            g_ffn[layer, :, near] = kept_b[layer, k]
            g_ffn[layer, :, there] = got_b[layer, k]


def finish(got_a, got_b, kept_b, output, grad):
    shapes = [
        ((4, 64, 768), BF16),
        ((4, 64, 768), F32),
        ((1, 512), F32),
        ((4, 768), F32),
        ((1, 128), F32),
        ((2, 6, 2304), F32),
        ((2, 6, 768), F32),
        ((2, 6, 3072), F32),
        ((2, 24, 768), F32),
    ]
    vmem = pl.BlockSpec(memory_space=pltpu.VMEM)
    return pl.pallas_call(
        finish_kernel,
        out_shape=[jax.ShapeDtypeStruct(shape, kind) for shape, kind in shapes],
        in_specs=[vmem] * 5,
        out_specs=[vmem] * len(shapes),
        compiler_params=pltpu.CompilerParams(vmem_limit_bytes=VMEM_BYTES),
        name="lay_out_results",
    )(got_a, got_b, kept_b, output, grad)


def sinusoid(timestep, feature_count):
    half_width = feature_count // 2
    frequency = jnp.exp(
        -math.log(10000.0) * jnp.arange(half_width).astype(timestep.dtype) / half_width
    )
    angles = timestep[:, None] * frequency[None, :]
    return jnp.concatenate([jnp.sin(angles), jnp.cos(angles)], axis=1)


def by_member(extra):
    split = extra.reshape(2, 4, 2, 2, 2, 2, 32, 128)
    return split.transpose(4, 1, 2, 3, 5, 0, 6, 7).reshape(16, 8, 32, 128)


def by_place(extra):
    split = extra.reshape(2, 4, 2, 2, 2, 2, 32, 128)
    return split.transpose(5, 1, 2, 3, 0, 4, 6, 7).reshape(2, 4, 4, 4, 32, 128)


def per_device(
    tokens,
    timestep,
    src_len,
    total_len,
    time_in,
    time_bias,
    time_out,
    qkv_weight,
    out_weight,
    norm1_gain,
    norm1_bias,
    ffn_in,
    ffn_bias,
    ffn_out,
    norm2_gain,
    norm2_bias,
    cotangent,
):
    stream = lax.axis_index("stream")
    pick = lambda values: lax.dynamic_slice_in_dim(values, stream, 1)
    norm_parts = jnp.stack([norm1_gain, norm1_bias, norm2_gain, norm2_bias], axis=1)
    small = jnp.concatenate(
        [time_bias, norm_parts.reshape(48), ffn_bias.reshape(48), jnp.zeros((28,), BF16)]
    ).astype(F32)[None, :]
    weights, extra, tokens_all, cotangent_all = gather(
        qkv_weight, out_weight, ffn_in, ffn_out, time_in, time_out, small, tokens, cotangent
    )
    extra = by_member(extra)
    time_out_all = extra[:, :6].transpose(0, 2, 1, 3).reshape(512, 768)
    time_in_all = extra[:, 6].reshape(128, 512)
    small_all = extra[:, 7].reshape(128, 4, 128)[:, 0].astype(F32)
    time_bias_all = small_all[:, :4].reshape(1, 512)
    norms = small_all[:, 4:52].reshape(128, 2, 4, 6).transpose(1, 2, 0, 3).reshape(2, 4, 768)
    norms = jnp.pad(norms, ((0, 0), (0, 4), (0, 0)))
    bias = small_all[:, 52:100].reshape(128, 2, 24).transpose(1, 0, 2).reshape(2, 1, 3072)

    emb_low = sinusoid(pick(timestep), 128).astype(BF16)
    time_pre = jnp.dot(emb_low, time_in_all, preferred_element_type=F32) + time_bias_all
    time_act = jax.nn.silu(time_pre).astype(BF16)
    temb = jnp.dot(time_act, time_out_all, preferred_element_type=F32)
    lens = jnp.concatenate([pick(src_len), pick(total_len)])

    state = tokens_all.astype(F32) + temb
    states, kept = [], []
    for layer in range(2):
        states.append(state)
        state, *saved = forward(layer, lens, state, norms[layer], bias[layer], weights)
        kept.append(saved)
    output = state.astype(BF16)
    grad = cotangent_all.astype(F32)
    grads, grad_norms, grad_biases = [None] * 2, [None] * 2, [None] * 2
    for layer in (1, 0):
        grad, grads[layer], grad_norms[layer], grad_biases[layer] = backward(
            layer, grad, states[layer], norms[layer], kept[layer], weights
        )
    temb_grad = jnp.sum(grad, axis=0, keepdims=True)
    act_grad = jnp.sum(temb_grad * time_out_all.astype(F32), axis=1)[None, :]
    sig = jax.nn.sigmoid(time_pre)
    pre_grad = act_grad * sig * (1.0 + time_pre * (1.0 - sig))
    grad_time_out = (time_act.astype(F32).reshape(512, 1) * temb_grad).astype(BF16)
    grad_time_in = (emb_low.astype(F32).reshape(128, 1) * pre_grad).astype(BF16)
    vectors = jnp.stack(grad_norms)[:, :4].reshape(2, 4, 128, 6).transpose(2, 0, 1, 3).reshape(128, 48)
    biases = jnp.stack(grad_biases).reshape(2, 128, 24).transpose(1, 0, 2).reshape(128, 48)
    grad_small = jnp.concatenate(
        [pre_grad.reshape(128, 4), vectors, biases, jnp.zeros((128, 28), F32)], axis=1
    ).astype(BF16)
    grad_small = jnp.pad(grad_small[:, None, :], ((0, 0), (0, 3), (0, 0)))
    grad_extra = jnp.concatenate(
        [
            grad_time_out.reshape(16, 32, 6, 128).transpose(0, 2, 1, 3),
            grad_time_in.reshape(16, 1, 32, 128),
            grad_small.reshape(16, 1, 32, 128),
        ],
        axis=1,
    )
    got = scatter(grads[0], grads[1], by_place(grad_extra), output, grad.astype(BF16))
    out, grad_x, g_tin, g_tout, g_small, g_qkv, g_out, g_in, g_ffn = finish(*got)
    g_norm = g_small[0, 4:52].reshape(2, 4, 6)
    return (
        out,
        grad_x,
        g_tin,
        g_small[0, :4],
        g_tout,
        g_qkv,
        g_out,
        g_norm[:, 0],
        g_norm[:, 1],
        g_in,
        g_small[0, 52:100].reshape(2, 24),
        g_ffn,
        g_norm[:, 2],
        g_norm[:, 3],
    )


def solution(mesh):
    in_specs = (
        P("batch", "stream", None),
        P("batch"),
        P("batch"),
        P("batch"),
        P(("batch", "stream"), None),
        P(("batch", "stream")),
        P(("batch", "stream"), None),
        P(None, ("batch", "stream"), None),
        P(None, ("batch", "stream"), None),
        P(None, ("batch", "stream")),
        P(None, ("batch", "stream")),
        P(None, ("batch", "stream"), None),
        P(None, ("batch", "stream")),
        P(None, ("batch", "stream"), None),
        P(None, ("batch", "stream")),
        P(None, ("batch", "stream")),
        P("batch", "stream", None),
    )
    out_specs = (
        P("batch", "stream", None),
        P("batch", "stream", None),
        P(("batch", "stream"), None),
        P(("batch", "stream")),
        P(("batch", "stream"), None),
        P(None, ("batch", "stream"), None),
        P(None, ("batch", "stream"), None),
        P(None, ("batch", "stream")),
        P(None, ("batch", "stream")),
        P(None, ("batch", "stream"), None),
        P(None, ("batch", "stream")),
        P(None, ("batch", "stream"), None),
        P(None, ("batch", "stream")),
        P(None, ("batch", "stream")),
    )
    return jax.shard_map(
        per_device, mesh=mesh, in_specs=in_specs, out_specs=out_specs, check_vma=False
    )
```

```python
from functools import partial
import math

import jax
import jax.numpy as jnp
from jax import lax
from jax.experimental import pallas as pl
from jax.experimental.pallas import tpu as pltpu
from jax.sharding import PartitionSpec as P

F32, BF16 = jnp.float32, jnp.bfloat16
EPS = 1e-05
NN = (((1,), (0,)), ((), ()))
NT = (((1,), (1,)), ((), ()))
TN = (((0,), (0,)), ((), ()))
MESH = pl.DeviceIdType.MESH
VMEM_BYTES = 65400 * 1024
AXES = ("zyx", "xzy", "yxz")
UNIT = (48, 128)
EXTRA = (32, 128)
GROUPS = [(x_hi, z, y_hi) for x_hi in range(2) for z in range(4) for y_hi in range(2)]
FLIPS = [(flip // 4, flip // 2 % 2, flip % 2) for flip in range(1, 8)]
TILES = (4, 4, 1)
ROUND_SPREAD, ROUND_REDUCE = 15, 14


def dot(left, right, dims=NN):
    return lax.dot_general(left, right, dims, preferred_element_type=F32)


def here():
    batch, stream = lax.axis_index("batch"), lax.axis_index("stream")
    return {
        "x": 2 * lax.div(batch, 16) + lax.div(stream, 2),
        "y": lax.rem(batch, 4),
        "z": lax.rem(lax.div(batch, 4), 4),
        "core": lax.rem(stream, 2),
    }


def device(at):
    return (
        lax.div(at["x"], 2) * 16 + at["z"] * 4 + at["y"],
        lax.rem(at["x"], 2) * 2 + at["core"],
    )


def moved(at, axis, by):
    return {**at, axis: lax.rem(at[axis] + by + 4, 4)}


def flipped(at, flip_y, flip_x, flip_core):
    new = dict(at)
    if flip_y:
        new["y"] = at["y"] + 1 - 2 * lax.rem(at["y"], 2)
    if flip_x:
        new["x"] = at["x"] + 1 - 2 * lax.rem(at["x"], 2)
    if flip_core:
        new["core"] = 1 - at["core"]
    return new


def member(at):
    return lax.rem(at["y"], 2) * 4 + lax.rem(at["x"], 2) * 2 + at["core"]


def stream_of(at):
    return lax.rem(at["x"], 2) * 2 + at["core"]


def signal(sem, to):
    pl.semaphore_signal(sem, inc=1, device_id=device(to), device_id_type=MESH)


def greet(at):
    partners = [flipped(at, *flip) for flip in FLIPS]
    partners += [moved(at, "z", 1), moved(at, "z", -1)]
    partners += [moved(at, axis, 2 * lax.rem(at[axis], 2) - 1) for axis in "xy"]
    partners += [moved(at, axis, 2) for axis in "xyz"]
    barrier = pltpu.get_barrier_semaphore()
    for partner in partners:
        signal(barrier, partner)
    pl.semaphore_wait(barrier, len(partners))


def remote(src, dst, send_sem, recv_sem, to):
    return pltpu.make_async_remote_copy(
        src_ref=src,
        dst_ref=dst,
        send_sem=send_sem,
        recv_sem=recv_sem,
        device_id=device(to),
        device_id_type=MESH,
    )


class Travel:
    def __init__(self, number, axes, at, sems):
        self.number, self.at = number, at
        self.axes, self.place = axes, [at[axis] for axis in axes]
        self.send_sems, self.recv_sems = sems
        self.copies, self.done = {}, 0

    def send(self, slot, src, dst, to):
        copy = remote(
            src, dst, self.send_sems.at[self.number, slot], self.recv_sems.at[self.number, slot], to
        )
        copy.start()
        self.copies[slot] = copy

    def turn(self, level, by):
        return lax.rem(self.place[level] + by + 4, 4)

    def neighbour(self, level, by):
        return moved(self.at, self.axes[level], by)

    def twin(self):
        return flipped(self.at, 0, 0, 1)

    def advance(self, until):
        while self.done < until:
            self.step(self.done)
            self.done += 1


class Spread(Travel):
    steps = 6

    def __init__(self, number, base, axes, at, sems):
        super().__init__(number, axes, at, sems)
        self.base = base.at[at["core"]]

    def line(self, slot, level, ref):
        for side, by in enumerate((1, -1, 2)):
            self.send(slot + side, ref, ref, self.neighbour(level, by))

    def arrive(self, slots):
        for slot in slots:
            self.copies[slot].wait_recv()

    def share(self, slot, ref):
        self.send(slot, ref, ref, self.twin())

    def step(self, number):
        c, b, a = self.place
        mine = self.base.at[c]
        if number == 0:
            self.line(0, 2, mine.at[b, a])
        elif number == 1:
            self.arrive((0, 1, 2))
            self.line(3, 1, mine.at[b])
        elif number == 2:
            self.arrive((3, 4, 5))
            self.send(6, mine, mine, self.neighbour(0, 1))
            self.send(7, mine, mine, self.neighbour(0, -1))
            self.share(10, mine)
        elif number == 3:
            for side, by in ((0, -1), (1, 1)):
                self.arrive((6 + side,))
                came = self.base.at[self.turn(0, by)]
                piece = came.at[pl.ds(2 * side, 2)]
                self.send(8 + side, piece, piece, self.neighbour(0, -by))
                self.share(11 + side, came)
        elif number == 4:
            for side in range(2):
                self.arrive((8 + side,))
                self.share(13 + side, self.base.at[self.turn(0, 2), pl.ds(2 * side, 2)])
        else:
            self.arrive(range(10, 15))

    def finish(self):
        for copy in self.copies.values():
            copy.wait_send()


class Reduce(Travel):
    steps = 6

    def __init__(self, number, grads, buffers, result, axes, at, sems, credits):
        super().__init__(number, axes, at, sems)
        core = at["core"]
        self.own, self.gone = grads.at[core], grads.at[1 - core]
        self.pair, self.half, self.full, self.row, self.cell = buffers
        self.result, self.credits = result, credits

    def meet(self, slot, by):
        self.copies[slot].wait_recv()
        plane = self.turn(0, by)

        def add(line, carry):
            self.own[plane, line] = self.own[plane, line] + self.pair[plane, line]
            return carry

        lax.fori_loop(0, 4, add, 0)

    def step(self, number):
        c, b, a = self.place
        if number == 0:
            if self.credits is not None:
                self.credits()
            for slot, by in enumerate((2, 1, -1, 0)):
                plane = self.turn(0, by)
                self.send(slot, self.gone.at[plane], self.pair.at[plane], self.twin())
        elif number == 1:
            self.meet(0, 2)
            for side, by in ((0, 1), (1, -1)):
                piece = self.own.at[self.turn(0, 2), pl.ds(2 * side, 2)]
                self.send(4 + side, piece, self.half.at[side], self.neighbour(0, by))
        elif number == 2:
            for side, by in ((0, 1), (1, -1)):
                self.meet(1 + side, by)
                self.copies[4 + side].wait_recv()
                plane = self.turn(0, by)

                def add(line, carry):
                    at = 2 * side + line
                    self.own[plane, at] = self.own[plane, at] + self.half[side, line]
                    return carry

                lax.fori_loop(0, 2, add, 0)
                self.send(6 + side, self.own.at[plane], self.full.at[side], self.neighbour(0, by))
        elif number == 3:
            self.meet(3, 0)
            for side in range(2):
                self.copies[6 + side].wait_recv()

            def settle(line, carry):
                total = self.own[c, line].astype(F32) + self.full[0, line].astype(F32)
                self.own[c, line] = (total + self.full[1, line].astype(F32)).astype(BF16)
                return carry

            lax.fori_loop(0, 4, settle, 0)
            for side, by in enumerate((1, -1, 2)):
                piece = self.own.at[c, self.turn(1, by)]
                self.send(8 + side, piece, self.row.at[side], self.neighbour(1, by))
        elif number == 4:
            for side in range(3):
                self.copies[8 + side].wait_recv()
            total = self.own[c, b].astype(F32)
            for side in range(3):
                total += self.row[side].astype(F32)
            self.own[c, b] = total.astype(BF16)
            for side, by in enumerate((1, -1, 2)):
                piece = self.own.at[c, b, self.turn(2, by)]
                self.send(11 + side, piece, self.cell.at[side], self.neighbour(2, by))
        else:
            for side in range(3):
                self.copies[11 + side].wait_recv()
            total = self.own[c, b, a].astype(F32)
            for side in range(3):
                total += self.cell[side].astype(F32)
            self.result(total)

    def finish(self):
        for copy in self.copies.values():
            copy.wait_send()


def place(k, core, x, y, z):
    at = {"x": x, "y": y, "z": z}
    return (core,) + tuple(at[name] for name in AXES[k])


def read_tile(weights, part, k, inner):
    y_lo, x_lo = lax.div(inner, 2), lax.rem(inner, 2)
    return jnp.concatenate(
        [
            jnp.concatenate(
                [
                    weights[(part, k) + place(k, core, 2 * x_hi + x_lo, 2 * y_hi + y_lo, z)]
                    for x_hi, z, y_hi in GROUPS
                ],
                axis=0,
            )
            for core in range(2)
        ],
        axis=1,
    )


def write_tile(grads, part, k, inner, values):
    y_lo, x_lo = lax.div(inner, 2), lax.rem(inner, 2)
    low = values.astype(BF16)
    for at, (x_hi, z, y_hi) in enumerate(GROUPS):
        for core in range(2):
            grads[(part, k) + place(k, core, 2 * x_hi + x_lo, 2 * y_hi + y_lo, z)] = low[
                48 * at : 48 * at + 48, 128 * core : 128 * core + 128
            ]


def read_rows(weights, step):
    x_hi, z = lax.div(step, 4), lax.rem(step, 4)
    return jnp.concatenate(
        [
            jnp.concatenate(
                [
                    weights[(2, k) + place(k, core, 2 * x_hi + x_lo, y, z)]
                    for y in range(4)
                    for x_lo in range(2)
                ],
                axis=0,
            )
            for core in range(2)
            for k in range(3)
        ],
        axis=1,
    )


def write_rows(grads, step, values):
    x_hi, z = lax.div(step, 4), lax.rem(step, 4)
    low = values.astype(BF16)
    for y in range(4):
        for x_lo in range(2):
            at = 48 * (2 * y + x_lo)
            for core in range(2):
                for k in range(3):
                    column = 128 * (3 * core + k)
                    grads[(2, k) + place(k, core, 2 * x_hi + x_lo, y, z)] = low[
                        at : at + 48, column : column + 128
                    ]


def chunks_of(ref, first, count):
    return jnp.concatenate([ref[first + at] for at in range(count)], axis=1)


def loop(start, stop, body):
    def step(at, carry):
        body(at)
        return carry

    lax.fori_loop(start, stop, step, 0)


def normalize(values):
    center = values - jnp.mean(values, axis=-1, keepdims=True)
    scale = lax.rsqrt(jnp.mean(center * center, axis=-1, keepdims=True) + EPS)
    return center * scale, scale


def normalize_back(grad, gain, normal, scale):
    grad_normal = grad * gain
    mean_one = jnp.mean(grad_normal, axis=-1, keepdims=True)
    mean_two = jnp.mean(grad_normal * normal, axis=-1, keepdims=True)
    return scale * (grad_normal - mean_one - normal * mean_two)


def half_masks():
    lane = lax.broadcasted_iota(jnp.int32, (1, 128), 1)
    first = jnp.where(lane < 64, 1.0, 0.0)
    return first.astype(BF16), (1.0 - first).astype(BF16)


class Kept:
    shapes = (
        ("proj", (18, 256, 128), BF16),
        ("soft", (12, 256, 256), BF16),
        ("mixed", (6, 256, 128), BF16),
        ("normal1", (256, 768), BF16),
        ("first_low", (256, 768), BF16),
        ("act", (24, 256, 128), BF16),
        ("slope", (24, 256, 128), BF16),
        ("normal2", (256, 768), F32),
        ("scales", (256, 2), F32),
    )

    def __init__(self, refs):
        for (name, _, _), ref in zip(self.shapes, refs):
            setattr(self, name, ref)


def forward_layer(state, lens, norms, bias, weights, kept, acc, need, tick):
    acc[...] = state()
    x_low = acc[...].astype(BF16)
    for k in range(3):
        need(0, k)

        def project(inner, k=k):
            out = dot(state().astype(BF16), read_tile(weights, 0, k, inner)).astype(BF16)
            chunk = 8 * k + 2 * inner
            kept.proj[chunk] = out[:, :128]
            kept.proj[chunk + 1] = out[:, 128:]

        loop(0, TILES[k], project)
        tick()

    key_at = lax.broadcasted_iota(jnp.int32, (1, 256), 1)
    bound = jnp.where(key_at < 128, lens[0], 128 + lens[1] - lens[0])
    shut = jnp.where(key_at < bound, 0.0, -1e30)
    low_half = lax.broadcasted_iota(jnp.int32, (256, 128), 1) < 64
    halves = half_masks()

    def attend(pair):
        queries = kept.proj[pair] * jnp.asarray(0.125, BF16)
        keys = kept.proj[6 + pair]
        values = kept.proj[12 + pair]
        outs = []
        for side in range(2):
            scores = dot(queries * halves[side], keys, NT) + shut
            top = jnp.max(scores, axis=-1, keepdims=True)
            exps = jnp.exp(scores - top)
            low = (exps * (1.0 / jnp.sum(exps, axis=-1, keepdims=True))).astype(BF16)
            kept.soft[2 * pair + side] = low
            outs.append(dot(low, values))
        kept.mixed[pair] = jnp.where(low_half, outs[0], outs[1]).astype(BF16)

    for pair in range(0, 6, 2):
        loop(pair, pair + 2, attend)
        tick()

    mixed_all = chunks_of(kept.mixed, 0, 6)
    for tile in range(3):
        columns = pl.ds(256 * tile, 256)
        acc[:, columns] += dot(mixed_all, read_tile(weights, 0, 2, 1 + tile))
    normal, scale = normalize(acc[...])
    kept.normal1[...] = normal.astype(BF16)
    kept.scales[:, 0:1] = scale
    first = normal * norms[0:1, :] + norms[1:2, :]
    acc[...] = first
    kept.first_low[...] = first.astype(BF16)
    tick()

    for k in range(3):
        need(1, k)

        def feed(inner, k=k):
            tile = 4 * k + inner
            columns = pl.ds(pl.multiple_of(256 * tile, 256), 256)
            pre = dot(kept.first_low[...], read_tile(weights, 1, k, inner)) + bias[0:1, columns]
            cdf = 0.5 * (1.0 + lax.erf(pre * math.sqrt(0.5)))
            out = (pre * cdf).astype(BF16)
            bell = jnp.exp(-0.5 * pre * pre) * (1.0 / math.sqrt(2 * math.pi))
            grad = (cdf + pre * bell).astype(BF16)
            kept.act[2 * tile] = out[:, :128]
            kept.act[2 * tile + 1] = out[:, 128:]
            kept.slope[2 * tile] = grad[:, :128]
            kept.slope[2 * tile + 1] = grad[:, 128:]

        loop(0, 4, feed)
        tick()
    for k in range(3):
        need(2, k)

    def unfeed(step):
        acc[...] += dot(chunks_of(kept.act, 3 * step, 3), read_rows(weights, step))

    for step in range(0, 8, 2):
        loop(step, step + 2, unfeed)
        tick()
    normal, scale = normalize(acc[...])
    kept.normal2[...] = normal
    kept.scales[:, 1:2] = scale


def backward_layer(state, grad, norms, weights, kept, acc, grad_norms, grad_bias, ready, tick):
    normal = kept.normal2[...]
    grad_norms[2] = jnp.sum(grad * normal, axis=0, keepdims=True)
    grad_norms[3] = jnp.sum(grad, axis=0, keepdims=True)
    acc[...] = normalize_back(grad, norms[2:3, :], normal, kept.scales[:, 1:2])

    def unfeed(step):
        branch = acc[...].astype(BF16)
        rows = read_rows(weights, step)
        grad_act = dot(branch, rows, NT)
        pre_low = (grad_act * chunks_of(kept.slope, 3 * step, 3).astype(F32)).astype(BF16)
        for at in range(3):
            kept.slope[3 * step + at] = pre_low[:, 128 * at : 128 * at + 128]
        grad_bias[step] = jnp.sum(pre_low.astype(F32), axis=0, keepdims=True)
        write_rows(weights, step, dot(chunks_of(kept.act, 3 * step, 3), branch, TN))

    for step in range(0, 8, 2):
        loop(step, step + 2, unfeed)
        if step == 6:
            for k in range(3):
                ready(2, k)
        tick()
    for k in range(3):

        def feed(inner, k=k):
            pre_low = chunks_of(kept.slope, 8 * k + 2 * inner, 2)
            acc[...] += dot(pre_low, read_tile(weights, 1, k, inner), NT)
            write_tile(weights, 1, k, inner, dot(kept.first_low[...], pre_low, TN))

        loop(0, 4, feed)
        ready(1, k)
        tick()

    grad = acc[...]
    normal = kept.normal1[...].astype(F32)
    grad_norms[0] = jnp.sum(grad * normal, axis=0, keepdims=True)
    grad_norms[1] = jnp.sum(grad, axis=0, keepdims=True)
    acc[...] = normalize_back(grad, norms[0:1, :], normal, kept.scales[:, 0:1])
    mixed_all = chunks_of(kept.mixed, 0, 6)
    total = jnp.zeros((256, 768), F32)
    for tile in range(3):
        part_low = acc[:, 256 * tile : 256 * tile + 256].astype(BF16)
        total += dot(part_low, read_tile(weights, 0, 2, 1 + tile), NT)
        write_tile(weights, 0, 2, 1 + tile, dot(mixed_all, part_low, TN))
    for chunk in range(6):
        kept.mixed[chunk] = total[:, 128 * chunk : 128 * chunk + 128].astype(BF16)
    tick()

    low_half = lax.broadcasted_iota(jnp.int32, (256, 128), 1) < 64
    halves = half_masks()

    def attend(pair):
        queries, keys, values = kept.proj[pair], kept.proj[6 + pair], kept.proj[12 + pair]
        back = kept.mixed[pair]
        grads_q, grads_k, grads_v = [], [], []
        for side in range(2):
            low = kept.soft[2 * pair + side]
            weight = low.astype(F32)
            grad_soft = dot(back * halves[side], values, NT)
            inner = jnp.sum(weight * grad_soft, axis=-1, keepdims=True)
            grad_score = (weight * (grad_soft - inner) * 0.125).astype(BF16)
            grads_q.append(dot(grad_score, keys))
            grads_k.append(dot(grad_score, queries, TN))
            grads_v.append(dot(low, back, TN))
        for first, both in ((0, grads_q), (6, grads_k), (12, grads_v)):
            kept.proj[first + pair] = jnp.where(low_half, both[0], both[1]).astype(BF16)

    for pair in range(0, 6, 2):
        loop(pair, pair + 2, attend)
        tick()

    for k in range(3):

        def project(inner, k=k):
            pair = chunks_of(kept.proj, 8 * k + 2 * inner, 2)
            acc[...] += dot(pair, read_tile(weights, 0, k, inner), NT)
            write_tile(weights, 0, k, inner, dot(state().astype(BF16), pair, TN))

        loop(0, TILES[k], project)
        ready(0, k)
        tick()


def member_rows(extra, who):
    y_lo, x_lo, core = who // 4, who // 2 % 2, who % 2
    return jnp.concatenate(
        [extra[core, z, 2 * y_hi + y_lo, 2 * x_hi + x_lo] for x_hi, z, y_hi in GROUPS], axis=0
    )


def write_member_rows(extra, who, values):
    y_lo, x_lo, core = who // 4, who // 2 % 2, who % 2
    for at, (x_hi, z, y_hi) in enumerate(GROUPS):
        extra[core, z, 2 * y_hi + y_lo, 2 * x_hi + x_lo] = values[32 * at : 32 * at + 32].astype(BF16)


def pick_rows(rows, columns, width):
    row = lax.broadcasted_iota(jnp.int32, (rows, columns), 0)
    column = lax.broadcasted_iota(jnp.int32, (rows, columns), 1)
    from_first = column - width * lax.shift_right_logical(row, 2)
    inside = jnp.logical_and(from_first >= 0, from_first < width)
    return jnp.where(inside, 1.0, 0.0).astype(BF16)


def pick_lanes(rows, columns, width):
    row = lax.broadcasted_iota(jnp.int32, (rows, columns), 0).astype(F32)
    column = lax.broadcasted_iota(jnp.int32, (rows, columns), 1).astype(F32)
    remainder = column - width * jnp.floor((column + 0.5) * (1.0 / width))
    return jnp.where(remainder == row, 1.0, 0.0)


def read_vectors(extra, norms, bias):
    small = member_rows(extra, 7)
    pick, lanes = pick_rows(256, 384, 6), pick_lanes(8, 384, 6)
    for at in range(2):
        spread = dot(small[256 * at : 256 * at + 256], pick, TN)
        for vector in range(8):
            value = jnp.sum(spread[8 + 8 * vector : 16 + 8 * vector] * lanes, axis=0, keepdims=True)
            norms[vector // 4, vector % 4 : vector % 4 + 1, 384 * at : 384 * at + 384] = value
    pick, lanes = pick_rows(64, 384, 24), pick_lanes(24, 384, 24)
    for at in range(8):
        spread = dot(small[64 * at : 64 * at + 64], pick, TN)
        for layer in range(2):
            value = spread[72 + 24 * layer : 96 + 24 * layer] * lanes
            bias[layer, :, 384 * at : 384 * at + 384] = jnp.sum(value, axis=0, keepdims=True)
    pick, lanes = pick_rows(128, 128, 4), pick_lanes(8, 128, 4)
    return jnp.concatenate(
        [
            jnp.sum(dot(small[128 * at : 128 * at + 128], pick, TN)[:8] * lanes, axis=0, keepdims=True)
            for at in range(4)
        ],
        axis=1,
    )


def time_weights(extra):
    return jnp.concatenate([member_rows(extra, who) for who in range(6)], axis=1)


def time_forward(extra, emb, time_bias, time_pre, time_act, temb):
    by_chunk = dot(emb[...], member_rows(extra, 6))
    pre = jnp.concatenate([by_chunk[at : at + 1] for at in range(4)], axis=1) + time_bias
    act = (pre * lax.logistic(pre)).astype(BF16)
    time_pre[...] = pre
    time_act[...] = act.astype(F32)
    temb[...] = dot(jnp.broadcast_to(act, (8, 512)), time_weights(extra))[0:1]


def high_low(values):
    high = values.astype(BF16).astype(F32)
    return high, values - high


def time_backward(extra, emb, time_pre, time_act, grad, grad_norms, grad_bias):
    zero = lambda rows, columns: jnp.zeros((rows, columns), F32)
    total = jnp.sum(grad, axis=0, keepdims=True)
    both = jnp.concatenate(high_low(total) + (zero(6, 768),), axis=0).astype(BF16)
    grad_act = jnp.sum(dot(both, time_weights(extra), NT), axis=0, keepdims=True)
    pre = time_pre[...]
    gate = lax.logistic(pre)
    grad_pre = grad_act * gate * (1.0 + pre * (1.0 - gate))
    act = time_act[...]
    acts = jnp.concatenate([act, act, zero(6, 512)], axis=0).astype(BF16)
    grad_out = dot(acts, both, TN)
    for who in range(6):
        write_member_rows(extra, who, grad_out[:, 128 * who : 128 * who + 128])
    high, low = high_low(grad_pre)
    by_chunk = [side[:, 128 * at : 128 * at + 128] for side in (high, low) for at in range(4)]
    write_member_rows(extra, 6, dot(emb[...], jnp.concatenate(by_chunk, axis=0).astype(BF16), TN))

    pieces = []
    pick, lanes = pick_rows(64, 384, 24), pick_lanes(24, 384, 24)
    for at in range(8):
        rows = [zero(72, 384)] + [lanes * grad_bias[layer, at] for layer in range(2)] + [zero(8, 384)]
        pieces.append(dot(pick, jnp.concatenate(rows, axis=0).astype(BF16), NT))
    small = jnp.concatenate(pieces, axis=0)
    pick, lanes, pieces = pick_rows(256, 384, 6), pick_lanes(8, 384, 6), []
    for at in range(2):
        rows = [zero(8, 384)]
        for layer in range(2):
            for vector in range(4):
                rows.append(lanes * grad_norms[layer, vector, :, 384 * at : 384 * at + 384])
        rows.append(zero(56, 384))
        pieces.append(dot(pick, jnp.concatenate(rows, axis=0).astype(BF16), NT))
    small += jnp.concatenate(pieces, axis=0)
    pick, lanes, pieces = pick_rows(128, 128, 4), pick_lanes(8, 128, 4), []
    for at in range(4):
        rows = [lanes * grad_pre[:, 128 * at : 128 * at + 128], zero(120, 128)]
        pieces.append(dot(pick, jnp.concatenate(rows, axis=0).astype(BF16), NT))
    write_member_rows(extra, 7, small + jnp.concatenate(pieces, axis=0))


class Clock:
    def __init__(self, plan):
        self.plan, self.now = plan, 0

    def tick(self):
        self.now += 1
        for travel, until in self.plan.get(self.now, ()):
            travel.advance(until)


def whole_kernel(*refs):
    refs = list(refs)
    take = lambda count: [refs.pop(0) for _ in range(count)]
    src_len, total_len = take(2)
    qkv, out_w, ffn_in, ffn_out, time_in, time_out, small, emb = take(8)
    tokens, cotangent = take(2)
    got_a, got_b, kept_b, output_part, grad_part = take(5)
    weights = take(2)
    kept = [Kept(take(len(Kept.shapes))) for _ in range(2)]
    acc, norms, bias, grad_norms, grad_bias = take(5)
    extra, time_pre, time_act, temb = take(4)
    tokens_all, cotangent_all, leaving = take(3)
    send_a, send_b, rows, rows_b = take(4)
    pair, half, full, row, cell, pair_x, half_x, full_x, row_x, cell_x = take(10)
    spread_sems, reduce_sems = take(2), take(2)
    first_send, first_recv, last_send, last_recv = take(4)
    move_send, move_recv, move_local = take(3)
    pair_free, ring_free = take(2)

    at = here()
    mine, core = member(at), at["core"]
    my_stream = stream_of(at)
    greet(at)

    def pack(layer):
        for to in range(8):
            for k in range(6):
                chunk = to + 8 * (k % 3)
                source, column = (qkv, chunk) if chunk < 18 else (out_w, chunk - 18)
                if k >= 3:
                    source, column = ffn_in, chunk
                piece = source[layer, :, 128 * column : 128 * column + 128]
                send_a[layer, to, k, 0:6, :] = piece.astype(F32)
        for k in range(3):
            column = pl.multiple_of(128 * (3 * (1 - core) + k), 128)
            send_b[layer, k] = ffn_out[layer, :, pl.ds(column, 128)].astype(F32)

    def trade(layer, from_a, into_a, from_b, into_b, sems, slots):
        copies = []
        for number, flip in enumerate(FLIPS):
            to = flipped(at, *flip)
            copies.append(
                remote(
                    from_a.at[layer, member(to), pl.ds(0, slots)],
                    into_a.at[layer, mine, pl.ds(0, slots)],
                    sems[0].at[layer, number],
                    sems[1].at[layer, number],
                    to,
                )
            )
        pair_sems = sems[0].at[layer, 7], sems[1].at[layer, 7]
        copies.append(
            remote(from_b.at[layer], into_b.at[layer], *pair_sems, flipped(at, 0, 0, 1))
        )
        for copy in copies:
            copy.start()
        into_a[layer, mine] = from_a[layer, mine]
        return copies

    pack(0)
    for to in range(8):
        send_a[0, to, 6] = jnp.zeros((8, 128), F32)
        if to < 6:
            send_a[0, to, 6, 0:4, :] = time_out[:, 128 * to : 128 * to + 128].astype(F32)
        elif to == 6:
            for chunk in range(4):
                columns = slice(128 * chunk, 128 * chunk + 128)
                send_a[0, to, 6, chunk : chunk + 1, :] = time_in[:, columns].astype(F32)
        else:
            send_a[0, to, 6, 0:1, :] = small[...]
    first = [trade(0, send_a, got_a, send_b, got_b, (first_send, first_recv), 7)]
    pack(1)
    first.append(trade(1, send_a, got_a, send_b, got_b, (first_send, first_recv), 6))

    moves = []

    def bring(number, src, dst, split):
        rows_of = lambda who: pl.ds(pl.multiple_of(64 * who, 64), 64)
        own_src = src.at[rows_of(my_stream)] if split else src.at[my_stream]
        own_dst = dst.at[my_stream] if split else dst.at[rows_of(my_stream)]
        copies = [pltpu.make_async_copy(own_src, own_dst, move_local.at[number])]
        for flip in range(1, 4):
            to = flipped(at, 0, flip // 2, flip % 2)
            there = src.at[rows_of(stream_of(to))] if split else src.at[stream_of(to)]
            sems = move_send.at[number, flip - 1], move_recv.at[number, flip - 1]
            copies.append(remote(there, own_dst, *sems, to))
        for copy in copies:
            copy.start()
        return copies

    def assemble(layer):
        for copy in first[layer]:
            copy.wait_recv()
        mine_at = [tuple(at[name] for name in AXES[k]) for k in range(3)]
        for part in range(2):
            for k in range(3):
                for frm in range(8):
                    rows[6 * frm : 6 * frm + 6, :] = got_a[layer, frm, 3 * part + k, 0:6, :]
                weights[layer][(part, k, core) + mine_at[k]] = rows[...].astype(BF16)
        for k in range(3):
            column = pl.multiple_of(128 * (3 * core + k), 128)
            rows_b[core] = ffn_out[layer, :, pl.ds(column, 128)].astype(F32)
            rows_b[1 - core] = got_b[layer, k]
            weights[layer][(2, k, core) + mine_at[k]] = rows_b[...].reshape(48, 128).astype(BF16)

    spread = {}
    for layer in range(2):
        for part in range(3):
            for k in range(3):
                number = 9 * layer + 3 * part + k
                base = weights[layer].at[part, k]
                spread[layer, part, k] = Spread(number, base, AXES[k], at, spread_sems)
    spread_x = Spread(18, extra, "zyx", at, spread_sems)

    def advance(layer, part, until):
        for k in range(3):
            spread[layer, part, k].advance(until)

    assemble(0)
    advance(0, 0, 1)
    for frm in range(8):
        rows[4 * frm : 4 * frm + 4, :] = got_a[0, frm, 6, 0:4, :]
    extra[core, at["z"], at["y"], at["x"]] = rows[0:32, :].astype(BF16)
    spread_x.advance(1)
    advance(0, 1, 1)
    advance(0, 2, 1)
    moves.append(bring(0, tokens, tokens_all, False))
    advance(0, 0, 2)
    spread_x.advance(2)
    advance(0, 1, 2)
    assemble(1)
    advance(0, 0, 3)
    spread_x.advance(3)
    for part in range(3):
        advance(1, part, 1)
    advance(0, 0, 4)
    spread_x.advance(4)
    advance(0, 1, 3)
    advance(0, 2, 2)
    spread_x.advance(6)
    time_bias = read_vectors(extra, norms, bias)
    time_forward(extra, emb, time_bias, time_pre, time_act, temb)
    advance(0, 0, 5)
    advance(0, 1, 4)
    advance(0, 2, 3)
    for copy in moves[0]:
        copy.wait()
    moves.append(bring(1, cotangent, cotangent_all, False))

    every = lambda table, layer, part, until: [(table[layer, part, k], until) for k in range(3)]
    plan = {
        1: every(spread, 0, 1, 5) + every(spread, 1, 0, 2),
        2: every(spread, 0, 2, 4),
        3: every(spread, 1, 1, 2),
        4: every(spread, 0, 2, 5) + every(spread, 1, 0, 3),
        5: every(spread, 1, 2, 2),
        6: every(spread, 1, 0, 4),
        7: every(spread, 1, 1, 3),
        8: every(spread, 1, 0, 5),
        9: every(spread, 1, 1, 4),
        10: every(spread, 1, 2, 3),
        11: every(spread, 1, 1, 5),
        12: every(spread, 1, 2, 4),
        14: every(spread, 1, 2, 5),
    }
    clock = Clock(plan)
    states = [
        lambda: tokens_all[...].astype(F32) + temb[...],
        lambda: kept[0].normal2[...] * norms[0, 2:3, :] + norms[0, 3:4, :],
    ]
    lens = (src_len[my_stream], total_len[my_stream])
    for layer in range(2):
        forward_layer(
            states[layer],
            lens,
            norms.at[layer],
            bias.at[layer],
            weights[layer],
            kept[layer],
            acc,
            lambda part, k: spread[layer, part, k].advance(6),
            clock.tick,
        )
    final = kept[1].normal2[...] * norms[1, 2:3, :] + norms[1, 3:4, :]
    leaving[...] = final.astype(BF16)
    moves.append(bring(2, leaving, output_part, True))
    for travel in spread.values():
        travel.finish()
    spread_x.finish()
    for copy in moves[1]:
        copy.wait()

    for copies in first:
        for copy in copies:
            copy.wait_send()

    there = pl.ds(pl.multiple_of(24 * (1 - core), 8), 24)
    near = pl.ds(pl.multiple_of(24 * core, 8), 24)

    def deliver(layer, part, k, total):
        rows[...] = total
        if part == 2:
            send_b[layer, k] = rows[there, :]
            kept_b[layer, k] = rows[near, :]
            return
        for to in range(8):
            send_a[layer, to, 3 * part + k, 0:6, :] = rows[6 * to : 6 * to + 6, :]

    def deliver_extra(total):
        rows[0:32, :] = total
        for to in range(8):
            send_a[0, to, 6, 0:4, :] = rows[4 * to : 4 * to + 4, :]

    around = [moved(at, axis, by) for axis in "xyz" for by in (1, -1, 2)]
    asked = set()

    def freed(part):
        if part not in asked:
            asked.add(part)
            pl.semaphore_wait(pair_free.at[part], 1)
            pl.semaphore_wait(ring_free.at[part], len(around))

    reduce = {}
    for layer in range(2):
        for part in range(3):
            for k in range(3):
                number = 9 * layer + 3 * part + k
                reduce[layer, part, k] = Reduce(
                    number,
                    weights[layer].at[part, k],
                    [ref.at[part, k] for ref in (pair, half, full, row, cell)],
                    partial(deliver, layer, part, k),
                    AXES[k],
                    at,
                    reduce_sems,
                    partial(freed, part) if layer == 0 else None,
                )
    reduce_x = Reduce(
        18, extra, (pair_x, half_x, full_x, row_x, cell_x), deliver_extra, "zyx", at, reduce_sems, None
    )

    class Free:
        def __init__(self, part):
            self.part, self.done = part, False

        def advance(self, until):
            if not self.done:
                self.done = True
                for k in range(3):
                    reduce[1, self.part, k].advance(6)
                    reduce[1, self.part, k].finish()
                signal(pair_free.at[self.part], flipped(at, 0, 0, 1))
                for to in around:
                    signal(ring_free.at[self.part], to)

    free = [Free(part) for part in range(3)]
    plan = {
        5: every(reduce, 1, 2, 2),
        8: every(reduce, 1, 2, 3),
        9: every(reduce, 1, 1, 2),
        10: every(reduce, 1, 2, 4),
        11: every(reduce, 1, 1, 3),
        12: every(reduce, 1, 2, 5),
        13: every(reduce, 1, 1, 4) ,
        14: [(free[2], 0)],
        15: every(reduce, 1, 1, 5) + every(reduce, 1, 0, 2),
        17: [(free[1], 0)] + every(reduce, 1, 0, 3),
        19: every(reduce, 1, 0, 4),
        20: every(reduce, 0, 2, 2),
        21: every(reduce, 1, 0, 5),
        22: [(free[0], 0)] + every(reduce, 0, 2, 3),
        23: every(reduce, 0, 1, 2),
        24: every(reduce, 0, 2, 4),
        25: every(reduce, 0, 1, 3),
        26: every(reduce, 0, 2, 5),
        27: every(reduce, 0, 1, 4),
        28: every(reduce, 0, 2, 6) + every(reduce, 0, 1, 5),
    }
    clock = Clock(plan)
    for layer in (1, 0):
        backward_layer(
            states[layer],
            cotangent_all[...].astype(F32) if layer else acc[...],
            norms.at[layer],
            weights[layer],
            kept[layer],
            acc,
            grad_norms.at[layer],
            grad_bias.at[layer],
            lambda part, k: reduce[layer, part, k].advance(1),
            clock.tick,
        )
    for k in range(3):
        reduce[0, 0, k].advance(2)
    for copy in moves[2]:
        copy.wait()
    leaving[...] = acc[...].astype(BF16)
    moves.append(bring(3, leaving, grad_part, True))
    last = [trade(1, send_a, got_a, send_b, got_b, (last_send, last_recv), 6)]
    time_backward(extra, emb, time_pre, time_act, acc[...], grad_norms, grad_bias)
    reduce_x.advance(1)
    for until in range(2, 7):
        for k in range(3):
            reduce[0, 0, k].advance(min(until + 1, 6))
        reduce_x.advance(until)
        if until == 2:
            for part in (2, 1):
                for k in range(3):
                    reduce[0, part, k].advance(6)

    last.append(trade(0, send_a, got_a, send_b, got_b, (last_send, last_recv), 7))
    for travel in list(reduce.values()) + [reduce_x]:
        if travel.number < 9 or travel.number == 18:
            travel.finish()
    for copies in last + moves[3:]:
        for copy in copies:
            copy.wait()


def whole(src_len, total_len, qkv, out_w, ffn_in, ffn_out, time_in, time_out, small, emb, tokens, cotangent):
    vmem, anywhere = pl.BlockSpec(memory_space=pltpu.VMEM), pl.BlockSpec(memory_space=pl.ANY)
    smem = pl.BlockSpec(memory_space=pltpu.SMEM)
    dma, regular = pltpu.SemaphoreType.DMA, pltpu.SemaphoreType.REGULAR
    buffers = lambda lead, unit: [
        pltpu.VMEM(lead + shape + unit, BF16)
        for shape in ((4, 4, 4), (2, 2, 4), (2, 4, 4), (3, 4), (3,))
    ]
    scratch = [pltpu.VMEM((3, 3, 2, 4, 4, 4) + UNIT, BF16) for _ in range(2)]
    for _ in range(2):
        scratch += [pltpu.VMEM(shape, kind) for _, shape, kind in Kept.shapes]
    scratch += [
        pltpu.VMEM((256, 768), F32),
        pltpu.VMEM((2, 8, 768), F32),
        pltpu.VMEM((2, 1, 3072), F32),
        pltpu.VMEM((2, 4, 1, 768), F32),
        pltpu.VMEM((2, 8, 1, 384), F32),
        pltpu.VMEM((2, 4, 4, 4) + EXTRA, BF16),
        pltpu.VMEM((1, 512), F32),
        pltpu.VMEM((1, 512), F32),
        pltpu.VMEM((1, 768), F32),
        pltpu.VMEM((256, 768), BF16),
        pltpu.VMEM((256, 768), BF16),
        pltpu.VMEM((256, 768), BF16),
        pltpu.VMEM((2, 8, 7, 8, 128), F32),
        pltpu.VMEM((2, 3, 24, 128), F32),
        pltpu.VMEM((48, 128), F32),
        pltpu.VMEM((2, 24, 128), F32),
    ]
    scratch += buffers((3, 3), UNIT) + buffers((), EXTRA)
    scratch += [
        dma((19, ROUND_SPREAD)),
        dma((19, ROUND_SPREAD)),
        dma((19, ROUND_REDUCE)),
        dma((19, ROUND_REDUCE)),
        dma((2, 8)),
        dma((2, 8)),
        dma((2, 8)),
        dma((2, 8)),
        dma((4, 3)),
        dma((4, 3)),
        dma((4,)),
        regular((3,)),
        regular((3,)),
    ]
    return pl.pallas_call(
        whole_kernel,
        out_shape=[
            jax.ShapeDtypeStruct((2, 8, 7, 8, 128), F32),
            jax.ShapeDtypeStruct((2, 3, 24, 128), F32),
            jax.ShapeDtypeStruct((2, 3, 24, 128), F32),
            jax.ShapeDtypeStruct((4, 64, 768), BF16),
            jax.ShapeDtypeStruct((4, 64, 768), BF16),
        ],
        in_specs=[smem] * 2 + [vmem] * 8 + [anywhere] * 2,
        out_specs=[vmem] * 3 + [anywhere] * 2,
        scratch_shapes=scratch,
        compiler_params=pltpu.CompilerParams(
            collective_id=1, has_side_effects=True, vmem_limit_bytes=VMEM_BYTES
        ),
        name="whole",
    )(src_len, total_len, qkv, out_w, ffn_in, ffn_out, time_in, time_out, small, emb, tokens, cotangent)


def finish_kernel(
    got_a, got_b, kept_b, output, grad, out, grad_x, g_tin, g_tout, g_small, g_qkv, g_out, g_in, g_ffn
):
    core = lax.rem(lax.axis_index("stream"), 2)
    out[...] = output[...]
    grad_x[...] = grad[...].astype(F32)
    for frm in range(8):
        for layer in range(2):
            for k in range(6):
                chunk = frm + 8 * (k % 3)
                piece = got_a[layer, frm, k, 0:6, :]
                if k >= 3:
                    g_in[layer, :, 128 * chunk : 128 * chunk + 128] = piece
                elif chunk < 18:
                    g_qkv[layer, :, 128 * chunk : 128 * chunk + 128] = piece
                else:
                    g_out[layer, :, 128 * (chunk - 18) : 128 * (chunk - 18) + 128] = piece
        if frm < 6:
            g_tout[:, 128 * frm : 128 * frm + 128] = got_a[0, frm, 6, 0:4, :]
        elif frm == 6:
            for chunk in range(4):
                g_tin[:, 128 * chunk : 128 * chunk + 128] = got_a[0, frm, 6, chunk : chunk + 1, :]
        else:
            g_small[...] = got_a[0, frm, 6, 0:1, :]
    for layer in range(2):
        for k in range(3):
            near = pl.ds(pl.multiple_of(128 * (3 * core + k), 128), 128)
            there = pl.ds(pl.multiple_of(128 * (3 * (1 - core) + k), 128), 128)
            g_ffn[layer, :, near] = kept_b[layer, k]
            g_ffn[layer, :, there] = got_b[layer, k]


def finish(got_a, got_b, kept_b, output, grad):
    shapes = [
        ((4, 64, 768), BF16),
        ((4, 64, 768), F32),
        ((1, 512), F32),
        ((4, 768), F32),
        ((1, 128), F32),
        ((2, 6, 2304), F32),
        ((2, 6, 768), F32),
        ((2, 6, 3072), F32),
        ((2, 24, 768), F32),
    ]
    vmem = pl.BlockSpec(memory_space=pltpu.VMEM)
    return pl.pallas_call(
        finish_kernel,
        out_shape=[jax.ShapeDtypeStruct(shape, kind) for shape, kind in shapes],
        in_specs=[vmem] * 5,
        out_specs=[vmem] * len(shapes),
        compiler_params=pltpu.CompilerParams(vmem_limit_bytes=VMEM_BYTES),
        name="lay_out_results",
    )(got_a, got_b, kept_b, output, grad)


def time_features(timestep):
    column = lax.broadcasted_iota(jnp.int32, (8, 512), 1)
    row = lax.broadcasted_iota(jnp.int32, (8, 512), 0)
    feature = column // 4
    half = jnp.where(feature < 64, feature, feature - 64).astype(F32)
    angles = timestep * jnp.exp(-math.log(10000.0) * half / 64)
    values = jnp.where(feature < 64, jnp.sin(angles), jnp.cos(angles))
    return jnp.where(column % 4 == row % 4, values, 0.0).astype(BF16)


def per_device(
    tokens,
    timestep,
    src_len,
    total_len,
    time_in,
    time_bias,
    time_out,
    qkv_weight,
    out_weight,
    norm1_gain,
    norm1_bias,
    ffn_in,
    ffn_bias,
    ffn_out,
    norm2_gain,
    norm2_bias,
    cotangent,
):
    stream = lax.axis_index("stream")
    my_step = jnp.sum(jnp.where(jnp.arange(4) == stream, timestep, 0.0))
    vectors = [(time_bias, 0)]
    for layer in range(2):
        for at, vector in enumerate((norm1_gain, norm1_bias, norm2_gain, norm2_bias)):
            vectors.append((vector[layer], 8 + 32 * layer + 8 * at))
        vectors.append((ffn_bias[layer], 72 + 24 * layer))
    small = sum(
        jnp.pad(vector.astype(F32), (first, 128 - first - vector.shape[0])) for vector, first in vectors
    )[None, :]
    got = whole(
        src_len,
        total_len,
        qkv_weight,
        out_weight,
        ffn_in,
        ffn_out,
        time_in,
        time_out,
        small,
        time_features(my_step),
        tokens,
        cotangent,
    )
    out, grad_x, g_tin, g_tout, g_small, g_qkv, g_out, g_in, g_ffn = finish(*got)
    g_norm = g_small[0, 8:72].reshape(2, 4, 8)[:, :, :6]
    return (
        out,
        grad_x,
        g_tin,
        g_small[0, :4],
        g_tout,
        g_qkv,
        g_out,
        g_norm[:, 0],
        g_norm[:, 1],
        g_in,
        g_small[0, 72:120].reshape(2, 24),
        g_ffn,
        g_norm[:, 2],
        g_norm[:, 3],
    )


def solution(mesh):
    in_specs = (
        P("batch", "stream", None),
        P("batch"),
        P("batch"),
        P("batch"),
        P(("batch", "stream"), None),
        P(("batch", "stream")),
        P(("batch", "stream"), None),
        P(None, ("batch", "stream"), None),
        P(None, ("batch", "stream"), None),
        P(None, ("batch", "stream")),
        P(None, ("batch", "stream")),
        P(None, ("batch", "stream"), None),
        P(None, ("batch", "stream")),
        P(None, ("batch", "stream"), None),
        P(None, ("batch", "stream")),
        P(None, ("batch", "stream")),
        P("batch", "stream", None),
    )
    out_specs = (
        P("batch", "stream", None),
        P("batch", "stream", None),
        P(("batch", "stream"), None),
        P(("batch", "stream")),
        P(("batch", "stream"), None),
        P(None, ("batch", "stream"), None),
        P(None, ("batch", "stream"), None),
        P(None, ("batch", "stream")),
        P(None, ("batch", "stream")),
        P(None, ("batch", "stream"), None),
        P(None, ("batch", "stream")),
        P(None, ("batch", "stream"), None),
        P(None, ("batch", "stream")),
        P(None, ("batch", "stream")),
    )
    return jax.shard_map(
        per_device, mesh=mesh, in_specs=in_specs, out_specs=out_specs, check_vma=False
    )
```

```python
from functools import partial
import math

import jax
import jax.numpy as jnp
from jax import lax
from jax.experimental import pallas as pl
from jax.experimental.pallas import tpu as pltpu
from jax.sharding import PartitionSpec as P

F32, BF16 = jnp.float32, jnp.bfloat16
EPS = 1e-05
NN = (((1,), (0,)), ((), ()))
NT = (((1,), (1,)), ((), ()))
TN = (((0,), (0,)), ((), ()))
MESH = pl.DeviceIdType.MESH
VMEM_BYTES = 65400 * 1024
AXES = ("zyx", "xzy", "yxz")
UNIT = (48, 128)
EXTRA = (32, 128)
GROUPS = [(x_hi, z, y_hi) for x_hi in range(2) for z in range(4) for y_hi in range(2)]
FLIPS = [(flip // 4, flip // 2 % 2, flip % 2) for flip in range(1, 8)]
TILES = (4, 4, 1)
SPREAD_SEMS, REDUCE_SEMS = 6, 7


def dot(left, right, dims=NN):
    return lax.dot_general(left, right, dims, preferred_element_type=F32)


def here():
    batch, stream = lax.axis_index("batch"), lax.axis_index("stream")
    return {
        "x": 2 * lax.div(batch, 16) + lax.div(stream, 2),
        "y": lax.rem(batch, 4),
        "z": lax.rem(lax.div(batch, 4), 4),
        "core": lax.rem(stream, 2),
    }


def device(at):
    return (
        lax.div(at["x"], 2) * 16 + at["z"] * 4 + at["y"],
        lax.rem(at["x"], 2) * 2 + at["core"],
    )


def moved(at, axis, by):
    return {**at, axis: lax.rem(at[axis] + by + 4, 4)}


def flipped(at, flip_y, flip_x, flip_core):
    new = dict(at)
    if flip_y:
        new["y"] = at["y"] + 1 - 2 * lax.rem(at["y"], 2)
    if flip_x:
        new["x"] = at["x"] + 1 - 2 * lax.rem(at["x"], 2)
    if flip_core:
        new["core"] = 1 - at["core"]
    return new


def member(at):
    return lax.rem(at["y"], 2) * 4 + lax.rem(at["x"], 2) * 2 + at["core"]


def stream_of(at):
    return lax.rem(at["x"], 2) * 2 + at["core"]


def signal(sem, to):
    pl.semaphore_signal(sem, inc=1, device_id=device(to), device_id_type=MESH)


def greet(at):
    partners = [flipped(at, *flip) for flip in FLIPS]
    partners += [moved(at, "z", 1), moved(at, "z", -1)]
    partners += [moved(at, axis, 2 * lax.rem(at[axis], 2) - 1) for axis in "xy"]
    partners += [moved(at, axis, 2) for axis in "xyz"]
    barrier = pltpu.get_barrier_semaphore()
    for partner in partners:
        signal(barrier, partner)
    pl.semaphore_wait(barrier, len(partners))


def remote(src, dst, send_sem, recv_sem, to):
    return pltpu.make_async_remote_copy(
        src_ref=src,
        dst_ref=dst,
        send_sem=send_sem,
        recv_sem=recv_sem,
        device_id=device(to),
        device_id_type=MESH,
    )


def wait_bytes(ref, sem):
    pltpu.make_async_copy(ref, ref, sem).wait()


class Travel:
    def __init__(self, number, blocks, orders, at, sems, ring):
        self.at, self.ring, self.blocks = at, ring, blocks
        self.orders = orders
        self.places = [[at[axis] for axis in order] for order in orders]
        self.recv_sem = lambda kind: sems[0].at[number, kind]
        self.send_sem = lambda kind: sems[1].at[number, kind]
        self.done, self.leaving = 0, None
        self.own = [blocks.at[k, at["core"]] for k in range(len(orders))]
        self.gone = [blocks.at[k, 1 - at["core"]] for k in range(len(orders))]

    def cells(self, count):
        return self.blocks.at[:, 0, 0, 0, pl.ds(0, count)]

    def lines(self, count):
        return self.blocks.at[:, 0, 0, pl.ds(0, count)]

    def planes(self, count):
        return self.blocks.at[:, 0, pl.ds(0, count)]

    def turn(self, k, level, by):
        return lax.rem(self.places[k][level] + by + 4, 4)

    def neighbour(self, k, level, by):
        return moved(self.at, self.orders[k][level], by)

    def twin(self):
        return flipped(self.at, 0, 0, 1)

    def arrive(self, kind, total):
        wait_bytes(total, self.recv_sem(kind))

    def depart(self, kind, pieces, total):
        self.departed()
        for src, dst, to in pieces:
            remote(src, dst, self.send_sem(0), self.recv_sem(kind), to).start()
        self.leaving = total

    def departed(self):
        if self.leaving is not None:
            wait_bytes(self.leaving, self.send_sem(0))
        self.leaving = None

    def crossed(self):
        wait_bytes(self.blocks.at[:, 0], self.send_sem(1))

    def advance(self, until):
        while self.done < until:
            self.step(self.done)
            self.done += 1


class Spread(Travel):
    def share(self, ref):
        remote(ref, ref, self.send_sem(1), self.recv_sem(5), self.twin()).start()

    def pass_on(self, kind, level, came, total):
        pieces = []
        for k in range(len(self.orders)):
            for side, by in ((0, -1), (1, 1)):
                piece = came(k, by).at[pl.ds(2 * side, 2)]
                pieces.append((piece, piece, self.neighbour(k, level, -by)))
        self.depart(kind, pieces, total)

    def send_block(self, kind, level, sides, block, total):
        pieces = []
        for k, place in enumerate(self.places):
            mine = block(self.own[k], place)
            pieces += [(mine, mine, self.neighbour(k, level, by)) for by in sides]
        self.depart(kind, pieces, total)

    def step(self, number):
        own = self.own
        if number == 0:
            self.send_block(0, 2, (1, -1, 2), lambda ref, to: ref.at[tuple(to)], self.cells(3))
        elif number == 1:
            self.arrive(0, self.cells(3))
            sides = (1, -1) if self.ring else (1, -1, 2)
            block = lambda ref, to: ref.at[to[0], to[1]]
            self.send_block(1, 1, sides, block, self.lines(len(sides)))
        elif number == 2 and self.ring:
            self.arrive(1, self.lines(2))
            came = lambda k, by: own[k].at[self.places[k][0], self.turn(k, 1, by)]
            self.pass_on(2, 1, came, self.lines(1))
        elif number == 3:
            if self.ring:
                self.arrive(2, self.lines(1))
            else:
                self.arrive(1, self.lines(3))
            self.send_block(3, 0, (1, -1), lambda ref, to: ref.at[to[0]], self.planes(2))
            for ref, to in zip(own, self.places):
                self.share(ref.at[to[0]])
        elif number == 4:
            self.arrive(3, self.planes(2))
            came = lambda k, by: own[k].at[self.turn(k, 0, by)]
            self.pass_on(4, 0, came, self.planes(1))
            for k in range(len(own)):
                for by in (1, -1):
                    self.share(came(k, by))
        elif number == 5:
            self.arrive(4, self.planes(1))
            for k in range(len(own)):
                self.share(own[k].at[self.turn(k, 0, 2)])
        elif number == 6:
            self.arrive(5, self.blocks.at[:, 0])

    def finish(self):
        self.departed()
        self.crossed()


class Reduce(Travel):
    def __init__(self, number, blocks, buffers, result, orders, at, sems, ring, credits, row_credits):
        super().__init__(number, blocks, orders, at, sems, ring)
        self.pair, self.half, self.full, self.row, self.cell = buffers
        self.result, self.traded = result, 0
        self.credits, self.row_credits = credits, row_credits

    def trade(self, k):
        if self.traded == 0 and self.credits is not None:
            self.credits()
        self.traded += 1
        for kind, by in ((0, 2), (1, 1), (1, -1), (1, 0)):
            plane = self.turn(k, 0, by)
            src, dst = self.gone[k].at[plane], self.pair.at[k, plane]
            remote(src, dst, self.send_sem(1), self.recv_sem(kind), self.twin()).start()

    def meet(self, k, by):
        plane = self.turn(k, 0, by)
        self.own[k][plane] = self.own[k][plane] + self.pair[k, plane]

    def start_ring(self, kind, level, opposite, halves, total):
        pieces = []
        for k in range(len(self.orders)):
            for side, by in ((0, 1), (1, -1)):
                piece = opposite(k).at[pl.ds(2 * side, 2)]
                pieces.append((piece, halves(k, side), self.neighbour(k, level, by)))
        self.depart(kind, pieces, total)

    def step(self, number):
        own, members = self.own, range(len(self.orders))
        if number == 0:
            for k in range(self.traded, len(self.orders)):
                self.trade(k)
        elif number == 1:
            self.arrive(0, self.planes(1))
            for k in members:
                self.meet(k, 2)
            opposite = lambda k: own[k].at[self.turn(k, 0, 2)]
            self.start_ring(2, 0, opposite, lambda k, side: self.half.at[k, side], self.planes(1))
        elif number == 2:
            self.arrive(1, self.planes(3))
            for k in members:
                for by in (1, -1, 0):
                    self.meet(k, by)
            self.arrive(2, self.planes(1))
            pieces = []
            for k in members:
                for side, by in ((0, 1), (1, -1)):
                    plane, rows = self.turn(k, 0, by), pl.ds(2 * side, 2)
                    own[k][plane, rows] = own[k][plane, rows] + self.half[k, side]
                    to = self.neighbour(k, 0, by)
                    pieces.append((own[k].at[plane], self.full.at[k, side], to))
            self.depart(3, pieces, self.planes(2))
        elif number == 3:
            self.arrive(3, self.planes(2))
            for k in members:
                c = self.places[k][0]
                total = own[k][c].astype(F32) + self.full[k, 0].astype(F32)
                own[k][c] = (total + self.full[k, 1].astype(F32)).astype(BF16)
            if self.row_credits is not None:
                self.row_credits()
            if self.ring:
                opposite = lambda k: own[k].at[self.places[k][0], self.turn(k, 1, 2)]
                halves = lambda k, side: self.row.at[k, 2, pl.ds(2 * side, 2)]
                self.start_ring(4, 1, opposite, halves, self.lines(1))
            else:
                pieces = []
                for k in members:
                    for side, by in enumerate((1, -1, 2)):
                        line = own[k].at[self.places[k][0], self.turn(k, 1, by)]
                        pieces.append((line, self.row.at[k, side], self.neighbour(k, 1, by)))
                self.depart(5, pieces, self.lines(3))
        elif number == 4 and self.ring:
            self.arrive(4, self.lines(1))
            pieces = []
            for k in members:
                c = self.places[k][0]
                for side, by in ((0, 1), (1, -1)):
                    line, cells = self.turn(k, 1, by), pl.ds(2 * side, 2)
                    own[k][c, line, cells] = own[k][c, line, cells] + self.row[k, 2, cells]
                    to = self.neighbour(k, 1, by)
                    pieces.append((own[k].at[c, line], self.row.at[k, side], to))
            self.depart(5, pieces, self.lines(2))
        elif number == 5:
            count = 2 if self.ring else 3
            self.arrive(5, self.lines(count))
            pieces = []
            for k in members:
                c, b, _ = self.places[k]
                total = own[k][c, b].astype(F32)
                for side in range(count):
                    total += self.row[k, side].astype(F32)
                own[k][c, b] = total.astype(BF16)
                for side, by in enumerate((1, -1, 2)):
                    cell = own[k].at[c, b, self.turn(k, 2, by)]
                    pieces.append((cell, self.cell.at[k, side], self.neighbour(k, 2, by)))
            self.depart(6, pieces, self.cells(3))
        elif number == 6:
            self.arrive(6, self.cells(3))
            for k in members:
                total = own[k][tuple(self.places[k])].astype(F32)
                for side in range(3):
                    total += self.cell[k, side].astype(F32)
                self.result(k, total)


def place(k, core, x, y, z):
    at = {"x": x, "y": y, "z": z}
    return (core,) + tuple(at[name] for name in AXES[k])


def read_tile(weights, part, k, inner, groups=GROUPS):
    y_lo, x_lo = inner // 2, inner % 2
    return jnp.concatenate(
        [
            jnp.concatenate(
                [
                    weights[(part, k) + place(k, core, 2 * x_hi + x_lo, 2 * y_hi + y_lo, z)]
                    for x_hi, z, y_hi in groups
                ],
                axis=0,
            )
            for core in range(2)
        ],
        axis=1,
    )


def write_tile(grads, part, k, inner, values):
    y_lo, x_lo = inner // 2, inner % 2
    low = values.astype(BF16)
    for at, (x_hi, z, y_hi) in enumerate(GROUPS):
        for core in range(2):
            grads[(part, k) + place(k, core, 2 * x_hi + x_lo, 2 * y_hi + y_lo, z)] = low[
                48 * at : 48 * at + 48, 128 * core : 128 * core + 128
            ]


def read_rows(weights, step, chunks=range(6)):
    x_hi, z = step // 4, step % 4
    return jnp.concatenate(
        [
            jnp.concatenate(
                [
                    weights[(2, chunk % 3) + place(chunk % 3, chunk // 3, 2 * x_hi + x_lo, y, z)]
                    for y in range(4)
                    for x_lo in range(2)
                ],
                axis=0,
            )
            for chunk in chunks
        ],
        axis=1,
    )


def write_rows(grads, step, values):
    x_hi, z = step // 4, step % 4
    low = values.astype(BF16)
    for y in range(4):
        for x_lo in range(2):
            at = 48 * (2 * y + x_lo)
            for core in range(2):
                for k in range(3):
                    column = 128 * (3 * core + k)
                    grads[(2, k) + place(k, core, 2 * x_hi + x_lo, y, z)] = low[
                        at : at + 48, column : column + 128
                    ]


def chunks_of(ref, first, count):
    return jnp.concatenate([ref[first + at] for at in range(count)], axis=1)


def by_rows(step):
    for first in range(0, 256, 64):
        step(pl.ds(first, 64))


def normalize(values):
    center = values - jnp.mean(values, axis=-1, keepdims=True)
    scale = lax.rsqrt(jnp.mean(center * center, axis=-1, keepdims=True) + EPS)
    return center * scale, scale


def normalize_back(grad, gain, normal, scale):
    grad_normal = grad * gain
    mean_one = jnp.mean(grad_normal, axis=-1, keepdims=True)
    mean_two = jnp.mean(grad_normal * normal, axis=-1, keepdims=True)
    return scale * (grad_normal - mean_one - normal * mean_two)


def half_masks():
    lane = lax.broadcasted_iota(jnp.int32, (1, 128), 1)
    first = jnp.where(lane < 64, 1.0, 0.0)
    return first.astype(BF16), (1.0 - first).astype(BF16)


class Kept:
    shapes = (
        ("proj", (18, 256, 128), BF16),
        ("soft", (12, 256, 256), BF16),
        ("mixed", (6, 256, 128), BF16),
        ("normal1", (256, 768), BF16),
        ("first_low", (256, 768), BF16),
        ("act", (24, 256, 128), BF16),
        ("slope", (24, 256, 128), BF16),
        ("normal2", (256, 768), F32),
        ("scales", (256, 2), F32),
    )

    def __init__(self, refs):
        for (name, _, _), ref in zip(self.shapes, refs):
            setattr(self, name, ref)


def forward_layer(state, norms, bias, shut, weights, kept, acc, need, tick):
    def enter(rows):
        values = state(rows)
        acc[rows, :] = values
        kept.first_low[rows, :] = values.astype(BF16)

    by_rows(enter)
    for k in range(3):
        need(0, k)
        for inner in range(TILES[k]):
            out = dot(kept.first_low[...], read_tile(weights, 0, k, inner)).astype(BF16)
            chunk = 8 * k + 2 * inner
            kept.proj[chunk] = out[:, :128]
            kept.proj[chunk + 1] = out[:, 128:]
        tick()

    low_half = lax.broadcasted_iota(jnp.int32, (256, 128), 1) < 64
    halves = half_masks()
    closed = jnp.concatenate([shut[...], shut[...]], axis=1)
    for pair in range(6):
        queries = kept.proj[pair] * jnp.asarray(0.125, BF16)
        keys = kept.proj[6 + pair]
        values = kept.proj[12 + pair]
        outs = []
        for side in range(2):
            scores = dot(keys, queries * halves[side], NT) + closed
            top = jnp.max(scores, axis=0, keepdims=True)
            exps = jnp.exp(scores - top)
            low = (exps * (1.0 / jnp.sum(exps, axis=0, keepdims=True))).astype(BF16)
            kept.soft[2 * pair + side] = low
            outs.append(dot(low, values, TN))
        kept.mixed[pair] = jnp.where(low_half, outs[0], outs[1]).astype(BF16)
        if pair % 3 == 2:
            tick()

    mixed_all = chunks_of(kept.mixed, 0, 6)
    for tile in range(3):
        columns = pl.ds(256 * tile, 256)
        acc[:, columns] += dot(mixed_all, read_tile(weights, 0, 2, 1 + tile))

    def first_norm(rows):
        normal, scale = normalize(acc[rows, :])
        kept.normal1[rows, :] = normal.astype(BF16)
        kept.scales[rows, 0:1] = scale
        first = normal * norms[0:1, :] + norms[1:2, :]
        acc[rows, :] = first
        kept.first_low[rows, :] = first.astype(BF16)

    by_rows(first_norm)
    tick()

    for k in range(3):
        need(1, k)
        for tile in range(4 * k, 4 * k + 4):
            columns = slice(256 * tile, 256 * tile + 256)
            pre = dot(kept.first_low[...], read_tile(weights, 1, k, tile % 4)) + bias[0:1, columns]
            cdf = 0.5 * (1.0 + lax.erf(pre * math.sqrt(0.5)))
            out = (pre * cdf).astype(BF16)
            bell = jnp.exp(-0.5 * pre * pre) * (1.0 / math.sqrt(2 * math.pi))
            grad = (cdf + pre * bell).astype(BF16)
            kept.act[2 * tile] = out[:, :128]
            kept.act[2 * tile + 1] = out[:, 128:]
            kept.slope[2 * tile] = grad[:, :128]
            kept.slope[2 * tile + 1] = grad[:, 128:]
        tick()
    for k in range(3):
        need(2, k)
    for side in range(2):
        for tile in range(3):
            columns = slice(256 * tile, 256 * tile + 256)
            pair = (2 * tile, 2 * tile + 1)
            rows = [read_rows(weights, 4 * side + step, pair) for step in range(4)]
            acc[:, columns] += dot(
                chunks_of(kept.act, 12 * side, 12), jnp.concatenate(rows, axis=0)
            )
        tick()

    def second_norm(rows):
        normal, scale = normalize(acc[rows, :])
        kept.normal2[rows, :] = normal
        kept.scales[rows, 1:2] = scale

    by_rows(second_norm)


def backward_layer(
    state, grad, norms, weights, kept, acc, low, turned, grad_norms, grad_bias, ready, tick
):
    def norm_back(which, normal_of, grad_of):
        sums = [jnp.zeros((1, 768), F32), jnp.zeros((1, 768), F32)]

        def step(rows):
            grad, normal = grad_of(rows), normal_of(rows)
            sums[0] += jnp.sum(grad * normal, axis=0, keepdims=True)
            sums[1] += jnp.sum(grad, axis=0, keepdims=True)
            scale = kept.scales[rows, which : which + 1]
            out = normalize_back(grad, norms[2 * which : 2 * which + 1, :], normal, scale)
            acc[rows, :] = out
            low[rows, :] = out.astype(BF16)

        by_rows(step)
        grad_norms[2 * which] = sums[0]
        grad_norms[2 * which + 1] = sums[1]

    norm_back(1, lambda rows: kept.normal2[rows, :], grad)
    for step in range(8):
        branch = low[...]
        grad_act = dot(branch, read_rows(weights, step), NT)
        pre_low = (grad_act * chunks_of(kept.slope, 3 * step, 3).astype(F32)).astype(BF16)
        for at in range(3):
            kept.slope[3 * step + at] = pre_low[:, 128 * at : 128 * at + 128]
        grad_bias[step] = jnp.sum(pre_low.astype(F32), axis=0, keepdims=True)
        write_rows(weights, step, dot(chunks_of(kept.act, 3 * step, 3), branch, TN))
        if step == 7:
            for k in range(3):
                ready(2, k)
        if step % 2:
            tick()
    turned[...] = kept.first_low[...].T
    for k in range(3):
        for inner in range(4):
            pre_low = chunks_of(kept.slope, 8 * k + 2 * inner, 2)
            acc[...] += dot(pre_low, read_tile(weights, 1, k, inner), NT)
            write_tile(weights, 1, k, inner, dot(turned[...], pre_low))
        ready(1, k)
        tick()

    norm_back(0, lambda rows: kept.normal1[rows, :].astype(F32), lambda rows: acc[rows, :])
    turned[...] = chunks_of(kept.mixed, 0, 6).T
    for side in range(2):
        groups = GROUPS[8 * side : 8 * side + 8]
        tiles = [read_tile(weights, 0, 2, 1 + tile, groups) for tile in range(3)]
        total = dot(low[...], jnp.concatenate(tiles, axis=1), NT)
        for chunk in range(3):
            columns = slice(128 * chunk, 128 * chunk + 128)
            kept.mixed[3 * side + chunk] = total[:, columns].astype(BF16)
    for tile in range(3):
        part_low = low[:, 256 * tile : 256 * tile + 256]
        write_tile(weights, 0, 2, 1 + tile, dot(turned[...], part_low))
    tick()

    low_half = lax.broadcasted_iota(jnp.int32, (256, 128), 1) < 64
    halves = half_masks()
    for pair in range(6):
        queries, keys, values = kept.proj[pair], kept.proj[6 + pair], kept.proj[12 + pair]
        back = kept.mixed[pair]
        scores, grads_k, grads_v = [], [], []
        for side in range(2):
            soft = kept.soft[2 * pair + side]
            weight = soft.astype(F32)
            grad_soft = dot(values, back * (halves[side] * jnp.asarray(0.125, BF16)), NT)
            inner = jnp.sum(weight * grad_soft, axis=0, keepdims=True)
            grad_score = (weight * (grad_soft - inner)).astype(BF16)
            scores.append(grad_score)
            grads_k.append(dot(grad_score, queries))
            grads_v.append(dot(soft, back))
        both_keys = jnp.concatenate([keys * halves[0], keys * halves[1]], axis=0)
        kept.proj[pair] = dot(jnp.concatenate(scores, axis=0), both_keys, TN).astype(BF16)
        for first, both in ((6, grads_k), (12, grads_v)):
            kept.proj[first + pair] = jnp.where(low_half, both[0], both[1]).astype(BF16)
        if pair % 3 == 2:
            tick()

    def turn(rows):
        turned[:, rows] = state(rows).astype(BF16).T

    for first in (0, 128):
        turn(pl.ds(first, 128))
    left = []
    for k in range(3):
        for inner in range(TILES[k]):
            pair = chunks_of(kept.proj, 8 * k + 2 * inner, 2)
            acc[...] += dot(pair, read_tile(weights, 0, k, inner), NT)
            write_tile(weights, 0, k, inner, dot(turned[...], pair))
        ready(0, k)
        tick()


def member_rows(extra, who):
    y_lo, x_lo, core = who // 4, who // 2 % 2, who % 2
    return jnp.concatenate(
        [extra[0, core, z, 2 * y_hi + y_lo, 2 * x_hi + x_lo] for x_hi, z, y_hi in GROUPS], axis=0
    )


def write_member_rows(extra, who, values):
    y_lo, x_lo, core = who // 4, who // 2 % 2, who % 2
    for at, (x_hi, z, y_hi) in enumerate(GROUPS):
        extra[0, core, z, 2 * y_hi + y_lo, 2 * x_hi + x_lo] = values[32 * at : 32 * at + 32].astype(BF16)


def pick_rows(rows, columns, width):
    row = lax.broadcasted_iota(jnp.int32, (rows, columns), 0)
    column = lax.broadcasted_iota(jnp.int32, (rows, columns), 1)
    from_first = column - width * lax.shift_right_logical(row, 2)
    inside = jnp.logical_and(from_first >= 0, from_first < width)
    return jnp.where(inside, 1.0, 0.0).astype(BF16)


def pick_lanes(rows, columns, width):
    row = lax.broadcasted_iota(jnp.int32, (rows, columns), 0).astype(F32)
    column = lax.broadcasted_iota(jnp.int32, (rows, columns), 1).astype(F32)
    remainder = column - width * jnp.floor((column + 0.5) * (1.0 / width))
    return jnp.where(remainder == row, 1.0, 0.0)


def read_time_bias(extra):
    small = member_rows(extra, 7)
    pick, lanes = pick_rows(128, 128, 4), pick_lanes(8, 128, 4)
    return jnp.concatenate(
        [
            jnp.sum(dot(small[128 * at : 128 * at + 128], pick, TN)[:8] * lanes, axis=0, keepdims=True)
            for at in range(4)
        ],
        axis=1,
    )


def read_vectors(extra, norms, bias):
    small = member_rows(extra, 7)
    pick, lanes = pick_rows(256, 384, 6), pick_lanes(8, 384, 6)
    for at in range(2):
        spread = dot(small[256 * at : 256 * at + 256], pick, TN)
        for vector in range(8):
            value = jnp.sum(spread[8 + 8 * vector : 16 + 8 * vector] * lanes, axis=0, keepdims=True)
            norms[vector // 4, vector % 4 : vector % 4 + 1, 384 * at : 384 * at + 384] = value
    pick, lanes = pick_rows(64, 384, 24), pick_lanes(24, 384, 24)
    for at in range(8):
        spread = dot(small[64 * at : 64 * at + 64], pick, TN)
        for layer in range(2):
            value = spread[72 + 24 * layer : 96 + 24 * layer] * lanes
            bias[layer, :, 384 * at : 384 * at + 384] = jnp.sum(value, axis=0, keepdims=True)


def time_weights(extra):
    return jnp.concatenate([member_rows(extra, who) for who in range(6)], axis=1)


def time_forward(extra, emb, time_bias, time_pre, time_act, temb):
    by_chunk = dot(emb[...], member_rows(extra, 6))
    pre = jnp.concatenate([by_chunk[at : at + 1] for at in range(4)], axis=1) + time_bias
    act = (pre * lax.logistic(pre)).astype(BF16)
    time_pre[...] = pre
    time_act[...] = act.astype(F32)
    temb[...] = dot(jnp.broadcast_to(act, (8, 512)), time_weights(extra))[0:1]


def high_low(values):
    high = values.astype(BF16).astype(F32)
    return high, values - high


def time_backward(extra, emb, time_pre, time_act, grad, grad_norms, grad_bias):
    zero = lambda rows, columns: jnp.zeros((rows, columns), F32)
    total = jnp.sum(grad, axis=0, keepdims=True)
    both = jnp.concatenate(high_low(total) + (zero(6, 768),), axis=0).astype(BF16)
    grad_act = jnp.sum(dot(both, time_weights(extra), NT), axis=0, keepdims=True)
    pre = time_pre[...]
    gate = lax.logistic(pre)
    grad_pre = grad_act * gate * (1.0 + pre * (1.0 - gate))
    act = time_act[...]
    acts = jnp.concatenate([act, act, zero(6, 512)], axis=0).astype(BF16)
    for who in range(6):
        write_member_rows(extra, who, dot(acts, both[:, 128 * who : 128 * who + 128], TN))
    high, low = high_low(grad_pre)
    by_chunk = [side[:, 128 * at : 128 * at + 128] for side in (high, low) for at in range(4)]
    write_member_rows(extra, 6, dot(emb[...], jnp.concatenate(by_chunk, axis=0).astype(BF16), TN))

    pieces = []
    pick, lanes = pick_rows(64, 384, 24), pick_lanes(24, 384, 24)
    for at in range(8):
        rows = [zero(72, 384)] + [lanes * grad_bias[layer, at] for layer in range(2)] + [zero(8, 384)]
        pieces.append(dot(pick, jnp.concatenate(rows, axis=0).astype(BF16), NT))
    small = jnp.concatenate(pieces, axis=0)
    pick, lanes, pieces = pick_rows(256, 384, 6), pick_lanes(8, 384, 6), []
    for at in range(2):
        rows = [zero(8, 384)]
        for layer in range(2):
            for vector in range(4):
                rows.append(lanes * grad_norms[layer, vector, :, 384 * at : 384 * at + 384])
        rows.append(zero(56, 384))
        pieces.append(dot(pick, jnp.concatenate(rows, axis=0).astype(BF16), NT))
    small += jnp.concatenate(pieces, axis=0)
    pick, lanes, pieces = pick_rows(128, 128, 4), pick_lanes(8, 128, 4), []
    for at in range(4):
        rows = [lanes * grad_pre[:, 128 * at : 128 * at + 128], zero(120, 128)]
        pieces.append(dot(pick, jnp.concatenate(rows, axis=0).astype(BF16), NT))
    write_member_rows(extra, 7, small + jnp.concatenate(pieces, axis=0))


class Clock:
    def __init__(self, plan):
        self.plan, self.now = plan, 0

    def tick(self):
        self.now += 1
        for travel, until in self.plan.get(self.now, ()):
            travel.advance(until)


def whole_kernel(*refs):
    refs = list(refs)
    take = lambda count: [refs.pop(0) for _ in range(count)]
    src_len, total_len = take(2)
    qkv, out_w, ffn_in, ffn_out, time_in, time_out, small, emb = take(8)
    tokens, cotangent = take(2)
    got_a, got_b, kept_b, output_part, grad_part = take(5)
    weights = take(2)
    kept = [Kept(take(len(Kept.shapes))) for _ in range(2)]
    acc, turned, shut, norms, bias, grad_norms, grad_bias = take(7)
    extra, time_pre, time_act, temb = take(4)
    tokens_all, cotangent_all, leaving = take(3)
    send_a, send_b, rows, rows_b = take(4)
    pair, half, full = take(3)
    buffers_x = take(5)
    spread_sems, reduce_sems = take(2), take(2)
    first_sems, last_sems, move_sems = take(3)
    pair_free, ring_free, gone_free = take(3)

    at = here()
    mine, core = member(at), at["core"]
    my_stream = stream_of(at)
    greet(at)

    def pack(layer):
        for to in range(8):
            for k in range(6):
                chunk = to + 8 * (k % 3)
                source, column = (qkv, chunk) if chunk < 18 else (out_w, chunk - 18)
                if k >= 3:
                    source, column = ffn_in, chunk
                piece = source[layer, :, 128 * column : 128 * column + 128]
                send_a[layer, to, k, 0:6, :] = piece.astype(F32)
        for k in range(3):
            column = pl.multiple_of(128 * (3 * (1 - core) + k), 128)
            send_b[layer, k] = ffn_out[layer, :, pl.ds(column, 128)].astype(F32)

    class Trade:
        def __init__(self, layer, sems, slots):
            self.sems = lambda kind: sems.at[layer, kind]
            self.all_a, self.all_b = got_a.at[layer, pl.ds(0, 7), pl.ds(0, slots)], got_b.at[layer]
            for flip in FLIPS:
                to = flipped(at, *flip)
                src = send_a.at[layer, member(to), pl.ds(0, slots)]
                dst = got_a.at[layer, mine, pl.ds(0, slots)]
                remote(src, dst, self.sems(0), self.sems(1), to).start()
            twin = flipped(at, 0, 0, 1)
            remote(send_b.at[layer], got_b.at[layer], self.sems(2), self.sems(3), twin).start()
            got_a[layer, mine] = send_a[layer, mine]

        def arrived(self):
            wait_bytes(self.all_a, self.sems(1))
            wait_bytes(self.all_b, self.sems(3))

        def left(self):
            wait_bytes(self.all_a, self.sems(0))
            wait_bytes(self.all_b, self.sems(2))

    class Move:
        def __init__(self, number, src, dst, split):
            self.sems = lambda kind: move_sems.at[number, kind]
            rows_of = lambda who: pl.ds(pl.multiple_of(64 * who, 64), 64)
            own_src = src.at[rows_of(my_stream)] if split else src.at[my_stream]
            own_dst = dst.at[my_stream] if split else dst.at[rows_of(my_stream)]
            self.keep = pltpu.make_async_copy(own_src, own_dst, self.sems(0))
            self.keep.start()
            for flip in range(1, 4):
                to = flipped(at, 0, flip // 2, flip % 2)
                there = src.at[rows_of(stream_of(to))] if split else src.at[stream_of(to)]
                remote(there, own_dst, self.sems(1), self.sems(2), to).start()

        def wait(self):
            self.keep.wait()
            for kind in (1, 2):
                wait_bytes(tokens_all.at[pl.ds(0, 192)], self.sems(kind))

    pack(0)
    for to in range(8):
        send_a[0, to, 6] = jnp.zeros((8, 128), F32)
        if to < 6:
            send_a[0, to, 6, 0:4, :] = time_out[:, 128 * to : 128 * to + 128].astype(F32)
        elif to == 6:
            for chunk in range(4):
                columns = slice(128 * chunk, 128 * chunk + 128)
                send_a[0, to, 6, chunk : chunk + 1, :] = time_in[:, columns].astype(F32)
        else:
            send_a[0, to, 6, 0:1, :] = small[...]
    first = [Trade(0, first_sems, 7)]
    pack(1)
    first.append(Trade(1, first_sems, 6))
    bring_tokens = Move(0, tokens, tokens_all, False)

    mine_at = [tuple(at[name] for name in AXES[k]) for k in range(3)]

    def assemble_part(layer, part):
        for k in range(3):
            if part == 2:
                column = pl.multiple_of(128 * (3 * core + k), 128)
                rows_b[core] = ffn_out[layer, :, pl.ds(column, 128)].astype(F32)
                rows_b[1 - core] = got_b[layer, k]
                unit = rows_b[...].reshape(48, 128)
            else:
                for frm in range(8):
                    rows[6 * frm : 6 * frm + 6, :] = got_a[layer, frm, 3 * part + k, 0:6, :]
                unit = rows[...]
            weights[layer][(part, k, core) + mine_at[k]] = unit.astype(BF16)

    spread = {}
    for layer in range(2):
        for part in range(3):
            blocks = weights[layer].at[part]
            ring = layer + part > 0
            spread[layer, part] = Spread(3 * layer + part, blocks, AXES, at, spread_sems, ring)
    spread_x = Spread(6, extra, AXES[:1], at, spread_sems, False)

    def advance(*steps):
        for layer, part, until in steps:
            spread[layer, part].advance(until)

    first[0].arrived()
    assemble_part(0, 0)
    advance((0, 0, 1))
    for frm in range(8):
        rows[4 * frm : 4 * frm + 4, :] = got_a[0, frm, 6, 0:4, :]
    extra[0, core, at["z"], at["y"], at["x"]] = rows[0:32, :].astype(BF16)
    spread_x.advance(1)
    for part in (1, 2):
        assemble_part(0, part)
        advance((0, part, 1))
    advance((0, 0, 2))
    spread_x.advance(2)
    advance((0, 1, 2), (0, 2, 2))
    first[1].arrived()
    for part in range(3):
        assemble_part(1, part)
    advance((0, 0, 4))
    spread_x.advance(4)
    advance((0, 1, 3), (0, 2, 3), (1, 0, 1), (1, 1, 1), (1, 2, 1))
    advance((0, 0, 5))
    spread_x.advance(7)
    time_forward(extra, emb, read_time_bias(extra), time_pre, time_act, temb)
    advance((0, 1, 4), (0, 2, 4), (0, 0, 6))
    read_vectors(extra, norms, bias)
    lens = (src_len[my_stream], total_len[my_stream])
    key_at = lax.broadcasted_iota(jnp.int32, (256, 128), 0)
    bound = jnp.where(key_at < 128, lens[0], 128 + lens[1] - lens[0])
    shut[...] = jnp.where(key_at < bound, 0.0, -1e30)
    bring_tokens.wait()
    bring_cotangent = Move(1, cotangent, cotangent_all, False)

    plan = {
        1: [(1, 0, 2)],
        2: [(1, 1, 2)],
        3: [(1, 2, 2)],
        4: [(1, 0, 3), (0, 1, 5)],
        5: [(1, 1, 3), (1, 2, 3)],
        6: [(0, 2, 5), (1, 0, 4)],
        9: [(0, 2, 6), (1, 1, 4)],
        11: [(1, 0, 5), (1, 2, 4)],
        12: [(1, 1, 5)],
        17: [(1, 2, 5)],
    }
    for stops in plan.values():
        stops[:] = [(spread[layer, part], until) for layer, part, until in stops]
    clock = Clock(plan)
    states = [
        lambda rows: tokens_all[rows, :].astype(F32) + temb[...],
        lambda rows: kept[0].normal2[rows, :] * norms[0, 2:3, :] + norms[0, 3:4, :],
    ]
    for layer in range(2):
        forward_layer(
            states[layer],
            norms.at[layer],
            bias.at[layer],
            shut,
            weights[layer],
            kept[layer],
            acc,
            lambda part, k: spread[layer, part].advance(7),
            clock.tick,
        )

    def leave(rows):
        final = kept[1].normal2[rows, :] * norms[1, 2:3, :] + norms[1, 3:4, :]
        leaving[rows, :] = final.astype(BF16)

    by_rows(leave)
    give_output = Move(2, leaving, output_part, True)
    for travel in list(spread.values()) + [spread_x]:
        travel.finish()
    for trade in first:
        trade.left()
    bring_cotangent.wait()

    there = pl.ds(pl.multiple_of(24 * (1 - core), 8), 24)
    near = pl.ds(pl.multiple_of(24 * core, 8), 24)

    def deliver(layer, part, k, total):
        rows[...] = total
        if part == 2:
            send_b[layer, k] = rows[there, :]
            kept_b[layer, k] = rows[near, :]
            return
        for to in range(8):
            send_a[layer, to, 3 * part + k, 0:6, :] = rows[6 * to : 6 * to + 6, :]

    def deliver_extra(_, total):
        rows[0:32, :] = total
        for to in range(8):
            send_a[0, to, 6, 0:4, :] = rows[4 * to : 4 * to + 4, :]

    around = [moved(at, axis, by) for axis in "xyz" for by in (1, -1, 2)]
    reduce = {}

    near_by = [moved(at, axis, by) for axis in "xyz" for by in (1, -1)]

    def gone(part):
        reduce[1, part].crossed()
        for to in around:
            signal(gone_free.at[part], to)

    def wait_gone(part):
        pl.semaphore_wait(gone_free.at[part], len(around))

    def free(part):
        reduce[1, part].advance(4)
        signal(pair_free.at[part], flipped(at, 0, 0, 1))
        for to in near_by:
            signal(ring_free.at[part], to)

    def freed(part):
        pl.semaphore_wait(pair_free.at[part], 1)
        pl.semaphore_wait(ring_free.at[part], len(near_by))

    for layer in range(2):
        for part in range(3):
            spare = weights[1].at[part, :, 1 - core, layer]
            small_buffers = [spare.at[:, pl.ds(0, 3)], spare.at[:, 3, pl.ds(0, 3)]]
            reduce[layer, part] = Reduce(
                3 * layer + part,
                weights[layer].at[part],
                [pair.at[part], half.at[part], full.at[part]] + small_buffers,
                partial(deliver, layer, part),
                AXES,
                at,
                reduce_sems,
                layer + part > 0,
                None if layer else partial(freed, part),
                partial(wait_gone, part) if layer else None,
            )
    reduce_x = Reduce(6, extra, buffers_x, deliver_extra, AXES[:1], at, reduce_sems, False, None, None)

    class Stop:
        def __init__(self, run):
            self.run, self.done = run, False

        def advance(self, until):
            if not self.done:
                self.run()
            self.done = True

    frees = [Stop(partial(free, part)) for part in range(3)]
    gones = [Stop(partial(gone, part)) for part in range(3)]
    second = lambda part, until: (reduce[1, part], until)
    early = lambda part, until: (reduce[0, part], until)
    plan = {
        6: [second(2, 2)],
        8: [second(1, 2)],
        10: [second(2, 3), (gones[2], 0)],
        13: [second(1, 3), (gones[1], 0), second(0, 2)],
        18: [(frees[2], 0), early(2, 1)],
        20: [early(2, 2)],
        22: [(frees[1], 0), early(1, 1), second(0, 3), (gones[0], 0)],
        23: [early(1, 2), second(2, 5)],
        24: [early(2, 3)],
        26: [second(1, 5)],
    }
    clock = Clock(plan)
    grads = [lambda rows: acc[rows, :], lambda rows: cotangent_all[rows, :].astype(F32)]
    for layer in (1, 0):
        backward_layer(
            states[layer],
            grads[layer],
            norms.at[layer],
            weights[layer],
            kept[layer],
            acc,
            cotangent_all,
            turned,
            grad_norms.at[layer],
            grad_bias.at[layer],
            lambda part, k: reduce[layer, part].trade(k) if layer else None,
            clock.tick,
        )

    give_output.wait()
    by_rows(lambda rows: leaving.__setitem__((rows, slice(None)), acc[rows, :].astype(BF16)))
    give_grad = Move(3, leaving, grad_part, True)
    early(1, 0)[0].advance(3)
    time_backward(extra, emb, time_pre, time_act, acc[...], grad_norms, grad_bias)
    reduce_x.advance(1)
    frees[0].advance(0)
    early(0, 0)[0].advance(1)
    rest = [
        second(2, 6), early(0, 2), (reduce_x, 2), early(2, 4), second(1, 6), (reduce_x, 3), early(0, 3),
        early(1, 4), (reduce_x, 4), second(0, 5), second(2, 7), early(2, 5), second(1, 7), (reduce_x, 6),
        early(0, 4), early(1, 5), second(0, 6), (reduce_x, 7), early(2, 6), early(0, 5), early(1, 6),
        second(0, 7),
    ]
    for travel, until in rest:
        travel.advance(until)
    last = [Trade(1, last_sems, 6)]
    for travel, until in (early(2, 7), early(0, 6), early(1, 7), early(0, 7)):
        travel.advance(until)
    last.append(Trade(0, last_sems, 7))
    for (layer, part), travel in reduce.items():
        travel.departed()
        if layer == 0:
            travel.crossed()
    reduce_x.departed()
    reduce_x.crossed()
    for trade in last:
        trade.arrived()
        trade.left()
    give_grad.wait()


def whole(src_len, total_len, qkv, out_w, ffn_in, ffn_out, time_in, time_out, small, emb, tokens, cotangent):
    vmem, anywhere = pl.BlockSpec(memory_space=pltpu.VMEM), pl.BlockSpec(memory_space=pl.ANY)
    smem = pl.BlockSpec(memory_space=pltpu.SMEM)
    dma, regular = pltpu.SemaphoreType.DMA, pltpu.SemaphoreType.REGULAR
    buffers = lambda lead, unit: [
        pltpu.VMEM(lead + shape + unit, BF16)
        for shape in ((4, 4, 4), (2, 2, 4), (2, 4, 4), (3, 4), (3,))
    ]
    scratch = [pltpu.VMEM((3, 3, 2, 4, 4, 4) + UNIT, BF16) for _ in range(2)]
    for _ in range(2):
        scratch += [pltpu.VMEM(shape, kind) for _, shape, kind in Kept.shapes]
    scratch += [
        pltpu.VMEM((256, 768), F32),
        pltpu.VMEM((768, 256), BF16),
        pltpu.VMEM((256, 128), F32),
        pltpu.VMEM((2, 8, 768), F32),
        pltpu.VMEM((2, 1, 3072), F32),
        pltpu.VMEM((2, 4, 1, 768), F32),
        pltpu.VMEM((2, 8, 1, 384), F32),
        pltpu.VMEM((1, 2, 4, 4, 4) + EXTRA, BF16),
        pltpu.VMEM((1, 512), F32),
        pltpu.VMEM((1, 512), F32),
        pltpu.VMEM((1, 768), F32),
        pltpu.VMEM((256, 768), BF16),
        pltpu.VMEM((256, 768), BF16),
        pltpu.VMEM((256, 768), BF16),
        pltpu.VMEM((2, 8, 7, 8, 128), F32),
        pltpu.VMEM((2, 3, 24, 128), F32),
        pltpu.VMEM((48, 128), F32),
        pltpu.VMEM((2, 24, 128), F32),
    ]
    scratch += buffers((3, 3), UNIT)[:3] + buffers((1,), EXTRA)
    scratch += [
        dma((7, SPREAD_SEMS)),
        dma((7, 2)),
        dma((7, REDUCE_SEMS)),
        dma((7, 2)),
        dma((2, 4)),
        dma((2, 4)),
        dma((4, 3)),
        regular((3,)),
        regular((3,)),
        regular((3,)),
    ]
    return pl.pallas_call(
        whole_kernel,
        out_shape=[
            jax.ShapeDtypeStruct((2, 8, 7, 8, 128), F32),
            jax.ShapeDtypeStruct((2, 3, 24, 128), F32),
            jax.ShapeDtypeStruct((2, 3, 24, 128), F32),
            jax.ShapeDtypeStruct((4, 64, 768), BF16),
            jax.ShapeDtypeStruct((4, 64, 768), BF16),
        ],
        in_specs=[smem] * 2 + [vmem] * 8 + [anywhere] * 2,
        out_specs=[vmem] * 3 + [anywhere] * 2,
        scratch_shapes=scratch,
        compiler_params=pltpu.CompilerParams(
            collective_id=1, has_side_effects=True, vmem_limit_bytes=VMEM_BYTES
        ),
        name="whole",
    )(src_len, total_len, qkv, out_w, ffn_in, ffn_out, time_in, time_out, small, emb, tokens, cotangent)


def finish_kernel(
    got_a, got_b, kept_b, output, grad, out, grad_x, g_tin, g_tout, g_small, g_qkv, g_out, g_in, g_ffn
):
    core = lax.rem(lax.axis_index("stream"), 2)
    out[...] = output[...]
    grad_x[...] = grad[...].astype(F32)
    for frm in range(8):
        for layer in range(2):
            for k in range(6):
                chunk = frm + 8 * (k % 3)
                piece = got_a[layer, frm, k, 0:6, :]
                if k >= 3:
                    g_in[layer, :, 128 * chunk : 128 * chunk + 128] = piece
                elif chunk < 18:
                    g_qkv[layer, :, 128 * chunk : 128 * chunk + 128] = piece
                else:
                    g_out[layer, :, 128 * (chunk - 18) : 128 * (chunk - 18) + 128] = piece
        if frm < 6:
            g_tout[:, 128 * frm : 128 * frm + 128] = got_a[0, frm, 6, 0:4, :]
        elif frm == 6:
            for chunk in range(4):
                g_tin[:, 128 * chunk : 128 * chunk + 128] = got_a[0, frm, 6, chunk : chunk + 1, :]
        else:
            g_small[...] = got_a[0, frm, 6, 0:1, :]
    for layer in range(2):
        for k in range(3):
            near = pl.ds(pl.multiple_of(128 * (3 * core + k), 128), 128)
            there = pl.ds(pl.multiple_of(128 * (3 * (1 - core) + k), 128), 128)
            g_ffn[layer, :, near] = kept_b[layer, k]
            g_ffn[layer, :, there] = got_b[layer, k]


def finish(got_a, got_b, kept_b, output, grad):
    shapes = [
        ((4, 64, 768), BF16),
        ((4, 64, 768), F32),
        ((1, 512), F32),
        ((4, 768), F32),
        ((1, 128), F32),
        ((2, 6, 2304), F32),
        ((2, 6, 768), F32),
        ((2, 6, 3072), F32),
        ((2, 24, 768), F32),
    ]
    vmem = pl.BlockSpec(memory_space=pltpu.VMEM)
    return pl.pallas_call(
        finish_kernel,
        out_shape=[jax.ShapeDtypeStruct(shape, kind) for shape, kind in shapes],
        in_specs=[vmem] * 5,
        out_specs=[vmem] * len(shapes),
        compiler_params=pltpu.CompilerParams(vmem_limit_bytes=VMEM_BYTES),
        name="lay_out_results",
    )(got_a, got_b, kept_b, output, grad)


def time_features(timestep):
    column = lax.broadcasted_iota(jnp.int32, (8, 512), 1)
    row = lax.broadcasted_iota(jnp.int32, (8, 512), 0)
    feature = column // 4
    half = jnp.where(feature < 64, feature, feature - 64).astype(F32)
    angles = timestep * jnp.exp(-math.log(10000.0) * half / 64)
    values = jnp.where(feature < 64, jnp.sin(angles), jnp.cos(angles))
    return jnp.where(column % 4 == row % 4, values, 0.0).astype(BF16)


def per_device(
    tokens,
    timestep,
    src_len,
    total_len,
    time_in,
    time_bias,
    time_out,
    qkv_weight,
    out_weight,
    norm1_gain,
    norm1_bias,
    ffn_in,
    ffn_bias,
    ffn_out,
    norm2_gain,
    norm2_bias,
    cotangent,
):
    stream = lax.axis_index("stream")
    my_step = jnp.sum(jnp.where(jnp.arange(4) == stream, timestep, 0.0))
    vectors = [(time_bias, 0)]
    for layer in range(2):
        for at, vector in enumerate((norm1_gain, norm1_bias, norm2_gain, norm2_bias)):
            vectors.append((vector[layer], 8 + 32 * layer + 8 * at))
        vectors.append((ffn_bias[layer], 72 + 24 * layer))
    small = sum(
        jnp.pad(vector.astype(F32), (first, 128 - first - vector.shape[0])) for vector, first in vectors
    )[None, :]
    got = whole(
        src_len,
        total_len,
        qkv_weight,
        out_weight,
        ffn_in,
        ffn_out,
        time_in,
        time_out,
        small,
        time_features(my_step),
        tokens,
        cotangent,
    )
    out, grad_x, g_tin, g_tout, g_small, g_qkv, g_out, g_in, g_ffn = finish(*got)
    g_norm = g_small[0, 8:72].reshape(2, 4, 8)[:, :, :6]
    return (
        out,
        grad_x,
        g_tin,
        g_small[0, :4],
        g_tout,
        g_qkv,
        g_out,
        g_norm[:, 0],
        g_norm[:, 1],
        g_in,
        g_small[0, 72:120].reshape(2, 24),
        g_ffn,
        g_norm[:, 2],
        g_norm[:, 3],
    )


def solution(mesh):
    in_specs = (
        P("batch", "stream", None),
        P("batch"),
        P("batch"),
        P("batch"),
        P(("batch", "stream"), None),
        P(("batch", "stream")),
        P(("batch", "stream"), None),
        P(None, ("batch", "stream"), None),
        P(None, ("batch", "stream"), None),
        P(None, ("batch", "stream")),
        P(None, ("batch", "stream")),
        P(None, ("batch", "stream"), None),
        P(None, ("batch", "stream")),
        P(None, ("batch", "stream"), None),
        P(None, ("batch", "stream")),
        P(None, ("batch", "stream")),
        P("batch", "stream", None),
    )
    out_specs = (
        P("batch", "stream", None),
        P("batch", "stream", None),
        P(("batch", "stream"), None),
        P(("batch", "stream")),
        P(("batch", "stream"), None),
        P(None, ("batch", "stream"), None),
        P(None, ("batch", "stream"), None),
        P(None, ("batch", "stream")),
        P(None, ("batch", "stream")),
        P(None, ("batch", "stream"), None),
        P(None, ("batch", "stream")),
        P(None, ("batch", "stream"), None),
        P(None, ("batch", "stream")),
        P(None, ("batch", "stream")),
    )
    return jax.shard_map(
        per_device, mesh=mesh, in_specs=in_specs, out_specs=out_specs, check_vma=False
    )
```

```python
from functools import partial
import math

import jax
import jax.numpy as jnp
import numpy as np
from jax import lax
from jax.experimental import pallas as pl
from jax.experimental.pallas import tpu as pltpu
from jax.sharding import PartitionSpec as P

F32, BF16 = jnp.float32, jnp.bfloat16
EPS = 1e-05
NN = (((1,), (0,)), ((), ()))
NT = (((1,), (1,)), ((), ()))
TN = (((0,), (0,)), ((), ()))
MESH = pl.DeviceIdType.MESH
VMEM_BYTES = 65400 * 1024
AXES = ("zyx", "xzy", "yxz")
UNIT = (48, 128)
EXTRA = (16, 128)
GROUPS = [(x_hi, z, y_hi) for x_hi in range(2) for z in range(4) for y_hi in range(2)]
FLIPS = [(flip // 4, flip // 2 % 2, flip % 2) for flip in range(1, 8)]
TILES = (4, 4, 1)
SPREAD_SEMS, REDUCE_SEMS = 6, 7


def dot(left, right, dims=NN):
    return lax.dot_general(left, right, dims, preferred_element_type=F32)


def here():
    batch, stream = lax.axis_index("batch"), lax.axis_index("stream")
    return {
        "x": 2 * lax.div(batch, 16) + lax.div(stream, 2),
        "y": lax.rem(batch, 4),
        "z": lax.rem(lax.div(batch, 4), 4),
        "core": lax.rem(stream, 2),
    }


def device(at):
    return (
        lax.div(at["x"], 2) * 16 + at["z"] * 4 + at["y"],
        lax.rem(at["x"], 2) * 2 + at["core"],
    )


def moved(at, axis, by):
    return {**at, axis: lax.rem(at[axis] + by + 4, 4)}


def flipped(at, flip_y, flip_x, flip_core):
    new = dict(at)
    if flip_y:
        new["y"] = at["y"] + 1 - 2 * lax.rem(at["y"], 2)
    if flip_x:
        new["x"] = at["x"] + 1 - 2 * lax.rem(at["x"], 2)
    if flip_core:
        new["core"] = 1 - at["core"]
    return new


def member(at):
    return lax.rem(at["y"], 2) * 4 + lax.rem(at["x"], 2) * 2 + at["core"]


def stream_of(at):
    return lax.rem(at["x"], 2) * 2 + at["core"]


def signal(sem, to):
    pl.semaphore_signal(sem, inc=1, device_id=device(to), device_id_type=MESH)


def greet(at):
    partners = [flipped(at, *flip) for flip in FLIPS]
    partners += [moved(at, "z", 1), moved(at, "z", -1)]
    partners += [moved(at, axis, 2 * lax.rem(at[axis], 2) - 1) for axis in "xy"]
    partners += [moved(at, axis, 2) for axis in "xyz"]
    barrier = pltpu.get_barrier_semaphore()
    for partner in partners:
        signal(barrier, partner)
    return len(partners)


def remote(src, dst, send_sem, recv_sem, to):
    return pltpu.make_async_remote_copy(
        src_ref=src,
        dst_ref=dst,
        send_sem=send_sem,
        recv_sem=recv_sem,
        device_id=device(to),
        device_id_type=MESH,
    )


def wait_bytes(ref, sem):
    pltpu.make_async_copy(ref, ref, sem).wait()


class Travel:
    def __init__(self, number, blocks, orders, at, sems, ring):
        self.at, self.ring, self.blocks = at, ring, blocks
        self.orders = orders
        self.places = [[at[axis] for axis in order] for order in orders]
        self.recv_sem = lambda kind: sems[0].at[number, kind]
        self.send_sem = lambda kind: sems[1].at[number, kind]
        self.done, self.leaving = 0, None
        self.own = [blocks.at[k, at["core"]] for k in range(len(orders))]
        self.gone = [blocks.at[k, 1 - at["core"]] for k in range(len(orders))]

    def cells(self, count):
        return self.blocks.at[:, 0, 0, 0, pl.ds(0, count)]

    def lines(self, count):
        return self.blocks.at[:, 0, 0, pl.ds(0, count)]

    def planes(self, count):
        return self.blocks.at[:, 0, pl.ds(0, count)]

    def turn(self, k, level, by):
        return lax.rem(self.places[k][level] + by + 4, 4)

    def neighbour(self, k, level, by):
        return moved(self.at, self.orders[k][level], by)

    def twin(self):
        return flipped(self.at, 0, 0, 1)

    def arrive(self, kind, total):
        wait_bytes(total, self.recv_sem(kind))

    def depart(self, kind, pieces, total):
        self.departed()
        for src, dst, to in pieces:
            remote(src, dst, self.send_sem(0), self.recv_sem(kind), to).start()
        self.leaving = total

    def departed(self):
        if self.leaving is not None:
            wait_bytes(self.leaving, self.send_sem(0))
        self.leaving = None

    def crossed(self):
        wait_bytes(self.blocks.at[:, 0], self.send_sem(1))

    def advance(self, until):
        while self.done < until:
            self.step(self.done)
            self.done += 1


class Spread(Travel):
    def share(self, ref):
        remote(ref, ref, self.send_sem(1), self.recv_sem(5), self.twin()).start()

    def pass_on(self, kind, level, came, total):
        pieces = []
        for k in range(len(self.orders)):
            for side, by in ((0, -1), (1, 1)):
                piece = came(k, by).at[pl.ds(2 * side, 2)]
                pieces.append((piece, piece, self.neighbour(k, level, -by)))
        self.depart(kind, pieces, total)

    def send_block(self, kind, level, sides, block, total):
        pieces = []
        for k, place in enumerate(self.places):
            mine = block(self.own[k], place)
            pieces += [(mine, mine, self.neighbour(k, level, by)) for by in sides]
        self.depart(kind, pieces, total)

    def step(self, number):
        own = self.own
        if number == 0:
            self.send_block(0, 2, (1, -1, 2), lambda ref, to: ref.at[tuple(to)], self.cells(3))
        elif number == 1:
            self.arrive(0, self.cells(3))
            sides = (1, -1) if self.ring else (1, -1, 2)
            block = lambda ref, to: ref.at[to[0], to[1]]
            self.send_block(1, 1, sides, block, self.lines(len(sides)))
        elif number == 2 and self.ring:
            self.arrive(1, self.lines(2))
            came = lambda k, by: own[k].at[self.places[k][0], self.turn(k, 1, by)]
            self.pass_on(2, 1, came, self.lines(1))
        elif number == 3:
            if self.ring:
                self.arrive(2, self.lines(1))
            else:
                self.arrive(1, self.lines(3))
            self.send_block(3, 0, (1, -1), lambda ref, to: ref.at[to[0]], self.planes(2))
            for ref, to in zip(own, self.places):
                self.share(ref.at[to[0]])
        elif number == 4:
            self.arrive(3, self.planes(2))
            came = lambda k, by: own[k].at[self.turn(k, 0, by)]
            self.pass_on(4, 0, came, self.planes(1))
            for k in range(len(own)):
                for by in (1, -1):
                    self.share(came(k, by))
        elif number == 5:
            self.arrive(4, self.planes(1))
            for k in range(len(own)):
                self.share(own[k].at[self.turn(k, 0, 2)])
        elif number == 6:
            self.arrive(5, self.blocks.at[:, 0])

    def finish(self):
        self.departed()
        self.crossed()


class Reduce(Travel):
    def __init__(self, number, blocks, buffers, result, orders, at, sems, ring, credits, row_credits):
        super().__init__(number, blocks, orders, at, sems, ring)
        self.pair, self.half, self.full, self.row, self.cell = buffers
        self.result, self.traded = result, 0
        self.credits, self.row_credits = credits, row_credits

    def trade(self, k):
        if self.traded == 0 and self.credits is not None:
            self.credits()
        self.traded += 1
        for kind, by in ((0, 2), (1, 1), (1, -1), (1, 0)):
            plane = self.turn(k, 0, by)
            src, dst = self.gone[k].at[plane], self.pair.at[k, plane]
            remote(src, dst, self.send_sem(1), self.recv_sem(kind), self.twin()).start()

    def meet(self, k, by):
        plane = self.turn(k, 0, by)
        self.own[k][plane] = self.own[k][plane] + self.pair[k, plane]

    def start_ring(self, kind, level, opposite, halves, total):
        pieces = []
        for k in range(len(self.orders)):
            for side, by in ((0, 1), (1, -1)):
                piece = opposite(k).at[pl.ds(2 * side, 2)]
                pieces.append((piece, halves(k, side), self.neighbour(k, level, by)))
        self.depart(kind, pieces, total)

    def step(self, number):
        own, members = self.own, range(len(self.orders))
        if number == 0:
            for k in range(self.traded, len(self.orders)):
                self.trade(k)
        elif number == 1:
            self.arrive(0, self.planes(1))
            for k in members:
                self.meet(k, 2)
            opposite = lambda k: own[k].at[self.turn(k, 0, 2)]
            self.start_ring(2, 0, opposite, lambda k, side: self.half.at[k, side], self.planes(1))
        elif number == 2:
            self.arrive(1, self.planes(3))
            for k in members:
                for by in (1, -1, 0):
                    self.meet(k, by)
            self.arrive(2, self.planes(1))
            pieces = []
            for k in members:
                for side, by in ((0, 1), (1, -1)):
                    plane, rows = self.turn(k, 0, by), pl.ds(2 * side, 2)
                    own[k][plane, rows] = own[k][plane, rows] + self.half[k, side]
                    to = self.neighbour(k, 0, by)
                    pieces.append((own[k].at[plane], self.full.at[k, side], to))
            self.depart(3, pieces, self.planes(2))
        elif number == 3:
            self.arrive(3, self.planes(2))
            for k in members:
                c = self.places[k][0]
                total = own[k][c].astype(F32) + self.full[k, 0].astype(F32)
                own[k][c] = (total + self.full[k, 1].astype(F32)).astype(BF16)
            if self.row_credits is not None:
                self.row_credits()
            if self.ring:
                opposite = lambda k: own[k].at[self.places[k][0], self.turn(k, 1, 2)]
                halves = lambda k, side: self.row.at[k, 2, pl.ds(2 * side, 2)]
                self.start_ring(4, 1, opposite, halves, self.lines(1))
            else:
                pieces = []
                for k in members:
                    for side, by in enumerate((1, -1, 2)):
                        line = own[k].at[self.places[k][0], self.turn(k, 1, by)]
                        pieces.append((line, self.row.at[k, side], self.neighbour(k, 1, by)))
                self.depart(5, pieces, self.lines(3))
        elif number == 4 and self.ring:
            self.arrive(4, self.lines(1))
            pieces = []
            for k in members:
                c = self.places[k][0]
                for side, by in ((0, 1), (1, -1)):
                    line, cells = self.turn(k, 1, by), pl.ds(2 * side, 2)
                    own[k][c, line, cells] = own[k][c, line, cells] + self.row[k, 2, cells]
                    to = self.neighbour(k, 1, by)
                    pieces.append((own[k].at[c, line], self.row.at[k, side], to))
            self.depart(5, pieces, self.lines(2))
        elif number == 5:
            count = 2 if self.ring else 3
            self.arrive(5, self.lines(count))
            pieces = []
            for k in members:
                c, b, _ = self.places[k]
                total = own[k][c, b].astype(F32)
                for side in range(count):
                    total += self.row[k, side].astype(F32)
                own[k][c, b] = total.astype(BF16)
                for side, by in enumerate((1, -1, 2)):
                    cell = own[k].at[c, b, self.turn(k, 2, by)]
                    pieces.append((cell, self.cell.at[k, side], self.neighbour(k, 2, by)))
            self.depart(6, pieces, self.cells(3))
        elif number == 6:
            self.arrive(6, self.cells(3))
            for k in members:
                total = own[k][tuple(self.places[k])].astype(F32)
                for side in range(3):
                    total += self.cell[k, side].astype(F32)
                self.result(k, total)


def place(k, core, x, y, z):
    at = {"x": x, "y": y, "z": z}
    return (core,) + tuple(at[name] for name in AXES[k])


def read_tile(weights, part, k, inner, groups=GROUPS):
    y_lo, x_lo = inner // 2, inner % 2
    return jnp.concatenate(
        [
            jnp.concatenate(
                [
                    weights[(part, k) + place(k, core, 2 * x_hi + x_lo, 2 * y_hi + y_lo, z)]
                    for x_hi, z, y_hi in groups
                ],
                axis=0,
            )
            for core in range(2)
        ],
        axis=1,
    )


def write_tile(grads, part, k, inner, values):
    y_lo, x_lo = inner // 2, inner % 2
    low = values.astype(BF16)
    for at, (x_hi, z, y_hi) in enumerate(GROUPS):
        for core in range(2):
            grads[(part, k) + place(k, core, 2 * x_hi + x_lo, 2 * y_hi + y_lo, z)] = low[
                48 * at : 48 * at + 48, 128 * core : 128 * core + 128
            ]


def read_rows(weights, step, chunks=range(6)):
    x_hi, z = step // 4, step % 4
    return jnp.concatenate(
        [
            jnp.concatenate(
                [
                    weights[(2, chunk % 3) + place(chunk % 3, chunk // 3, 2 * x_hi + x_lo, y, z)]
                    for y in range(4)
                    for x_lo in range(2)
                ],
                axis=0,
            )
            for chunk in chunks
        ],
        axis=1,
    )


def write_rows(grads, step, values):
    x_hi, z = step // 4, step % 4
    low = values.astype(BF16)
    for y in range(4):
        for x_lo in range(2):
            at = 48 * (2 * y + x_lo)
            for core in range(2):
                for k in range(3):
                    column = 128 * (3 * core + k)
                    grads[(2, k) + place(k, core, 2 * x_hi + x_lo, y, z)] = low[
                        at : at + 48, column : column + 128
                    ]


def chunks_of(ref, first, count):
    return jnp.concatenate([ref[first + at] for at in range(count)], axis=1)


def by_rows(step):
    for first in range(0, 256, 64):
        step(pl.ds(first, 64))


def normalize(values):
    center = values - jnp.mean(values, axis=-1, keepdims=True)
    scale = lax.rsqrt(jnp.mean(center * center, axis=-1, keepdims=True) + EPS)
    return center * scale, scale


def normalize_back(grad, gain, normal, scale):
    grad_normal = grad * gain
    mean_one = jnp.mean(grad_normal, axis=-1, keepdims=True)
    mean_two = jnp.mean(grad_normal * normal, axis=-1, keepdims=True)
    return scale * (grad_normal - mean_one - normal * mean_two)


def half_masks():
    lane = lax.broadcasted_iota(jnp.int32, (1, 128), 1)
    first = jnp.where(lane < 64, 1.0, 0.0)
    return first.astype(BF16), (1.0 - first).astype(BF16)


class Kept:
    shapes = (
        ("proj", (18, 256, 128), BF16),
        ("soft", (12, 256, 256), BF16),
        ("mixed", (6, 256, 128), BF16),
        ("normal1", (256, 768), BF16),
        ("first_low", (256, 768), BF16),
        ("act", (24, 256, 128), BF16),
        ("slope", (24, 256, 128), BF16),
        ("normal2", (256, 768), F32),
        ("scales", (256, 2), F32),
    )

    def __init__(self, refs):
        for (name, _, _), ref in zip(self.shapes, refs):
            setattr(self, name, ref)


def forward_layer(state, norms, bias, shut, weights, kept, acc, need, tick):
    def enter(rows):
        values = state(rows)
        acc[rows, :] = values
        kept.first_low[rows, :] = values.astype(BF16)

    by_rows(enter)
    for k in range(3):
        need(0, k)
        for inner in range(TILES[k]):
            out = dot(kept.first_low[...], read_tile(weights, 0, k, inner)).astype(BF16)
            chunk = 8 * k + 2 * inner
            kept.proj[chunk] = out[:, :128]
            kept.proj[chunk + 1] = out[:, 128:]
        tick()

    low_half = lax.broadcasted_iota(jnp.int32, (256, 128), 1) < 64
    halves = half_masks()
    closed = jnp.concatenate([shut[...], shut[...]], axis=1)
    for pair in range(6):
        queries = kept.proj[pair] * jnp.asarray(0.125, BF16)
        keys = kept.proj[6 + pair]
        values = kept.proj[12 + pair]
        outs = []
        for side in range(2):
            scores = dot(keys, queries * halves[side], NT) + closed
            top = jnp.max(scores, axis=0, keepdims=True)
            exps = jnp.exp(scores - top)
            low = (exps * (1.0 / jnp.sum(exps, axis=0, keepdims=True))).astype(BF16)
            kept.soft[2 * pair + side] = low
            outs.append(dot(low, values, TN))
        kept.mixed[pair] = jnp.where(low_half, outs[0], outs[1]).astype(BF16)
        if pair % 3 == 2:
            tick()

    mixed_all = chunks_of(kept.mixed, 0, 6)
    for tile in range(3):
        columns = pl.ds(256 * tile, 256)
        acc[:, columns] += dot(mixed_all, read_tile(weights, 0, 2, 1 + tile))

    def first_norm(rows):
        normal, scale = normalize(acc[rows, :])
        kept.normal1[rows, :] = normal.astype(BF16)
        kept.scales[rows, 0:1] = scale
        first = normal * norms[0:1, :] + norms[1:2, :]
        acc[rows, :] = first
        kept.first_low[rows, :] = first.astype(BF16)

    by_rows(first_norm)
    tick()

    for k in range(3):
        need(1, k)
        for tile in range(4 * k, 4 * k + 4):
            columns = slice(256 * tile, 256 * tile + 256)
            pre = dot(kept.first_low[...], read_tile(weights, 1, k, tile % 4)) + bias[0:1, columns]
            cdf = 0.5 * (1.0 + lax.erf(pre * math.sqrt(0.5)))
            out = (pre * cdf).astype(BF16)
            bell = jnp.exp(-0.5 * pre * pre) * (1.0 / math.sqrt(2 * math.pi))
            grad = (cdf + pre * bell).astype(BF16)
            kept.act[2 * tile] = out[:, :128]
            kept.act[2 * tile + 1] = out[:, 128:]
            kept.slope[2 * tile] = grad[:, :128]
            kept.slope[2 * tile + 1] = grad[:, 128:]
        tick()
    for k in range(3):
        need(2, k)
    for side in range(2):
        for tile in range(3):
            columns = slice(256 * tile, 256 * tile + 256)
            pair = (2 * tile, 2 * tile + 1)
            rows = [read_rows(weights, 4 * side + step, pair) for step in range(4)]
            acc[:, columns] += dot(
                chunks_of(kept.act, 12 * side, 12), jnp.concatenate(rows, axis=0)
            )
        tick()

    def second_norm(rows):
        normal, scale = normalize(acc[rows, :])
        kept.normal2[rows, :] = normal
        kept.scales[rows, 1:2] = scale

    by_rows(second_norm)


def backward_layer(
    state, grad, norms, weights, kept, acc, low, turned, grad_norms, grad_bias, ready, tick
):
    def norm_back(which, normal_of, grad_of):
        sums = [jnp.zeros((1, 768), F32), jnp.zeros((1, 768), F32)]

        def step(rows):
            grad, normal = grad_of(rows), normal_of(rows)
            sums[0] += jnp.sum(grad * normal, axis=0, keepdims=True)
            sums[1] += jnp.sum(grad, axis=0, keepdims=True)
            scale = kept.scales[rows, which : which + 1]
            out = normalize_back(grad, norms[2 * which : 2 * which + 1, :], normal, scale)
            acc[rows, :] = out
            low[rows, :] = out.astype(BF16)

        by_rows(step)
        grad_norms[2 * which] = sums[0]
        grad_norms[2 * which + 1] = sums[1]

    norm_back(1, lambda rows: kept.normal2[rows, :], grad)
    for step in range(8):
        branch = low[...]
        grad_act = dot(branch, read_rows(weights, step), NT)
        pre_low = (grad_act * chunks_of(kept.slope, 3 * step, 3).astype(F32)).astype(BF16)
        for at in range(3):
            kept.slope[3 * step + at] = pre_low[:, 128 * at : 128 * at + 128]
        grad_bias[step] = jnp.sum(pre_low.astype(F32), axis=0, keepdims=True)
        write_rows(weights, step, dot(chunks_of(kept.act, 3 * step, 3), branch, TN))
        if step == 7:
            for k in range(3):
                ready(2, k)
        if step % 2:
            tick()
    turned[...] = kept.first_low[...].T
    for k in range(3):
        for inner in range(4):
            pre_low = chunks_of(kept.slope, 8 * k + 2 * inner, 2)
            acc[...] += dot(pre_low, read_tile(weights, 1, k, inner), NT)
            write_tile(weights, 1, k, inner, dot(turned[...], pre_low))
        ready(1, k)
        tick()

    norm_back(0, lambda rows: kept.normal1[rows, :].astype(F32), lambda rows: acc[rows, :])
    turned[...] = chunks_of(kept.mixed, 0, 6).T
    for side in range(2):
        groups = GROUPS[8 * side : 8 * side + 8]
        tiles = [read_tile(weights, 0, 2, 1 + tile, groups) for tile in range(3)]
        total = dot(low[...], jnp.concatenate(tiles, axis=1), NT)
        for chunk in range(3):
            columns = slice(128 * chunk, 128 * chunk + 128)
            kept.mixed[3 * side + chunk] = total[:, columns].astype(BF16)
    for tile in range(3):
        part_low = low[:, 256 * tile : 256 * tile + 256]
        write_tile(weights, 0, 2, 1 + tile, dot(turned[...], part_low))
    tick()

    low_half = lax.broadcasted_iota(jnp.int32, (256, 128), 1) < 64
    halves = half_masks()
    for pair in range(6):
        queries, keys, values = kept.proj[pair], kept.proj[6 + pair], kept.proj[12 + pair]
        back = kept.mixed[pair]
        scores, grads_k, grads_v = [], [], []
        for side in range(2):
            soft = kept.soft[2 * pair + side]
            weight = soft.astype(F32)
            grad_soft = dot(values, back * (halves[side] * jnp.asarray(0.125, BF16)), NT)
            inner = jnp.sum(weight * grad_soft, axis=0, keepdims=True)
            grad_score = (weight * (grad_soft - inner)).astype(BF16)
            scores.append(grad_score)
            grads_k.append(dot(grad_score, queries))
            grads_v.append(dot(soft, back))
        both_keys = jnp.concatenate([keys * halves[0], keys * halves[1]], axis=0)
        kept.proj[pair] = dot(jnp.concatenate(scores, axis=0), both_keys, TN).astype(BF16)
        for first, both in ((6, grads_k), (12, grads_v)):
            kept.proj[first + pair] = jnp.where(low_half, both[0], both[1]).astype(BF16)
        if pair % 3 == 2:
            tick()

    def turn(rows):
        turned[:, rows] = state(rows).astype(BF16).T

    for first in (0, 128):
        turn(pl.ds(first, 128))
    left = []
    for k in range(3):
        for inner in range(TILES[k]):
            pair = chunks_of(kept.proj, 8 * k + 2 * inner, 2)
            acc[...] += dot(pair, read_tile(weights, 0, k, inner), NT)
            write_tile(weights, 0, k, inner, dot(turned[...], pair))
        ready(0, k)
        tick()


def member_rows(extra, who):
    y_lo, x_lo, core = who // 4, who // 2 % 2, who % 2
    return jnp.concatenate(
        [
            extra[(k,) + place(k, core, 2 * x_hi + x_lo, 2 * y_hi + y_lo, z)]
            for x_hi, z, y_hi in GROUPS
            for k in range(2)
        ],
        axis=0,
    )


def write_member_rows(extra, who, values):
    y_lo, x_lo, core = who // 4, who // 2 % 2, who % 2
    for at, (x_hi, z, y_hi) in enumerate(GROUPS):
        for k in range(2):
            first = 32 * at + 16 * k
            into = (k,) + place(k, core, 2 * x_hi + x_lo, 2 * y_hi + y_lo, z)
            extra[into] = values[first : first + 16].astype(BF16)


def pick_rows(rows, columns, width):
    row = lax.broadcasted_iota(jnp.int32, (rows, columns), 0)
    column = lax.broadcasted_iota(jnp.int32, (rows, columns), 1)
    from_first = column - width * lax.shift_right_logical(row, 2)
    inside = jnp.logical_and(from_first >= 0, from_first < width)
    return jnp.where(inside, 1.0, 0.0).astype(BF16)


def pick_lanes(rows, columns, width):
    row = lax.broadcasted_iota(jnp.int32, (rows, columns), 0).astype(F32)
    column = lax.broadcasted_iota(jnp.int32, (rows, columns), 1).astype(F32)
    remainder = column - width * jnp.floor((column + 0.5) * (1.0 / width))
    return jnp.where(remainder == row, 1.0, 0.0)


def read_time_bias(extra):
    small = member_rows(extra, 7)
    pick, lanes = pick_rows(128, 128, 4), pick_lanes(8, 128, 4)
    return jnp.concatenate(
        [
            jnp.sum(dot(small[128 * at : 128 * at + 128], pick, TN)[:8] * lanes, axis=0, keepdims=True)
            for at in range(4)
        ],
        axis=1,
    )


def read_vectors(extra, norms, bias):
    small = member_rows(extra, 7)
    pick, lanes = pick_rows(256, 384, 6), pick_lanes(8, 384, 6)
    for at in range(2):
        spread = dot(small[256 * at : 256 * at + 256], pick, TN)
        for vector in range(8):
            value = jnp.sum(spread[8 + 8 * vector : 16 + 8 * vector] * lanes, axis=0, keepdims=True)
            norms[vector // 4, vector % 4 : vector % 4 + 1, 384 * at : 384 * at + 384] = value
    pick, lanes = pick_rows(64, 384, 24), pick_lanes(24, 384, 24)
    for at in range(8):
        spread = dot(small[64 * at : 64 * at + 64], pick, TN)
        for layer in range(2):
            value = spread[72 + 24 * layer : 96 + 24 * layer] * lanes
            bias[layer, :, 384 * at : 384 * at + 384] = jnp.sum(value, axis=0, keepdims=True)


def time_weights(extra):
    return jnp.concatenate([member_rows(extra, who) for who in range(6)], axis=1)


def time_forward(extra, emb, time_bias, time_pre, time_act, temb):
    by_chunk = dot(emb[...], member_rows(extra, 6))
    pre = jnp.concatenate([by_chunk[at : at + 1] for at in range(4)], axis=1) + time_bias
    act = (pre * lax.logistic(pre)).astype(BF16)
    time_pre[...] = pre
    time_act[...] = act.astype(F32)
    temb[...] = dot(jnp.broadcast_to(act, (8, 512)), time_weights(extra))[0:1]


def high_low(values):
    high = values.astype(BF16).astype(F32)
    return high, values - high


def time_backward(extra, emb, time_pre, time_act, grad, grad_norms, grad_bias):
    zero = lambda rows, columns: jnp.zeros((rows, columns), F32)
    total = jnp.sum(grad, axis=0, keepdims=True)
    both = jnp.concatenate(high_low(total) + (zero(6, 768),), axis=0).astype(BF16)
    grad_act = jnp.sum(dot(both, time_weights(extra), NT), axis=0, keepdims=True)
    pre = time_pre[...]
    gate = lax.logistic(pre)
    grad_pre = grad_act * gate * (1.0 + pre * (1.0 - gate))
    act = time_act[...]
    acts = jnp.concatenate([act, act, zero(6, 512)], axis=0).astype(BF16)
    for who in range(6):
        write_member_rows(extra, who, dot(acts, both[:, 128 * who : 128 * who + 128], TN))
    high, low = high_low(grad_pre)
    by_chunk = [side[:, 128 * at : 128 * at + 128] for side in (high, low) for at in range(4)]
    write_member_rows(extra, 6, dot(emb[...], jnp.concatenate(by_chunk, axis=0).astype(BF16), TN))

    pieces = []
    pick, lanes = pick_rows(64, 384, 24), pick_lanes(24, 384, 24)
    for at in range(8):
        rows = [zero(72, 384)] + [lanes * grad_bias[layer, at] for layer in range(2)] + [zero(8, 384)]
        pieces.append(dot(pick, jnp.concatenate(rows, axis=0).astype(BF16), NT))
    small = jnp.concatenate(pieces, axis=0)
    pick, lanes, pieces = pick_rows(256, 384, 6), pick_lanes(8, 384, 6), []
    for at in range(2):
        rows = [zero(8, 384)]
        for layer in range(2):
            for vector in range(4):
                rows.append(lanes * grad_norms[layer, vector, :, 384 * at : 384 * at + 384])
        rows.append(zero(56, 384))
        pieces.append(dot(pick, jnp.concatenate(rows, axis=0).astype(BF16), NT))
    small += jnp.concatenate(pieces, axis=0)
    pick, lanes, pieces = pick_rows(128, 128, 4), pick_lanes(8, 128, 4), []
    for at in range(4):
        rows = [lanes * grad_pre[:, 128 * at : 128 * at + 128], zero(120, 128)]
        pieces.append(dot(pick, jnp.concatenate(rows, axis=0).astype(BF16), NT))
    write_member_rows(extra, 7, small + jnp.concatenate(pieces, axis=0))


class Stop:
    def __init__(self, run):
        self.run, self.done, self.result = run, False, None

    def advance(self, until):
        if not self.done:
            self.result = self.run()
        self.done = True


class Clock:
    def __init__(self, plan):
        self.plan, self.now = plan, 0

    def tick(self):
        self.now += 1
        for travel, until in self.plan.get(self.now, ()):
            travel.advance(until)


def whole_kernel(*refs):
    refs = list(refs)
    take = lambda count: [refs.pop(0) for _ in range(count)]
    src_len, total_len = take(2)
    step_of, frequencies = take(2)
    qkv, out_w, ffn_in, ffn_out, time_in, time_out, time_bias, ffn_bias = take(8)
    norm_parts = take(4)
    tokens, cotangent = take(2)
    got_a, got_b, kept_b, output_part, grad_part = take(5)
    weights = take(2)
    kept = [Kept(take(len(Kept.shapes))) for _ in range(2)]
    acc, turned, shut, norms, bias, grad_norms, grad_bias = take(7)
    extra, emb, time_pre, time_act, temb = take(5)
    tokens_all, cotangent_all, leaving = take(3)
    send_a, send_b, rows, rows_b = take(4)
    pair, half, full = take(3)
    buffers_x = take(5)
    spread_sems, reduce_sems = take(2), take(2)
    first_sems, last_sems, move_sems = take(3)
    pair_free, ring_free, gone_free = take(3)

    at = here()
    mine, core = member(at), at["core"]
    my_stream = stream_of(at)
    partners = greet(at)

    def pack(layer):
        for to in range(8):
            for k in range(6):
                chunk = to + 8 * (k % 3)
                source, column = (qkv, chunk) if chunk < 18 else (out_w, chunk - 18)
                if k >= 3:
                    source, column = ffn_in, chunk
                piece = source[:, layer, 128 * column : 128 * column + 128]
                send_a[layer, to, k, 0:6, :] = piece.astype(F32)
        for k in range(3):
            column = pl.multiple_of(128 * (3 * (1 - core) + k), 128)
            send_b[layer, k] = ffn_out[layer, :, pl.ds(column, 128)].astype(F32)

    class Trade:
        def __init__(self, layer, sems, slots):
            self.sems = lambda kind: sems.at[layer, kind]
            self.all_a, self.all_b = got_a.at[layer, pl.ds(0, 7), pl.ds(0, slots)], got_b.at[layer]
            for flip in FLIPS:
                to = flipped(at, *flip)
                src = send_a.at[layer, member(to), pl.ds(0, slots)]
                dst = got_a.at[layer, mine, pl.ds(0, slots)]
                remote(src, dst, self.sems(0), self.sems(1), to).start()
            twin = flipped(at, 0, 0, 1)
            remote(send_b.at[layer], got_b.at[layer], self.sems(2), self.sems(3), twin).start()
            got_a[layer, mine] = send_a[layer, mine]

        def arrived(self):
            wait_bytes(self.all_a, self.sems(1))
            wait_bytes(self.all_b, self.sems(3))

        def left(self):
            wait_bytes(self.all_a, self.sems(0))
            wait_bytes(self.all_b, self.sems(2))

    class Move:
        def __init__(self, number, src, dst, split):
            self.sems = lambda kind: move_sems.at[number, kind]
            rows_of = lambda who: pl.ds(pl.multiple_of(64 * who, 64), 64)
            own_src = src.at[rows_of(my_stream)] if split else src.at[my_stream]
            own_dst = dst.at[my_stream] if split else dst.at[rows_of(my_stream)]
            self.keep = pltpu.make_async_copy(own_src, own_dst, self.sems(0))
            self.keep.start()
            for flip in range(1, 4):
                to = flipped(at, 0, flip // 2, flip % 2)
                there = src.at[rows_of(stream_of(to))] if split else src.at[stream_of(to)]
                remote(there, own_dst, self.sems(1), self.sems(2), to).start()

        def wait(self):
            self.keep.wait()
            for kind in (1, 2):
                wait_bytes(tokens_all.at[pl.ds(0, 192)], self.sems(kind))

    pack(0)
    for to in range(8):
        send_a[0, to, 6] = jnp.zeros((8, 128), F32)
        if to < 6:
            send_a[0, to, 6, 0:4, :] = time_out[:, 128 * to : 128 * to + 128].astype(F32)
        elif to == 6:
            for chunk in range(4):
                columns = slice(128 * chunk, 128 * chunk + 128)
                send_a[0, to, 6, chunk : chunk + 1, :] = time_in[:, columns].astype(F32)
        else:
            send_a[0, to, 6, 0:1, 0:4] = time_bias[...].astype(F32)
            for layer in range(2):
                for vector in range(4):
                    first_lane = 8 + 32 * layer + 8 * vector
                    values = norm_parts[vector][layer : layer + 1, :].astype(F32)
                    send_a[0, to, 6, 0:1, first_lane : first_lane + 6] = values
                first_lane = 72 + 24 * layer
                values = ffn_bias[layer : layer + 1, :].astype(F32)
                send_a[0, to, 6, 0:1, first_lane : first_lane + 24] = values
    pl.semaphore_wait(pltpu.get_barrier_semaphore(), partners)
    first = [Trade(0, first_sems, 7)]
    pack(1)
    first.append(Trade(1, first_sems, 6))
    bring_tokens = Move(0, tokens, tokens_all, False)

    mine_at = [tuple(at[name] for name in AXES[k]) for k in range(3)]

    def assemble_part(layer, part):
        for k in range(3):
            if part == 2:
                column = pl.multiple_of(128 * (3 * core + k), 128)
                rows_b[core] = ffn_out[layer, :, pl.ds(column, 128)].astype(F32)
                rows_b[1 - core] = got_b[layer, k]
                unit = rows_b[...].reshape(48, 128)
            else:
                for frm in range(8):
                    rows[6 * frm : 6 * frm + 6, :] = got_a[layer, frm, 3 * part + k, 0:6, :]
                unit = rows[...]
            weights[layer][(part, k, core) + mine_at[k]] = unit.astype(BF16)

    spread = {}
    for layer in range(2):
        for part in range(3):
            blocks = weights[layer].at[part]
            ring = layer + part > 0
            spread[layer, part] = Spread(3 * layer + part, blocks, AXES, at, spread_sems, ring)
    spread_x = Spread(6, extra, AXES[:2], at, spread_sems, False)

    def advance(*steps):
        for layer, part, until in steps:
            spread[layer, part].advance(until)

    angles = step_of[my_stream] * frequencies[...]
    column = lax.broadcasted_iota(jnp.int32, (1, 512), 1)
    features = jnp.where(column < 256, jnp.sin(angles), jnp.cos(angles))
    column = lax.broadcasted_iota(jnp.int32, (8, 512), 1)
    row = lax.broadcasted_iota(jnp.int32, (8, 512), 0)
    same = lax.bitwise_and(column, 3) == lax.bitwise_and(row, 3)
    emb[...] = jnp.where(same, jnp.broadcast_to(features, (8, 512)), 0.0).astype(BF16)

    first[0].arrived()
    assemble_part(0, 0)
    advance((0, 0, 1))
    for frm in range(8):
        rows[4 * frm : 4 * frm + 4, :] = got_a[0, frm, 6, 0:4, :]
    for k in range(2):
        extra[(k, core) + mine_at[k]] = rows[16 * k : 16 * k + 16, :].astype(BF16)
    spread_x.advance(1)
    for part in (1, 2):
        assemble_part(0, part)
        advance((0, part, 1))
    advance((0, 0, 2))
    spread_x.advance(2)
    advance((0, 1, 2), (0, 2, 2))
    first[1].arrived()
    for part in range(3):
        assemble_part(1, part)
        advance((1, part, 1))
    advance((0, 0, 4))
    spread_x.advance(4)
    advance((0, 1, 3), (0, 2, 3), (1, 0, 2), (1, 1, 2), (1, 2, 2), (0, 0, 5))
    spread_x.advance(5)
    advance((0, 1, 4), (0, 2, 4), (1, 0, 3), (1, 1, 3), (1, 2, 3), (0, 0, 6))
    spread_x.advance(7)
    time_forward(extra, emb, read_time_bias(extra), time_pre, time_act, temb)
    advance((0, 1, 5), (0, 0, 7))
    read_vectors(extra, norms, bias)
    lens = (src_len[my_stream], total_len[my_stream])
    key_at = lax.broadcasted_iota(jnp.int32, (256, 128), 0)
    bound = jnp.where(key_at < 128, lens[0], 128 + lens[1] - lens[0])
    shut[...] = jnp.where(key_at < bound, 0.0, -1e30)
    bring_tokens.wait()

    plan = {
        1: [(0, 2, 5), (1, 0, 4), (1, 1, 4)],
        4: [(0, 1, 6)],
        6: [(0, 1, 7), (0, 2, 6)],
        9: [(0, 2, 7)],
        10: [(1, 0, 5), (1, 2, 4)],
        11: [(1, 1, 5), (1, 0, 6)],
        14: [(1, 2, 5)],
        16: [(1, 1, 6)],
        18: [(1, 2, 6)],
    }
    for stops in plan.values():
        stops[:] = [(spread[layer, part], until) for layer, part, until in stops]
    bring_cotangent = Stop(lambda: Move(1, cotangent, cotangent_all, False))
    plan[14].append((bring_cotangent, 0))
    clock = Clock(plan)
    states = [
        lambda rows: tokens_all[rows, :].astype(F32) + temb[...],
        lambda rows: kept[0].normal2[rows, :] * norms[0, 2:3, :] + norms[0, 3:4, :],
    ]
    for layer in range(2):
        forward_layer(
            states[layer],
            norms.at[layer],
            bias.at[layer],
            shut,
            weights[layer],
            kept[layer],
            acc,
            lambda part, k: spread[layer, part].advance(7),
            clock.tick,
        )

    def leave(rows):
        final = kept[1].normal2[rows, :] * norms[1, 2:3, :] + norms[1, 3:4, :]
        leaving[rows, :] = final.astype(BF16)

    by_rows(leave)
    give_output = Move(2, leaving, output_part, True)
    for travel in list(spread.values()) + [spread_x]:
        travel.finish()
    for trade in first:
        trade.left()
    bring_cotangent.result.wait()

    there = pl.ds(pl.multiple_of(24 * (1 - core), 8), 24)
    near = pl.ds(pl.multiple_of(24 * core, 8), 24)

    def deliver(layer, part, k, total):
        rows[...] = total
        if part == 2:
            send_b[layer, k] = rows[there, :]
            kept_b[layer, k] = rows[near, :]
            return
        for to in range(8):
            send_a[layer, to, 3 * part + k, 0:6, :] = rows[6 * to : 6 * to + 6, :]

    def deliver_extra(k, total):
        rows[0:16, :] = total
        for to in range(4):
            send_a[0, 4 * k + to, 6, 0:4, :] = rows[4 * to : 4 * to + 4, :]

    around = [moved(at, axis, by) for axis in "xyz" for by in (1, -1, 2)]
    reduce = {}

    near_by = [moved(at, axis, by) for axis in "xyz" for by in (1, -1)]

    def gone(part):
        reduce[1, part].crossed()
        for to in around:
            signal(gone_free.at[part], to)

    def wait_gone(part):
        pl.semaphore_wait(gone_free.at[part], len(around))

    def free(part):
        reduce[1, part].advance(4)
        signal(pair_free.at[part], flipped(at, 0, 0, 1))
        for to in near_by:
            signal(ring_free.at[part], to)

    def freed(part):
        pl.semaphore_wait(pair_free.at[part], 1)
        pl.semaphore_wait(ring_free.at[part], len(near_by))

    for layer in range(2):
        for part in range(3):
            spare = weights[1].at[part, :, 1 - core, layer]
            small_buffers = [spare.at[:, pl.ds(0, 3)], spare.at[:, 3, pl.ds(0, 3)]]
            reduce[layer, part] = Reduce(
                3 * layer + part,
                weights[layer].at[part],
                [pair.at[part], half.at[part], full.at[part]] + small_buffers,
                partial(deliver, layer, part),
                AXES,
                at,
                reduce_sems,
                layer + part > 0,
                None if layer else partial(freed, part),
                partial(wait_gone, part) if layer else None,
            )
    reduce_x = Reduce(6, extra, buffers_x, deliver_extra, AXES[:2], at, reduce_sems, False, None, None)

    frees = [Stop(partial(free, part)) for part in range(3)]
    gones = [Stop(partial(gone, part)) for part in range(3)]
    second = lambda part, until: (reduce[1, part], until)
    early = lambda part, until: (reduce[0, part], until)
    plan = {
        6: [second(2, 2)],
        9: [second(1, 2), second(2, 3), (gones[2], 0)],
        13: [second(1, 3), (gones[1], 0)],
        15: [second(0, 2)],
        17: [(frees[2], 0)],
        19: [early(2, 1)],
        21: [early(2, 2), (frees[1], 0)],
        22: [early(1, 1), second(0, 3), (gones[0], 0), second(2, 5)],
        23: [early(1, 2), early(2, 3), second(1, 5)],
    }
    clock = Clock(plan)
    grads = [lambda rows: acc[rows, :], lambda rows: cotangent_all[rows, :].astype(F32)]
    for layer in (1, 0):
        backward_layer(
            states[layer],
            grads[layer],
            norms.at[layer],
            weights[layer],
            kept[layer],
            acc,
            cotangent_all,
            turned,
            grad_norms.at[layer],
            grad_bias.at[layer],
            lambda part, k: reduce[layer, part].trade(k) if layer else None,
            clock.tick,
        )

    give_output.wait()
    by_rows(lambda rows: leaving.__setitem__((rows, slice(None)), acc[rows, :].astype(BF16)))
    time_backward(extra, emb, time_pre, time_act, acc[...], grad_norms, grad_bias)
    give_grad = Stop(lambda: Move(3, leaving, grad_part, True))
    give_rows = [Stop(partial(Trade, layer, last_sems, 7 - layer)) for layer in range(2)]
    rest = [
        (frees[0], 0), second(2, 6), (reduce_x, 1), early(0, 1), (reduce_x, 2), early(1, 3), early(0, 2),
        early(2, 4), second(1, 6), second(0, 5), second(2, 7), (reduce_x, 3), early(1, 4), early(0, 3),
        early(2, 5), second(1, 7), second(0, 6), (reduce_x, 4), early(1, 5), (reduce_x, 5), early(0, 5),
        early(2, 6), second(0, 7), (give_rows[1], 0), (reduce_x, 6), early(1, 6), early(0, 6), (give_grad, 0),
        early(2, 7), (reduce_x, 7), early(1, 7), early(0, 7), (give_rows[0], 0),
    ]
    for travel, until in rest:
        travel.advance(until)
    for (layer, part), travel in reduce.items():
        travel.departed()
        if layer == 0:
            travel.crossed()
    reduce_x.departed()
    reduce_x.crossed()
    for give in give_rows:
        give.result.arrived()
        give.result.left()
    give_grad.result.wait()


def whole(*operands):
    vmem, anywhere = pl.BlockSpec(memory_space=pltpu.VMEM), pl.BlockSpec(memory_space=pl.ANY)
    smem = pl.BlockSpec(memory_space=pltpu.SMEM)
    dma, regular = pltpu.SemaphoreType.DMA, pltpu.SemaphoreType.REGULAR
    buffers = lambda lead, unit: [
        pltpu.VMEM(lead + shape + unit, BF16)
        for shape in ((4, 4, 4), (2, 2, 4), (2, 4, 4), (3, 4), (3,))
    ]
    scratch = [pltpu.VMEM((3, 3, 2, 4, 4, 4) + UNIT, BF16) for _ in range(2)]
    for _ in range(2):
        scratch += [pltpu.VMEM(shape, kind) for _, shape, kind in Kept.shapes]
    scratch += [
        pltpu.VMEM((256, 768), F32),
        pltpu.VMEM((768, 256), BF16),
        pltpu.VMEM((256, 128), F32),
        pltpu.VMEM((2, 8, 768), F32),
        pltpu.VMEM((2, 1, 3072), F32),
        pltpu.VMEM((2, 4, 1, 768), F32),
        pltpu.VMEM((2, 8, 1, 384), F32),
        pltpu.VMEM((2, 2, 4, 4, 4) + EXTRA, BF16),
        pltpu.VMEM((8, 512), BF16),
        pltpu.VMEM((1, 512), F32),
        pltpu.VMEM((1, 512), F32),
        pltpu.VMEM((1, 768), F32),
        pltpu.VMEM((256, 768), BF16),
        pltpu.VMEM((256, 768), BF16),
        pltpu.VMEM((256, 768), BF16),
        pltpu.VMEM((2, 8, 7, 8, 128), F32),
        pltpu.VMEM((2, 3, 24, 128), F32),
        pltpu.VMEM((48, 128), F32),
        pltpu.VMEM((2, 24, 128), F32),
    ]
    scratch += buffers((3, 3), UNIT)[:3] + buffers((2,), EXTRA)
    scratch += [
        dma((7, SPREAD_SEMS)),
        dma((7, 2)),
        dma((7, REDUCE_SEMS)),
        dma((7, 2)),
        dma((2, 4)),
        dma((2, 4)),
        dma((4, 3)),
        regular((3,)),
        regular((3,)),
        regular((3,)),
    ]
    return pl.pallas_call(
        whole_kernel,
        out_shape=[
            jax.ShapeDtypeStruct((2, 8, 7, 8, 128), F32),
            jax.ShapeDtypeStruct((2, 3, 24, 128), F32),
            jax.ShapeDtypeStruct((2, 3, 24, 128), F32),
            jax.ShapeDtypeStruct((4, 64, 768), BF16),
            jax.ShapeDtypeStruct((4, 64, 768), BF16),
        ],
        in_specs=[smem] * 3 + [vmem] * 13 + [anywhere] * 2,
        out_specs=[vmem] * 3 + [anywhere] * 2,
        scratch_shapes=scratch,
        compiler_params=pltpu.CompilerParams(
            collective_id=1, has_side_effects=True, vmem_limit_bytes=VMEM_BYTES
        ),
        name="whole",
    )(*operands)


def finish_kernel(got_a, got_b, kept_b, output, grad, *results):
    out, grad_x, g_tin, g_bias, g_tout, g_qkv, g_out = results[:7]
    norm1_gain, norm1_bias, g_in, g_ffn_bias, g_ffn, norm2_gain, norm2_bias = results[7:]
    core = lax.rem(lax.axis_index("stream"), 2)
    out[...] = output[...]
    grad_x[...] = grad[...].astype(F32)
    for frm in range(8):
        for layer in range(2):
            for k in range(6):
                chunk = frm + 8 * (k % 3)
                into, column = (g_qkv, chunk) if chunk < 18 else (g_out, chunk - 18)
                if k >= 3:
                    into, column = g_in, chunk
                into[:, layer, 128 * column : 128 * column + 128] = got_a[layer, frm, k, 0:6, :]
        if frm < 6:
            g_tout[:, 128 * frm : 128 * frm + 128] = got_a[0, frm, 6, 0:4, :]
        elif frm == 6:
            for chunk in range(4):
                g_tin[:, 128 * chunk : 128 * chunk + 128] = got_a[0, frm, 6, chunk : chunk + 1, :]
        else:
            g_bias[...] = got_a[0, frm, 6, 0:1, 0:4]
            vectors = (norm1_gain, norm1_bias, norm2_gain, norm2_bias)
            for layer in range(2):
                here_at = slice(layer, layer + 1)
                for at, vector in enumerate(vectors):
                    lane = 8 + 32 * layer + 8 * at
                    vector[here_at, :] = got_a[0, frm, 6, 0:1, lane : lane + 6]
                lane = 72 + 24 * layer
                g_ffn_bias[here_at, :] = got_a[0, frm, 6, 0:1, lane : lane + 24]
    for layer in range(2):
        for k in range(3):
            near = pl.ds(pl.multiple_of(128 * (3 * core + k), 128), 128)
            there = pl.ds(pl.multiple_of(128 * (3 * (1 - core) + k), 128), 128)
            g_ffn[layer, :, near] = kept_b[layer, k]
            g_ffn[layer, :, there] = got_b[layer, k]


def finish(got_a, got_b, kept_b, output, grad):
    shapes = [
        (4, 64, 768),
        (4, 64, 768),
        (1, 512),
        (1, 4),
        (4, 768),
        (6, 2, 2304),
        (6, 2, 768),
        (2, 6),
        (2, 6),
        (6, 2, 3072),
        (2, 24),
        (2, 24, 768),
        (2, 6),
        (2, 6),
    ]
    vmem = pl.BlockSpec(memory_space=pltpu.VMEM)
    return pl.pallas_call(
        finish_kernel,
        out_shape=[
            jax.ShapeDtypeStruct(shape, F32 if at else BF16) for at, shape in enumerate(shapes)
        ],
        in_specs=[vmem] * 5,
        out_specs=[vmem] * len(shapes),
        compiler_params=pltpu.CompilerParams(vmem_limit_bytes=VMEM_BYTES),
        name="lay_out_results",
    )(got_a, got_b, kept_b, output, grad)


def per_device(
    tokens,
    timestep,
    src_len,
    total_len,
    time_in,
    time_bias,
    time_out,
    qkv_weight,
    out_weight,
    norm1_gain,
    norm1_bias,
    ffn_in,
    ffn_bias,
    ffn_out,
    norm2_gain,
    norm2_bias,
    cotangent,
):
    frequencies = np.exp(-math.log(10000.0) * np.arange(64) / 64)
    by_layer = lambda weight: weight.transpose(1, 0, 2)
    got = whole(
        src_len,
        total_len,
        timestep,
        jnp.asarray(np.repeat(np.tile(frequencies, 2), 4)[None, :], F32),
        by_layer(qkv_weight),
        by_layer(out_weight),
        by_layer(ffn_in),
        ffn_out,
        time_in,
        time_out,
        time_bias[None, :],
        ffn_bias,
        norm1_gain,
        norm1_bias,
        norm2_gain,
        norm2_bias,
        tokens,
        cotangent,
    )
    results = list(finish(*got))
    results[3] = results[3][0]
    for at in (5, 6, 9):
        results[at] = by_layer(results[at])
    return tuple(results)


def solution(mesh):
    in_specs = (
        P("batch", "stream", None),
        P("batch"),
        P("batch"),
        P("batch"),
        P(("batch", "stream"), None),
        P(("batch", "stream")),
        P(("batch", "stream"), None),
        P(None, ("batch", "stream"), None),
        P(None, ("batch", "stream"), None),
        P(None, ("batch", "stream")),
        P(None, ("batch", "stream")),
        P(None, ("batch", "stream"), None),
        P(None, ("batch", "stream")),
        P(None, ("batch", "stream"), None),
        P(None, ("batch", "stream")),
        P(None, ("batch", "stream")),
        P("batch", "stream", None),
    )
    out_specs = (
        P("batch", "stream", None),
        P("batch", "stream", None),
        P(("batch", "stream"), None),
        P(("batch", "stream")),
        P(("batch", "stream"), None),
        P(None, ("batch", "stream"), None),
        P(None, ("batch", "stream"), None),
        P(None, ("batch", "stream")),
        P(None, ("batch", "stream")),
        P(None, ("batch", "stream"), None),
        P(None, ("batch", "stream")),
        P(None, ("batch", "stream"), None),
        P(None, ("batch", "stream")),
        P(None, ("batch", "stream")),
    )
    return jax.shard_map(
        per_device, mesh=mesh, in_specs=in_specs, out_specs=out_specs, check_vma=False
    )
```

```python
from functools import partial
import math

import jax
import jax.numpy as jnp
import numpy as np
from jax import lax
from jax.experimental import pallas as pl
from jax.experimental.pallas import tpu as pltpu
from jax.sharding import PartitionSpec as P

F32, BF16 = jnp.float32, jnp.bfloat16
EPS = 1e-05
NN = (((1,), (0,)), ((), ()))
NT = (((1,), (1,)), ((), ()))
TN = (((0,), (0,)), ((), ()))
MESH = pl.DeviceIdType.MESH
VMEM_BYTES = 65400 * 1024
AXES = ("zyx", "xzy", "yxz")
UNIT = (48, 128)
EXTRA = (16, 128)
GROUPS = [(x_hi, z, y_hi) for x_hi in range(2) for z in range(4) for y_hi in range(2)]
FLIPS = [(flip // 4, flip // 2 % 2, flip % 2) for flip in range(1, 8)]
TILES = (4, 4, 1)
SPREAD_SEMS, REDUCE_SEMS = 6, 7


def dot(left, right, dims=NN):
    return lax.dot_general(left, right, dims, preferred_element_type=F32)


def here():
    batch, stream = lax.axis_index("batch"), lax.axis_index("stream")
    return {
        "x": 2 * lax.div(batch, 16) + lax.div(stream, 2),
        "y": lax.rem(batch, 4),
        "z": lax.rem(lax.div(batch, 4), 4),
        "core": lax.rem(stream, 2),
    }


def device(at):
    return (
        lax.div(at["x"], 2) * 16 + at["z"] * 4 + at["y"],
        lax.rem(at["x"], 2) * 2 + at["core"],
    )


def moved(at, axis, by):
    return {**at, axis: lax.rem(at[axis] + by + 4, 4)}


def flipped(at, flip_y, flip_x, flip_core):
    new = dict(at)
    if flip_y:
        new["y"] = at["y"] + 1 - 2 * lax.rem(at["y"], 2)
    if flip_x:
        new["x"] = at["x"] + 1 - 2 * lax.rem(at["x"], 2)
    if flip_core:
        new["core"] = 1 - at["core"]
    return new


def member(at):
    return lax.rem(at["y"], 2) * 4 + lax.rem(at["x"], 2) * 2 + at["core"]


def stream_of(at):
    return lax.rem(at["x"], 2) * 2 + at["core"]


def signal(sem, to):
    pl.semaphore_signal(sem, inc=1, device_id=device(to), device_id_type=MESH)


def greet(at):
    partners = [flipped(at, *flip) for flip in FLIPS]
    partners += [moved(at, "z", 1), moved(at, "z", -1)]
    partners += [moved(at, axis, 2 * lax.rem(at[axis], 2) - 1) for axis in "xy"]
    partners += [moved(at, axis, 2) for axis in "xyz"]
    barrier = pltpu.get_barrier_semaphore()
    for partner in partners:
        signal(barrier, partner)
    return len(partners)


def remote(src, dst, send_sem, recv_sem, to):
    return pltpu.make_async_remote_copy(
        src_ref=src,
        dst_ref=dst,
        send_sem=send_sem,
        recv_sem=recv_sem,
        device_id=device(to),
        device_id_type=MESH,
    )


def wait_bytes(ref, sem):
    pltpu.make_async_copy(ref, ref, sem).wait()


def pick(k, options):
    if isinstance(k, int):
        return options[k]
    first, second, third = options
    return (
        lax.div((1 - k) * (2 - k), 2) * first + k * (2 - k) * second + lax.div(k * (k - 1), 2) * third
    )


class Travel:
    def __init__(self, number, blocks, at, sems, ring):
        self.at, self.ring, self.blocks = at, ring, blocks
        self.units = blocks.shape[0]
        self.recv_sem = lambda kind: sems[0].at[number, kind]
        self.send_sem = lambda kind: sems[1].at[number, kind]
        self.done = 0

    def own(self, k):
        return self.blocks.at[k, self.at["core"]]

    def gone(self, k):
        return self.blocks.at[k, 1 - self.at["core"]]

    def cells(self, count):
        return self.blocks.at[:, 0, 0, 0, pl.ds(0, count)]

    def lines(self, count):
        return self.blocks.at[:, 0, 0, pl.ds(0, count)]

    def planes(self, count):
        return self.blocks.at[:, 0, pl.ds(0, count)]

    def turn(self, k, level, by=0):
        place = pick(k, [self.at[order[level]] for order in AXES])
        return lax.rem(place + by + 4, 4) if by else place

    def neighbour(self, k, level, by):
        new = self.turn(k, level, by)
        to = dict(self.at)
        for axis in "xyz":
            here_it_is = pick(k, [int(order[level] == axis) for order in AXES])
            to[axis] = self.at[axis] + here_it_is * (new - self.at[axis])
        return to

    def twin(self):
        return flipped(self.at, 0, 0, 1)

    def each(self, body):
        def step(k, carry):
            body(k)
            return carry

        lax.fori_loop(0, self.units, step, 0)

    def arrive(self, kind, total):
        wait_bytes(total, self.recv_sem(kind))

    def depart(self, kind, pieces, before):
        if before is not None:
            self.departed(before)

        def start(k):
            for src, dst, to in pieces(k):
                remote(src, dst, self.send_sem(0), self.recv_sem(kind), to).start()

        self.each(start)

    def departed(self, total):
        wait_bytes(total, self.send_sem(0))

    def crossed(self):
        wait_bytes(self.blocks.at[:, 0], self.send_sem(1))

    def steps(self, until):
        first, self.done = self.done, max(self.done, until)
        return [partial(self.step, number) for number in range(first, until)]

    def advance(self, until):
        for step in self.steps(until):
            step()


class Spread(Travel):
    def share(self, ref):
        remote(ref, ref, self.send_sem(1), self.recv_sem(5), self.twin()).start()

    def pass_on(self, kind, level, came, before):
        def pieces(k):
            for side, by in ((0, -1), (1, 1)):
                piece = came(k, by).at[pl.ds(2 * side, 2)]
                yield piece, piece, self.neighbour(k, level, -by)

        self.depart(kind, pieces, before)

    def send_block(self, kind, level, sides, block, before):
        def pieces(k):
            mine = block(k)
            return [(mine, mine, self.neighbour(k, level, by)) for by in sides]

        self.depart(kind, pieces, before)

    def step(self, number):
        own, turn = self.own, self.turn
        plane = lambda k, by=0: own(k).at[turn(k, 0, by)]
        line = lambda k, by=0: own(k).at[turn(k, 0), turn(k, 1, by)]
        cell = lambda k: own(k).at[turn(k, 0), turn(k, 1), turn(k, 2)]
        if number == 0:
            self.send_block(0, 2, (1, -1, 2), cell, None)
        elif number == 1:
            self.arrive(0, self.cells(3))
            sides = (1, -1) if self.ring else (1, -1, 2)
            self.send_block(1, 1, sides, line, self.cells(3))
        elif number == 2 and self.ring:
            self.arrive(1, self.lines(2))
            self.pass_on(2, 1, line, self.lines(2))
        elif number == 3:
            if self.ring:
                self.arrive(2, self.lines(1))
            else:
                self.arrive(1, self.lines(3))
            self.send_block(3, 0, (1, -1), plane, self.lines(1 if self.ring else 3))
            self.each(lambda k: self.share(plane(k)))
        elif number == 4:
            self.arrive(3, self.planes(2))
            self.pass_on(4, 0, plane, self.planes(2))

            def share(k):
                for by in (1, -1):
                    self.share(plane(k, by))

            self.each(share)
        elif number == 5:
            self.arrive(4, self.planes(1))
            self.each(lambda k: self.share(plane(k, 2)))
        elif number == 6:
            self.arrive(5, self.blocks.at[:, 0])

    def finish(self):
        self.departed(self.planes(1))
        self.crossed()


class Reduce(Travel):
    def __init__(self, number, blocks, buffers, result, at, sems, ring, credits, row_credits):
        super().__init__(number, blocks, at, sems, ring)
        self.pair, self.half, self.full, self.row, self.cell = buffers
        self.result, self.traded = result, 0
        self.credits, self.row_credits = credits, row_credits

    def trade(self, k):
        for kind, by in ((0, 2), (1, 1), (1, -1), (1, 0)):
            plane = self.turn(k, 0, by)
            src, dst = self.gone(k).at[plane], self.pair.at[k, plane]
            remote(src, dst, self.send_sem(1), self.recv_sem(kind), self.twin()).start()

    def meet(self, k, by):
        plane, own = self.turn(k, 0, by), self.own(k)
        own[plane] = own[plane] + self.pair[k, plane]

    def start_ring(self, kind, level, opposite, halves, before):
        def pieces(k):
            for side, by in ((0, 1), (1, -1)):
                piece = opposite(k).at[pl.ds(2 * side, 2)]
                yield piece, halves(k, side), self.neighbour(k, level, by)

        self.depart(kind, pieces, before)

    def step(self, number):
        own, turn = self.own, self.turn
        if number == 0:
            if self.credits is not None:
                self.credits()
            self.each(self.trade)
        elif number == 1:
            self.arrive(0, self.planes(1))
            self.each(lambda k: self.meet(k, 2))
            opposite = lambda k: own(k).at[turn(k, 0, 2)]
            self.start_ring(2, 0, opposite, lambda k, side: self.half.at[k, side], None)
        elif number == 2:
            self.arrive(1, self.planes(3))

            def meet(k):
                for by in (1, -1, 0):
                    self.meet(k, by)

            self.each(meet)
            self.arrive(2, self.planes(1))

            def pieces(k):
                ref = own(k)
                for side, by in ((0, 1), (1, -1)):
                    plane, rows = turn(k, 0, by), pl.ds(2 * side, 2)
                    ref[plane, rows] = ref[plane, rows] + self.half[k, side]
                    yield ref.at[plane], self.full.at[k, side], self.neighbour(k, 0, by)

            self.depart(3, pieces, self.planes(1))
        elif number == 3:
            self.arrive(3, self.planes(2))

            def settle(k):
                c, ref = turn(k, 0), own(k)
                total = ref[c].astype(F32) + self.full[k, 0].astype(F32)
                ref[c] = (total + self.full[k, 1].astype(F32)).astype(BF16)

            self.each(settle)
            if self.row_credits is not None:
                self.row_credits()
            if self.ring:
                opposite = lambda k: own(k).at[turn(k, 0), turn(k, 1, 2)]
                halves = lambda k, side: self.row.at[k, 2, pl.ds(2 * side, 2)]
                self.start_ring(4, 1, opposite, halves, self.planes(2))
            else:

                def pieces(k):
                    for side, by in enumerate((1, -1, 2)):
                        line = own(k).at[turn(k, 0), turn(k, 1, by)]
                        yield line, self.row.at[k, side], self.neighbour(k, 1, by)

                self.depart(5, pieces, self.planes(2))
        elif number == 4 and self.ring:
            self.arrive(4, self.lines(1))

            def pieces(k):
                c, ref = turn(k, 0), own(k)
                for side, by in ((0, 1), (1, -1)):
                    line, cells = turn(k, 1, by), pl.ds(2 * side, 2)
                    ref[c, line, cells] = ref[c, line, cells] + self.row[k, 2, cells]
                    yield ref.at[c, line], self.row.at[k, side], self.neighbour(k, 1, by)

            self.depart(5, pieces, self.lines(1))
        elif number == 5:
            count = 2 if self.ring else 3
            self.arrive(5, self.lines(count))

            def pieces(k):
                c, b, ref = turn(k, 0), turn(k, 1), own(k)
                total = ref[c, b].astype(F32)
                for side in range(count):
                    total += self.row[k, side].astype(F32)
                ref[c, b] = total.astype(BF16)
                for side, by in enumerate((1, -1, 2)):
                    yield ref.at[c, b, turn(k, 2, by)], self.cell.at[k, side], self.neighbour(k, 2, by)

            self.depart(6, pieces, self.lines(count))
        elif number == 6:
            self.arrive(6, self.cells(3))

            def settle(k):
                total = own(k)[turn(k, 0), turn(k, 1), turn(k, 2)].astype(F32)
                for side in range(3):
                    total += self.cell[k, side].astype(F32)
                self.result(k, total)

            self.each(settle)

    def finish(self):
        self.departed(self.cells(3))


def place(k, core, x, y, z):
    at = {"x": x, "y": y, "z": z}
    return (core,) + tuple(at[name] for name in AXES[k])


def read_tile(weights, part, k, inner, groups=GROUPS):
    y_lo, x_lo = inner // 2, inner % 2
    return jnp.concatenate(
        [
            jnp.concatenate(
                [
                    weights[(part, k) + place(k, core, 2 * x_hi + x_lo, 2 * y_hi + y_lo, z)]
                    for x_hi, z, y_hi in groups
                ],
                axis=0,
            )
            for core in range(2)
        ],
        axis=1,
    )


def write_tile(grads, part, k, inner, values):
    y_lo, x_lo = inner // 2, inner % 2
    low = values.astype(BF16)
    for at, (x_hi, z, y_hi) in enumerate(GROUPS):
        for core in range(2):
            grads[(part, k) + place(k, core, 2 * x_hi + x_lo, 2 * y_hi + y_lo, z)] = low[
                48 * at : 48 * at + 48, 128 * core : 128 * core + 128
            ]


def read_rows(weights, step, chunks=range(6)):
    x_hi, z = step // 4, step % 4
    return jnp.concatenate(
        [
            jnp.concatenate(
                [
                    weights[(2, chunk % 3) + place(chunk % 3, chunk // 3, 2 * x_hi + x_lo, y, z)]
                    for y in range(4)
                    for x_lo in range(2)
                ],
                axis=0,
            )
            for chunk in chunks
        ],
        axis=1,
    )


def write_rows(grads, step, values):
    x_hi, z = step // 4, step % 4
    low = values.astype(BF16)
    for y in range(4):
        for x_lo in range(2):
            at = 48 * (2 * y + x_lo)
            for core in range(2):
                for k in range(3):
                    column = 128 * (3 * core + k)
                    grads[(2, k) + place(k, core, 2 * x_hi + x_lo, y, z)] = low[
                        at : at + 48, column : column + 128
                    ]


def chunks_of(ref, first, count):
    return jnp.concatenate([ref[first + at] for at in range(count)], axis=1)


def by_rows(step):
    for first in range(0, 256, 64):
        step(pl.ds(first, 64))


def normalize(values):
    center = values - jnp.mean(values, axis=-1, keepdims=True)
    scale = lax.rsqrt(jnp.mean(center * center, axis=-1, keepdims=True) + EPS)
    return center * scale, scale


def normalize_back(grad, gain, normal, scale):
    grad_normal = grad * gain
    mean_one = jnp.mean(grad_normal, axis=-1, keepdims=True)
    mean_two = jnp.mean(grad_normal * normal, axis=-1, keepdims=True)
    return scale * (grad_normal - mean_one - normal * mean_two)


def half_masks():
    lane = lax.broadcasted_iota(jnp.int32, (1, 128), 1)
    first = jnp.where(lane < 64, 1.0, 0.0)
    return first.astype(BF16), (1.0 - first).astype(BF16)


class Kept:
    shapes = (
        ("proj", (18, 256, 128), BF16),
        ("soft", (12, 256, 256), BF16),
        ("mixed", (6, 256, 128), BF16),
        ("normal1", (256, 768), BF16),
        ("first_low", (256, 768), BF16),
        ("act", (24, 256, 128), BF16),
        ("slope", (24, 256, 128), BF16),
        ("normal2", (256, 768), F32),
        ("scales", (256, 2), F32),
    )

    def __init__(self, refs, layer):
        for (name, _, _), ref in zip(self.shapes, refs):
            setattr(self, name, ref.at[layer])


def forward_layer(enter_state, norms, bias, shut, weights, kept, acc, tick):
    def enter(state, rows):
        values = state(rows)
        acc[rows, :] = values
        kept.first_low[rows, :] = values.astype(BF16)

    enter_state(lambda state: by_rows(partial(enter, state)))
    tick("qkv")
    for k in range(3):
        for inner in range(TILES[k]):
            out = dot(kept.first_low[...], read_tile(weights, 0, k, inner)).astype(BF16)
            chunk = 8 * k + 2 * inner
            kept.proj[chunk] = out[:, :128]
            kept.proj[chunk + 1] = out[:, 128:]
        tick(1 + k)

    low_half = lax.broadcasted_iota(jnp.int32, (256, 128), 1) < 64
    halves = half_masks()
    closed = jnp.concatenate([shut[...], shut[...]], axis=1)
    for pair in range(6):
        queries = kept.proj[pair] * jnp.asarray(0.125, BF16)
        keys = kept.proj[6 + pair]
        values = kept.proj[12 + pair]
        outs = []
        for side in range(2):
            scores = dot(keys, queries * halves[side], NT) + closed
            top = jnp.max(scores, axis=0, keepdims=True)
            exps = jnp.exp(scores - top)
            low = (exps * (1.0 / jnp.sum(exps, axis=0, keepdims=True))).astype(BF16)
            kept.soft[2 * pair + side] = low
            outs.append(dot(low, values, TN))
        kept.mixed[pair] = jnp.where(low_half, outs[0], outs[1]).astype(BF16)
        if pair % 3 == 2:
            tick(4 + pair // 3)

    mixed_all = chunks_of(kept.mixed, 0, 6)
    for tile in range(3):
        columns = pl.ds(256 * tile, 256)
        acc[:, columns] += dot(mixed_all, read_tile(weights, 0, 2, 1 + tile))

    def first_norm(rows):
        normal, scale = normalize(acc[rows, :])
        kept.normal1[rows, :] = normal.astype(BF16)
        kept.scales[rows, 0:1] = scale
        first = normal * norms[0:1, :] + norms[1:2, :]
        acc[rows, :] = first
        kept.first_low[rows, :] = first.astype(BF16)

    by_rows(first_norm)
    tick(6)
    tick("feed")

    for k in range(3):
        for tile in range(4 * k, 4 * k + 4):
            columns = slice(256 * tile, 256 * tile + 256)
            pre = dot(kept.first_low[...], read_tile(weights, 1, k, tile % 4)) + bias[0:1, columns]
            cdf = 0.5 * (1.0 + lax.erf(pre * math.sqrt(0.5)))
            out = (pre * cdf).astype(BF16)
            bell = jnp.exp(-0.5 * pre * pre) * (1.0 / math.sqrt(2 * math.pi))
            grad = (cdf + pre * bell).astype(BF16)
            kept.act[2 * tile] = out[:, :128]
            kept.act[2 * tile + 1] = out[:, 128:]
            kept.slope[2 * tile] = grad[:, :128]
            kept.slope[2 * tile + 1] = grad[:, 128:]
        tick(7 + k)
    tick("unfeed")
    for side in range(2):
        for tile in range(3):
            columns = slice(256 * tile, 256 * tile + 256)
            pair = (2 * tile, 2 * tile + 1)
            rows = [read_rows(weights, 4 * side + step, pair) for step in range(4)]
            acc[:, columns] += dot(
                chunks_of(kept.act, 12 * side, 12), jnp.concatenate(rows, axis=0)
            )
        tick(10 + side)

    def second_norm(rows):
        normal, scale = normalize(acc[rows, :])
        kept.normal2[rows, :] = normal
        kept.scales[rows, 1:2] = scale

    by_rows(second_norm)


def backward_layer(
    turn_state, norms, weights, kept, acc, low, turned, grad_norms, grad_bias, tick
):
    def norm_back(which, normal_of, grad_of):
        sums = [jnp.zeros((1, 768), F32), jnp.zeros((1, 768), F32)]

        def step(rows):
            grad, normal = grad_of(rows), normal_of(rows)
            sums[0] += jnp.sum(grad * normal, axis=0, keepdims=True)
            sums[1] += jnp.sum(grad, axis=0, keepdims=True)
            scale = kept.scales[rows, which : which + 1]
            out = normalize_back(grad, norms[2 * which : 2 * which + 1, :], normal, scale)
            acc[rows, :] = out
            low[rows, :] = out.astype(BF16)

        by_rows(step)
        grad_norms[2 * which] = sums[0]
        grad_norms[2 * which + 1] = sums[1]

    norm_back(1, lambda rows: kept.normal2[rows, :], lambda rows: acc[rows, :])
    for step in range(8):
        branch = low[...]
        grad_act = dot(branch, read_rows(weights, step), NT)
        pre_low = (grad_act * chunks_of(kept.slope, 3 * step, 3).astype(F32)).astype(BF16)
        for at in range(3):
            kept.slope[3 * step + at] = pre_low[:, 128 * at : 128 * at + 128]
        grad_bias[step] = jnp.sum(pre_low.astype(F32), axis=0, keepdims=True)
        write_rows(weights, step, dot(chunks_of(kept.act, 3 * step, 3), branch, TN))
        if step % 2:
            tick(1 + step // 2)
    turned[...] = kept.first_low[...].T
    for k in range(3):
        for inner in range(4):
            pre_low = chunks_of(kept.slope, 8 * k + 2 * inner, 2)
            acc[...] += dot(pre_low, read_tile(weights, 1, k, inner), NT)
            write_tile(weights, 1, k, inner, dot(turned[...], pre_low))
        tick(5 + k)

    norm_back(0, lambda rows: kept.normal1[rows, :].astype(F32), lambda rows: acc[rows, :])
    turned[...] = chunks_of(kept.mixed, 0, 6).T
    for side in range(2):
        groups = GROUPS[8 * side : 8 * side + 8]
        tiles = [read_tile(weights, 0, 2, 1 + tile, groups) for tile in range(3)]
        total = dot(low[...], jnp.concatenate(tiles, axis=1), NT)
        for chunk in range(3):
            columns = slice(128 * chunk, 128 * chunk + 128)
            kept.mixed[3 * side + chunk] = total[:, columns].astype(BF16)
    for tile in range(3):
        part_low = low[:, 256 * tile : 256 * tile + 256]
        write_tile(weights, 0, 2, 1 + tile, dot(turned[...], part_low))
    tick(8)

    low_half = lax.broadcasted_iota(jnp.int32, (256, 128), 1) < 64
    halves = half_masks()
    for pair in range(6):
        queries, keys, values = kept.proj[pair], kept.proj[6 + pair], kept.proj[12 + pair]
        back = kept.mixed[pair]
        scores, grads_k, grads_v = [], [], []
        for side in range(2):
            soft = kept.soft[2 * pair + side]
            weight = soft.astype(F32)
            grad_soft = dot(values, back * (halves[side] * jnp.asarray(0.125, BF16)), NT)
            inner = jnp.sum(weight * grad_soft, axis=0, keepdims=True)
            grad_score = (weight * (grad_soft - inner)).astype(BF16)
            scores.append(grad_score)
            grads_k.append(dot(grad_score, queries))
            grads_v.append(dot(soft, back))
        both_keys = jnp.concatenate([keys * halves[0], keys * halves[1]], axis=0)
        kept.proj[pair] = dot(jnp.concatenate(scores, axis=0), both_keys, TN).astype(BF16)
        for first, both in ((6, grads_k), (12, grads_v)):
            kept.proj[first + pair] = jnp.where(low_half, both[0], both[1]).astype(BF16)
        if pair % 3 == 2:
            tick(9 + pair // 3)

    def turn(state):
        for first in (0, 128):
            rows = pl.ds(first, 128)
            turned[:, rows] = state(rows).astype(BF16).T

    turn_state(turn)
    for k in range(3):
        for inner in range(TILES[k]):
            pair = chunks_of(kept.proj, 8 * k + 2 * inner, 2)
            acc[...] += dot(pair, read_tile(weights, 0, k, inner), NT)
            write_tile(weights, 0, k, inner, dot(turned[...], pair))
        tick(11 + k)


def member_rows(extra, who):
    y_lo, x_lo, core = who // 4, who // 2 % 2, who % 2
    return jnp.concatenate(
        [
            extra[(k,) + place(k, core, 2 * x_hi + x_lo, 2 * y_hi + y_lo, z)]
            for x_hi, z, y_hi in GROUPS
            for k in range(2)
        ],
        axis=0,
    )


def write_member_rows(extra, who, values):
    y_lo, x_lo, core = who // 4, who // 2 % 2, who % 2
    for at, (x_hi, z, y_hi) in enumerate(GROUPS):
        for k in range(2):
            first = 32 * at + 16 * k
            into = (k,) + place(k, core, 2 * x_hi + x_lo, 2 * y_hi + y_lo, z)
            extra[into] = values[first : first + 16].astype(BF16)


def pick_rows(rows, columns, width):
    row = lax.broadcasted_iota(jnp.int32, (rows, columns), 0)
    column = lax.broadcasted_iota(jnp.int32, (rows, columns), 1)
    from_first = column - width * lax.shift_right_logical(row, 2)
    inside = jnp.logical_and(from_first >= 0, from_first < width)
    return jnp.where(inside, 1.0, 0.0).astype(BF16)


def pick_lanes(rows, columns, width):
    row = lax.broadcasted_iota(jnp.int32, (rows, columns), 0).astype(F32)
    column = lax.broadcasted_iota(jnp.int32, (rows, columns), 1).astype(F32)
    remainder = column - width * jnp.floor((column + 0.5) * (1.0 / width))
    return jnp.where(remainder == row, 1.0, 0.0)


def read_time_bias(extra):
    small = member_rows(extra, 7)
    pick, lanes = pick_rows(128, 128, 4), pick_lanes(8, 128, 4)
    return jnp.concatenate(
        [
            jnp.sum(dot(small[128 * at : 128 * at + 128], pick, TN)[:8] * lanes, axis=0, keepdims=True)
            for at in range(4)
        ],
        axis=1,
    )


def read_vectors(extra, norms, bias):
    small = member_rows(extra, 7)
    pick, lanes = pick_rows(256, 384, 6), pick_lanes(8, 384, 6)
    for at in range(2):
        spread = dot(small[256 * at : 256 * at + 256], pick, TN)
        for vector in range(8):
            value = jnp.sum(spread[8 + 8 * vector : 16 + 8 * vector] * lanes, axis=0, keepdims=True)
            norms[vector // 4, vector % 4 : vector % 4 + 1, 384 * at : 384 * at + 384] = value
    pick, lanes = pick_rows(64, 384, 24), pick_lanes(24, 384, 24)
    for at in range(8):
        spread = dot(small[64 * at : 64 * at + 64], pick, TN)
        for layer in range(2):
            value = spread[72 + 24 * layer : 96 + 24 * layer] * lanes
            bias[layer, :, 384 * at : 384 * at + 384] = jnp.sum(value, axis=0, keepdims=True)


def time_weights(extra):
    return jnp.concatenate([member_rows(extra, who) for who in range(6)], axis=1)


def time_forward(extra, emb, time_bias, time_pre, time_act, temb):
    by_chunk = dot(emb[...], member_rows(extra, 6))
    pre = jnp.concatenate([by_chunk[at : at + 1] for at in range(4)], axis=1) + time_bias
    act = (pre * lax.logistic(pre)).astype(BF16)
    time_pre[...] = pre
    time_act[...] = act.astype(F32)
    temb[...] = dot(jnp.broadcast_to(act, (8, 512)), time_weights(extra))[0:1]


def high_low(values):
    high = values.astype(BF16).astype(F32)
    return high, values - high


def time_backward(extra, emb, time_pre, time_act, grad, grad_norms, grad_bias):
    zero = lambda rows, columns: jnp.zeros((rows, columns), F32)
    total = jnp.sum(grad, axis=0, keepdims=True)
    both = jnp.concatenate(high_low(total) + (zero(6, 768),), axis=0).astype(BF16)
    grad_act = jnp.sum(dot(both, time_weights(extra), NT), axis=0, keepdims=True)
    pre = time_pre[...]
    gate = lax.logistic(pre)
    grad_pre = grad_act * gate * (1.0 + pre * (1.0 - gate))
    act = time_act[...]
    acts = jnp.concatenate([act, act, zero(6, 512)], axis=0).astype(BF16)
    for who in range(6):
        write_member_rows(extra, who, dot(acts, both[:, 128 * who : 128 * who + 128], TN))
    high, low = high_low(grad_pre)
    by_chunk = [side[:, 128 * at : 128 * at + 128] for side in (high, low) for at in range(4)]
    write_member_rows(extra, 6, dot(emb[...], jnp.concatenate(by_chunk, axis=0).astype(BF16), TN))

    pieces = []
    pick, lanes = pick_rows(64, 384, 24), pick_lanes(24, 384, 24)
    for at in range(8):
        rows = [zero(72, 384)] + [lanes * grad_bias[layer, at] for layer in range(2)] + [zero(8, 384)]
        pieces.append(dot(pick, jnp.concatenate(rows, axis=0).astype(BF16), NT))
    small = jnp.concatenate(pieces, axis=0)
    pick, lanes, pieces = pick_rows(256, 384, 6), pick_lanes(8, 384, 6), []
    for at in range(2):
        rows = [zero(8, 384)]
        for layer in range(2):
            for vector in range(4):
                rows.append(lanes * grad_norms[layer, vector, :, 384 * at : 384 * at + 384])
        rows.append(zero(56, 384))
        pieces.append(dot(pick, jnp.concatenate(rows, axis=0).astype(BF16), NT))
    small += jnp.concatenate(pieces, axis=0)
    pick, lanes, pieces = pick_rows(128, 128, 4), pick_lanes(8, 128, 4), []
    for at in range(4):
        rows = [lanes * grad_pre[:, 128 * at : 128 * at + 128], zero(120, 128)]
        pieces.append(dot(pick, jnp.concatenate(rows, axis=0).astype(BF16), NT))
    write_member_rows(extra, 7, small + jnp.concatenate(pieces, axis=0))


class Stop:
    def __init__(self, run):
        self.run, self.done, self.result = run, False, None

    def once(self):
        self.result = self.run()

    def steps(self, until):
        first, self.done = self.done, True
        return [] if first else [self.once]

    def advance(self, until):
        for step in self.steps(until):
            step()


class Clock:
    def __init__(self, plans):
        self.plans = [
            {
                stop: [step for travel, until in events for step in travel.steps(until)]
                for stop, events in plan.items()
            }
            for plan in plans
        ]

    def tick(self, index, stop):
        for at, plan in enumerate(self.plans):
            if plan.get(stop):

                @pl.when(index == at)
                def _(steps=plan[stop]):
                    for step in steps:
                        step()


def either(index, run, choices):
    for at, choice in enumerate(choices):

        @pl.when(index == at)
        def _(choice=choice):
            run(choice)


def whole_kernel(*refs):
    refs = list(refs)
    take = lambda count: [refs.pop(0) for _ in range(count)]
    src_len, total_len = take(2)
    step_of, frequencies = take(2)
    qkv, out_w, ffn_in, ffn_out, time_in, time_out, time_bias, ffn_bias = take(8)
    norm_parts = take(4)
    tokens, cotangent = take(2)
    got_a, got_b, kept_b, output_part, grad_part = take(5)
    (all_weights,) = take(1)
    weights = [all_weights.at[layer] for layer in range(2)]
    kept_refs = take(len(Kept.shapes))
    kept = [Kept(kept_refs, layer) for layer in range(2)]
    acc, turned, shut, norms, bias, grad_norms, grad_bias = take(7)
    extra, emb, time_pre, time_act, temb = take(5)
    tokens_all, cotangent_all, leaving = take(3)
    send_a, send_b, rows, rows_b = take(4)
    pair, half, full = take(3)
    buffers_x = take(5)
    spread_sems, reduce_sems = take(2), take(2)
    first_sems, last_sems, move_sems = take(3)
    pair_free, ring_free, gone_free = take(3)

    at = here()
    mine, core = member(at), at["core"]
    my_stream = stream_of(at)
    partners = greet(at)

    def pack(layer):
        for to in range(8):
            for k in range(6):
                chunk = to + 8 * (k % 3)
                source, column = (qkv, chunk) if chunk < 18 else (out_w, chunk - 18)
                if k >= 3:
                    source, column = ffn_in, chunk
                piece = source[:, layer, 128 * column : 128 * column + 128]
                send_a[layer, to, k, 0:6, :] = piece.astype(F32)
        for k in range(3):
            column = pl.multiple_of(128 * (3 * (1 - core) + k), 128)
            send_b[layer, k] = ffn_out[layer, :, pl.ds(column, 128)].astype(F32)

    class Trade:
        def __init__(self, layer, sems, slots):
            self.sems = lambda kind: sems.at[layer, kind]
            self.all_a, self.all_b = got_a.at[layer, pl.ds(0, 7), pl.ds(0, slots)], got_b.at[layer]
            for flip in FLIPS:
                to = flipped(at, *flip)
                src = send_a.at[layer, member(to), pl.ds(0, slots)]
                dst = got_a.at[layer, mine, pl.ds(0, slots)]
                remote(src, dst, self.sems(0), self.sems(1), to).start()
            twin = flipped(at, 0, 0, 1)
            remote(send_b.at[layer], got_b.at[layer], self.sems(2), self.sems(3), twin).start()
            got_a[layer, mine] = send_a[layer, mine]

        def arrived(self):
            wait_bytes(self.all_a, self.sems(1))
            wait_bytes(self.all_b, self.sems(3))

        def left(self):
            wait_bytes(self.all_a, self.sems(0))
            wait_bytes(self.all_b, self.sems(2))

    class Move:
        def __init__(self, number, src, dst, split, later=False):
            self.sems = lambda kind: move_sems.at[number, kind]
            self.what = (src, dst, split)
            if not later:
                self.start()

        def start(self):
            src, dst, split = self.what
            rows_of = lambda who: pl.ds(pl.multiple_of(64 * who, 64), 64)
            own_src = src.at[rows_of(my_stream)] if split else src.at[my_stream]
            own_dst = dst.at[my_stream] if split else dst.at[rows_of(my_stream)]
            pltpu.make_async_copy(own_src, own_dst, self.sems(0)).start()
            for flip in range(1, 4):
                to = flipped(at, 0, flip // 2, flip % 2)
                there = src.at[rows_of(stream_of(to))] if split else src.at[stream_of(to)]
                remote(there, own_dst, self.sems(1), self.sems(2), to).start()

        def wait(self):
            wait_bytes(tokens_all.at[pl.ds(0, 64)], self.sems(0))
            for kind in (1, 2):
                wait_bytes(tokens_all.at[pl.ds(0, 192)], self.sems(kind))

    pack(0)
    for to in range(8):
        send_a[0, to, 6] = jnp.zeros((8, 128), F32)
        if to < 6:
            send_a[0, to, 6, 0:4, :] = time_out[:, 128 * to : 128 * to + 128].astype(F32)
        elif to == 6:
            for chunk in range(4):
                columns = slice(128 * chunk, 128 * chunk + 128)
                send_a[0, to, 6, chunk : chunk + 1, :] = time_in[:, columns].astype(F32)
        else:
            send_a[0, to, 6, 0:1, 0:4] = time_bias[...].astype(F32)
            for layer in range(2):
                for vector in range(4):
                    first_lane = 8 + 32 * layer + 8 * vector
                    values = norm_parts[vector][layer : layer + 1, :].astype(F32)
                    send_a[0, to, 6, 0:1, first_lane : first_lane + 6] = values
                first_lane = 72 + 24 * layer
                values = ffn_bias[layer : layer + 1, :].astype(F32)
                send_a[0, to, 6, 0:1, first_lane : first_lane + 24] = values
    pl.semaphore_wait(pltpu.get_barrier_semaphore(), partners)
    first = [Trade(0, first_sems, 7)]
    pack(1)
    first.append(Trade(1, first_sems, 6))
    bring_tokens = Move(0, tokens, tokens_all, False)

    mine_at = [tuple(at[name] for name in AXES[k]) for k in range(3)]

    def assemble_part(layer, part):
        for k in range(3):
            if part == 2:
                column = pl.multiple_of(128 * (3 * core + k), 128)
                rows_b[core] = ffn_out[layer, :, pl.ds(column, 128)].astype(F32)
                rows_b[1 - core] = got_b[layer, k]
                unit = rows_b[...].reshape(48, 128)
            else:
                for frm in range(8):
                    rows[6 * frm : 6 * frm + 6, :] = got_a[layer, frm, 3 * part + k, 0:6, :]
                unit = rows[...]
            weights[layer][(part, k, core) + mine_at[k]] = unit.astype(BF16)

    spread = {}
    for layer in range(2):
        for part in range(3):
            blocks = weights[layer].at[part]
            ring = layer + part > 0
            spread[layer, part] = Spread(3 * layer + part, blocks, at, spread_sems, ring)
    spread_x = Spread(6, extra, at, spread_sems, False)

    def advance(*steps):
        for layer, part, until in steps:
            spread[layer, part].advance(until)

    angles = step_of[my_stream] * frequencies[...]
    column = lax.broadcasted_iota(jnp.int32, (1, 512), 1)
    features = jnp.where(column < 256, jnp.sin(angles), jnp.cos(angles))
    column = lax.broadcasted_iota(jnp.int32, (8, 512), 1)
    row = lax.broadcasted_iota(jnp.int32, (8, 512), 0)
    same = lax.bitwise_and(column, 3) == lax.bitwise_and(row, 3)
    emb[...] = jnp.where(same, jnp.broadcast_to(features, (8, 512)), 0.0).astype(BF16)

    first[0].arrived()
    assemble_part(0, 0)
    advance((0, 0, 1))
    for frm in range(8):
        rows[4 * frm : 4 * frm + 4, :] = got_a[0, frm, 6, 0:4, :]
    for k in range(2):
        extra[(k, core) + mine_at[k]] = rows[16 * k : 16 * k + 16, :].astype(BF16)
    spread_x.advance(1)
    for part in (1, 2):
        assemble_part(0, part)
        advance((0, part, 1))
    advance((0, 0, 2))
    spread_x.advance(2)
    advance((0, 1, 2), (0, 2, 2))
    first[1].arrived()
    for part in range(3):
        assemble_part(1, part)
        advance((1, part, 1))
    advance((0, 0, 4))
    spread_x.advance(4)
    advance((0, 1, 3), (0, 2, 3), (1, 0, 2), (1, 1, 2), (1, 2, 2), (0, 0, 5))
    spread_x.advance(5)
    advance((0, 1, 4), (0, 2, 4), (1, 0, 3), (1, 1, 3), (1, 2, 3), (0, 0, 6))
    spread_x.advance(7)
    time_forward(extra, emb, read_time_bias(extra), time_pre, time_act, temb)
    advance((0, 1, 5), (0, 0, 7))
    read_vectors(extra, norms, bias)
    lens = (src_len[my_stream], total_len[my_stream])
    key_at = lax.broadcasted_iota(jnp.int32, (256, 128), 0)
    bound = jnp.where(key_at < 128, lens[0], 128 + lens[1] - lens[0])
    shut[...] = jnp.where(key_at < bound, 0.0, -1e30)
    bring_tokens.wait()

    first_plan = {
        1: [(0, 2, 5), (1, 0, 4), (1, 1, 4)],
        4: [(0, 1, 6)],
        6: [(0, 1, 7), (0, 2, 6)],
        "unfeed": [(0, 2, 7)],
        10: [(1, 0, 5), (1, 2, 4)],
        11: [(1, 1, 5), (1, 0, 6)],
    }
    second_plan = {
        "qkv": [(1, 0, 7)],
        3: [(1, 2, 5)],
        5: [(1, 1, 6)],
        "feed": [(1, 1, 7)],
        7: [(1, 2, 6)],
        "unfeed": [(1, 2, 7)],
    }
    for plan in (first_plan, second_plan):
        for stops in plan.values():
            stops[:] = [(spread[layer, part], until) for layer, part, until in stops]
    bring_cotangent = Move(1, cotangent, cotangent_all, False, later=True)
    second_plan[3].append((Stop(bring_cotangent.start), 0))
    clock = Clock([first_plan, second_plan])
    states = [
        lambda rows: tokens_all[rows, :].astype(F32) + temb[...],
        lambda rows: kept[0].normal2[rows, :] * norms[0, 2:3, :] + norms[0, 3:4, :],
    ]

    def forward(layer, carry):
        forward_layer(
            lambda run: either(layer, run, states),
            norms.at[layer],
            bias.at[layer],
            shut,
            all_weights.at[layer],
            Kept(kept_refs, layer),
            acc,
            partial(clock.tick, layer),
        )
        return carry

    lax.fori_loop(0, 2, forward, 0)

    def leave(rows):
        final = kept[1].normal2[rows, :] * norms[1, 2:3, :] + norms[1, 3:4, :]
        leaving[rows, :] = final.astype(BF16)

    by_rows(leave)
    give_output = Move(2, leaving, output_part, True)
    for travel in list(spread.values()) + [spread_x]:
        travel.finish()
    for trade in first:
        trade.left()
    bring_cotangent.wait()
    by_rows(lambda rows: acc.__setitem__((rows, slice(None)), cotangent_all[rows, :].astype(F32)))

    there = pl.ds(pl.multiple_of(24 * (1 - core), 8), 24)
    near = pl.ds(pl.multiple_of(24 * core, 8), 24)

    def deliver(layer, part, k, total):
        rows[...] = total
        if part == 2:
            send_b[layer, k] = rows[there, :]
            kept_b[layer, k] = rows[near, :]
            return
        for to in range(8):
            send_a[layer, to, 3 * part + k, 0:6, :] = rows[6 * to : 6 * to + 6, :]

    def deliver_extra(k, total):
        rows[0:16, :] = total
        for to in range(4):
            send_a[0, 4 * k + to, 6, 0:4, :] = rows[4 * to : 4 * to + 4, :]

    around = [moved(at, axis, by) for axis in "xyz" for by in (1, -1, 2)]
    reduce = {}

    near_by = [moved(at, axis, by) for axis in "xyz" for by in (1, -1)]

    def gone(part):
        reduce[1, part].crossed()
        for to in around:
            signal(gone_free.at[part], to)

    def wait_gone(part):
        pl.semaphore_wait(gone_free.at[part], len(around))

    def free(part):
        signal(pair_free.at[part], flipped(at, 0, 0, 1))
        for to in near_by:
            signal(ring_free.at[part], to)

    def freed(part):
        pl.semaphore_wait(pair_free.at[part], 1)
        pl.semaphore_wait(ring_free.at[part], len(near_by))

    for layer in range(2):
        for part in range(3):
            spare = weights[1].at[part, :, 1 - core, layer]
            small_buffers = [spare.at[:, pl.ds(0, 3)], spare.at[:, 3, pl.ds(0, 3)]]
            reduce[layer, part] = Reduce(
                3 * layer + part,
                weights[layer].at[part],
                [pair.at[part], half.at[part], full.at[part]] + small_buffers,
                partial(deliver, layer, part),
                at,
                reduce_sems,
                layer + part > 0,
                None if layer else partial(freed, part),
                partial(wait_gone, part) if layer else None,
            )
    reduce_x = Reduce(6, extra, buffers_x, deliver_extra, at, reduce_sems, False, None, None)

    frees = [Stop(partial(free, part)) for part in range(3)]
    gones = [Stop(partial(gone, part)) for part in range(3)]
    second = lambda part, until: (reduce[1, part], until)
    early = lambda part, until: (reduce[0, part], until)
    give = lambda part, k: (Stop(partial(reduce[1, part].trade, k)), 0)
    for part in range(3):
        reduce[1, part].done = 1
    second_plan = {
        4: [give(2, 0), give(2, 1), give(2, 2)],
        5: [give(1, 0)],
        6: [give(1, 1), second(2, 2)],
        7: [give(1, 2)],
        9: [second(1, 2), second(2, 3), (gones[2], 0)],
        11: [give(0, 0)],
        12: [give(0, 1)],
        13: [give(0, 2), second(1, 3), (gones[1], 0)],
    }
    first_plan = {
        2: [second(0, 2)],
        4: [second(2, 4), (frees[2], 0)],
        6: [early(2, 1)],
        8: [early(2, 2), second(1, 4), (frees[1], 0)],
        9: [early(1, 1), second(0, 3), (gones[0], 0), second(2, 5)],
        10: [early(1, 2), early(2, 3), second(1, 5)],
    }
    clock = Clock([second_plan, first_plan])

    def backward(index, carry):
        layer = 1 - index
        backward_layer(
            lambda run: either(layer, run, states),
            norms.at[layer],
            all_weights.at[layer],
            Kept(kept_refs, layer),
            acc,
            cotangent_all,
            turned,
            grad_norms.at[layer],
            grad_bias.at[layer],
            partial(clock.tick, index),
        )
        return carry

    lax.fori_loop(0, 2, backward, 0)

    give_output.wait()
    by_rows(lambda rows: leaving.__setitem__((rows, slice(None)), acc[rows, :].astype(BF16)))
    time_backward(extra, emb, time_pre, time_act, acc[...], grad_norms, grad_bias)
    give_grad = Stop(lambda: Move(3, leaving, grad_part, True))
    give_rows = [Stop(partial(Trade, layer, last_sems, 7 - layer)) for layer in range(2)]
    rest = [
        second(0, 4), (frees[0], 0), second(2, 6), (reduce_x, 1), early(0, 1), (reduce_x, 2), early(1, 3), early(0, 2),
        early(2, 4), second(1, 6), second(0, 5), second(2, 7), (reduce_x, 3), early(1, 4), early(0, 3),
        early(2, 5), second(1, 7), second(0, 6), (reduce_x, 4), early(1, 5), (reduce_x, 5), early(0, 5),
        early(2, 6), second(0, 7), (give_rows[1], 0), (reduce_x, 6), early(1, 6), early(0, 6), (give_grad, 0),
        early(2, 7), (reduce_x, 7), early(1, 7), early(0, 7), (give_rows[0], 0),
    ]
    for travel, until in rest:
        travel.advance(until)
    for (layer, part), travel in reduce.items():
        travel.finish()
        if layer == 0:
            travel.crossed()
    reduce_x.finish()
    reduce_x.crossed()
    for give in give_rows:
        give.result.arrived()
        give.result.left()
    give_grad.result.wait()


def whole(*operands):
    vmem, anywhere = pl.BlockSpec(memory_space=pltpu.VMEM), pl.BlockSpec(memory_space=pl.ANY)
    smem = pl.BlockSpec(memory_space=pltpu.SMEM)
    dma, regular = pltpu.SemaphoreType.DMA, pltpu.SemaphoreType.REGULAR
    buffers = lambda lead, unit: [
        pltpu.VMEM(lead + shape + unit, BF16)
        for shape in ((4, 4, 4), (2, 2, 4), (2, 4, 4), (3, 4), (3,))
    ]
    scratch = [pltpu.VMEM((2, 3, 3, 2, 4, 4, 4) + UNIT, BF16)]
    scratch += [pltpu.VMEM((2,) + shape, kind) for _, shape, kind in Kept.shapes]
    scratch += [
        pltpu.VMEM((256, 768), F32),
        pltpu.VMEM((768, 256), BF16),
        pltpu.VMEM((256, 128), F32),
        pltpu.VMEM((2, 8, 768), F32),
        pltpu.VMEM((2, 1, 3072), F32),
        pltpu.VMEM((2, 4, 1, 768), F32),
        pltpu.VMEM((2, 8, 1, 384), F32),
        pltpu.VMEM((2, 2, 4, 4, 4) + EXTRA, BF16),
        pltpu.VMEM((8, 512), BF16),
        pltpu.VMEM((1, 512), F32),
        pltpu.VMEM((1, 512), F32),
        pltpu.VMEM((1, 768), F32),
        pltpu.VMEM((256, 768), BF16),
        pltpu.VMEM((256, 768), BF16),
        pltpu.VMEM((256, 768), BF16),
        pltpu.VMEM((2, 8, 7, 8, 128), F32),
        pltpu.VMEM((2, 3, 24, 128), F32),
        pltpu.VMEM((48, 128), F32),
        pltpu.VMEM((2, 24, 128), F32),
    ]
    scratch += buffers((3, 3), UNIT)[:3] + buffers((2,), EXTRA)
    scratch += [
        dma((7, SPREAD_SEMS)),
        dma((7, 2)),
        dma((7, REDUCE_SEMS)),
        dma((7, 2)),
        dma((2, 4)),
        dma((2, 4)),
        dma((4, 3)),
        regular((3,)),
        regular((3,)),
        regular((3,)),
    ]
    return pl.pallas_call(
        whole_kernel,
        out_shape=[
            jax.ShapeDtypeStruct((2, 8, 7, 8, 128), F32),
            jax.ShapeDtypeStruct((2, 3, 24, 128), F32),
            jax.ShapeDtypeStruct((2, 3, 24, 128), F32),
            jax.ShapeDtypeStruct((4, 64, 768), BF16),
            jax.ShapeDtypeStruct((4, 64, 768), BF16),
        ],
        in_specs=[smem] * 3 + [vmem] * 13 + [anywhere] * 2,
        out_specs=[vmem] * 3 + [anywhere] * 2,
        scratch_shapes=scratch,
        compiler_params=pltpu.CompilerParams(
            collective_id=1, has_side_effects=True, vmem_limit_bytes=VMEM_BYTES
        ),
        name="whole",
    )(*operands)


def finish_kernel(got_a, got_b, kept_b, output, grad, *results):
    out, grad_x, g_tin, g_bias, g_tout, g_qkv, g_out = results[:7]
    norm1_gain, norm1_bias, g_in, g_ffn_bias, g_ffn, norm2_gain, norm2_bias = results[7:]
    core = lax.rem(lax.axis_index("stream"), 2)
    out[...] = output[...]
    grad_x[...] = grad[...].astype(F32)
    for frm in range(8):
        for layer in range(2):
            for k in range(6):
                chunk = frm + 8 * (k % 3)
                into, column = (g_qkv, chunk) if chunk < 18 else (g_out, chunk - 18)
                if k >= 3:
                    into, column = g_in, chunk
                into[:, layer, 128 * column : 128 * column + 128] = got_a[layer, frm, k, 0:6, :]
        if frm < 6:
            g_tout[:, 128 * frm : 128 * frm + 128] = got_a[0, frm, 6, 0:4, :]
        elif frm == 6:
            for chunk in range(4):
                g_tin[:, 128 * chunk : 128 * chunk + 128] = got_a[0, frm, 6, chunk : chunk + 1, :]
        else:
            g_bias[...] = got_a[0, frm, 6, 0:1, 0:4]
            vectors = (norm1_gain, norm1_bias, norm2_gain, norm2_bias)
            for layer in range(2):
                here_at = slice(layer, layer + 1)
                for at, vector in enumerate(vectors):
                    lane = 8 + 32 * layer + 8 * at
                    vector[here_at, :] = got_a[0, frm, 6, 0:1, lane : lane + 6]
                lane = 72 + 24 * layer
                g_ffn_bias[here_at, :] = got_a[0, frm, 6, 0:1, lane : lane + 24]
    for layer in range(2):
        for k in range(3):
            near = pl.ds(pl.multiple_of(128 * (3 * core + k), 128), 128)
            there = pl.ds(pl.multiple_of(128 * (3 * (1 - core) + k), 128), 128)
            g_ffn[layer, :, near] = kept_b[layer, k]
            g_ffn[layer, :, there] = got_b[layer, k]


def finish(got_a, got_b, kept_b, output, grad):
    shapes = [
        (4, 64, 768),
        (4, 64, 768),
        (1, 512),
        (1, 4),
        (4, 768),
        (6, 2, 2304),
        (6, 2, 768),
        (2, 6),
        (2, 6),
        (6, 2, 3072),
        (2, 24),
        (2, 24, 768),
        (2, 6),
        (2, 6),
    ]
    vmem = pl.BlockSpec(memory_space=pltpu.VMEM)
    return pl.pallas_call(
        finish_kernel,
        out_shape=[
            jax.ShapeDtypeStruct(shape, F32 if at else BF16) for at, shape in enumerate(shapes)
        ],
        in_specs=[vmem] * 5,
        out_specs=[vmem] * len(shapes),
        compiler_params=pltpu.CompilerParams(vmem_limit_bytes=VMEM_BYTES),
        name="lay_out_results",
    )(got_a, got_b, kept_b, output, grad)


def per_device(
    tokens,
    timestep,
    src_len,
    total_len,
    time_in,
    time_bias,
    time_out,
    qkv_weight,
    out_weight,
    norm1_gain,
    norm1_bias,
    ffn_in,
    ffn_bias,
    ffn_out,
    norm2_gain,
    norm2_bias,
    cotangent,
):
    frequencies = np.exp(-math.log(10000.0) * np.arange(64) / 64)
    by_layer = lambda weight: weight.transpose(1, 0, 2)
    got = whole(
        src_len,
        total_len,
        timestep,
        jnp.asarray(np.repeat(np.tile(frequencies, 2), 4)[None, :], F32),
        by_layer(qkv_weight),
        by_layer(out_weight),
        by_layer(ffn_in),
        ffn_out,
        time_in,
        time_out,
        time_bias[None, :],
        ffn_bias,
        norm1_gain,
        norm1_bias,
        norm2_gain,
        norm2_bias,
        tokens,
        cotangent,
    )
    results = list(finish(*got))
    results[3] = results[3][0]
    for at in (5, 6, 9):
        results[at] = by_layer(results[at])
    return tuple(results)


def solution(mesh):
    in_specs = (
        P("batch", "stream", None),
        P("batch"),
        P("batch"),
        P("batch"),
        P(("batch", "stream"), None),
        P(("batch", "stream")),
        P(("batch", "stream"), None),
        P(None, ("batch", "stream"), None),
        P(None, ("batch", "stream"), None),
        P(None, ("batch", "stream")),
        P(None, ("batch", "stream")),
        P(None, ("batch", "stream"), None),
        P(None, ("batch", "stream")),
        P(None, ("batch", "stream"), None),
        P(None, ("batch", "stream")),
        P(None, ("batch", "stream")),
        P("batch", "stream", None),
    )
    out_specs = (
        P("batch", "stream", None),
        P("batch", "stream", None),
        P(("batch", "stream"), None),
        P(("batch", "stream")),
        P(("batch", "stream"), None),
        P(None, ("batch", "stream"), None),
        P(None, ("batch", "stream"), None),
        P(None, ("batch", "stream")),
        P(None, ("batch", "stream")),
        P(None, ("batch", "stream"), None),
        P(None, ("batch", "stream")),
        P(None, ("batch", "stream"), None),
        P(None, ("batch", "stream")),
        P(None, ("batch", "stream")),
    )
    return jax.shard_map(
        per_device, mesh=mesh, in_specs=in_specs, out_specs=out_specs, check_vma=False
    )
```

```python
from functools import partial
import math

import jax
import jax.numpy as jnp
import numpy as np
from jax import lax
from jax.experimental import pallas as pl
from jax.experimental.pallas import tpu as pltpu
from jax.sharding import PartitionSpec as P

F32, BF16 = jnp.float32, jnp.bfloat16
EPS = 1e-05
NN = (((1,), (0,)), ((), ()))
NT = (((1,), (1,)), ((), ()))
TN = (((0,), (0,)), ((), ()))
MESH = pl.DeviceIdType.MESH
VMEM_BYTES = 65400 * 1024
AXES = ("zyx", "xzy", "yxz")
UNIT = (48, 128)
EXTRA = (16, 128)
GROUPS = [(x_hi, z, y_hi) for x_hi in range(2) for z in range(4) for y_hi in range(2)]
FLIPS = [(flip // 4, flip // 2 % 2, flip % 2) for flip in range(1, 8)]
TILES = (4, 4, 1)
SPREAD_SEMS, REDUCE_SEMS = 6, 7


def dot(left, right, dims=NN):
    return lax.dot_general(left, right, dims, preferred_element_type=F32)


def here():
    batch, stream = lax.axis_index("batch"), lax.axis_index("stream")
    return {
        "x": 2 * lax.div(batch, 16) + lax.div(stream, 2),
        "y": lax.rem(batch, 4),
        "z": lax.rem(lax.div(batch, 4), 4),
        "core": lax.rem(stream, 2),
    }


def device(at):
    return (
        lax.div(at["x"], 2) * 16 + at["z"] * 4 + at["y"],
        lax.rem(at["x"], 2) * 2 + at["core"],
    )


def moved(at, axis, by):
    return {**at, axis: lax.rem(at[axis] + by + 4, 4)}


def flipped(at, flip_y, flip_x, flip_core):
    new = dict(at)
    if flip_y:
        new["y"] = at["y"] + 1 - 2 * lax.rem(at["y"], 2)
    if flip_x:
        new["x"] = at["x"] + 1 - 2 * lax.rem(at["x"], 2)
    if flip_core:
        new["core"] = 1 - at["core"]
    return new


def member(at):
    return lax.rem(at["y"], 2) * 4 + lax.rem(at["x"], 2) * 2 + at["core"]


def stream_of(at):
    return lax.rem(at["x"], 2) * 2 + at["core"]


def signal(sem, to):
    pl.semaphore_signal(sem, inc=1, device_id=device(to), device_id_type=MESH)


def greet(at):
    partners = [flipped(at, *flip) for flip in FLIPS]
    partners += [moved(at, "z", 1), moved(at, "z", -1)]
    partners += [moved(at, axis, 2 * lax.rem(at[axis], 2) - 1) for axis in "xy"]
    partners += [moved(at, axis, 2) for axis in "xyz"]
    barrier = pltpu.get_barrier_semaphore()
    for partner in partners:
        signal(barrier, partner)
    return len(partners)


def remote(src, dst, send_sem, recv_sem, to):
    return pltpu.make_async_remote_copy(
        src_ref=src,
        dst_ref=dst,
        send_sem=send_sem,
        recv_sem=recv_sem,
        device_id=device(to),
        device_id_type=MESH,
    )


def wait_bytes(ref, sem):
    pltpu.make_async_copy(ref, ref, sem).wait()


def pick(k, options):
    if isinstance(k, int):
        return options[k]
    first, second, third = options
    return (
        lax.div((1 - k) * (2 - k), 2) * first + k * (2 - k) * second + lax.div(k * (k - 1), 2) * third
    )


class Travel:
    def __init__(self, number, blocks, at, sems, ring):
        self.at, self.ring, self.blocks = at, ring, blocks
        self.units = blocks.shape[0]
        self.recv_sem = lambda kind: sems[0].at[number, kind]
        self.send_sem = lambda kind: sems[1].at[number, kind]
        self.done = 0

    def own(self, k):
        return self.blocks.at[k, self.at["core"]]

    def gone(self, k):
        return self.blocks.at[k, 1 - self.at["core"]]

    def cells(self, count):
        return self.blocks.at[:, 0, 0, 0, pl.ds(0, count)]

    def lines(self, count):
        return self.blocks.at[:, 0, 0, pl.ds(0, count)]

    def planes(self, count):
        return self.blocks.at[:, 0, pl.ds(0, count)]

    def turn(self, k, level, by=0):
        place = pick(k, [self.at[order[level]] for order in AXES])
        return lax.rem(place + by + 4, 4) if by else place

    def neighbour(self, k, level, by):
        new = self.turn(k, level, by)
        to = dict(self.at)
        for axis in "xyz":
            here_it_is = pick(k, [int(order[level] == axis) for order in AXES])
            to[axis] = self.at[axis] + here_it_is * (new - self.at[axis])
        return to

    def twin(self):
        return flipped(self.at, 0, 0, 1)

    def each(self, body):
        def step(k, carry):
            body(k)
            return carry

        lax.fori_loop(0, self.units, step, 0)

    def arrive(self, kind, total):
        wait_bytes(total, self.recv_sem(kind))

    def depart(self, kind, pieces, before):
        if before is not None:
            self.departed(before)

        def start(k):
            for src, dst, to in pieces(k):
                remote(src, dst, self.send_sem(0), self.recv_sem(kind), to).start()

        self.each(start)

    def departed(self, total):
        wait_bytes(total, self.send_sem(0))

    def crossed(self):
        wait_bytes(self.blocks.at[:, 0], self.send_sem(1))

    def steps(self, until):
        first, self.done = self.done, max(self.done, until)
        return [partial(self.step, number) for number in range(first, until)]

    def advance(self, until):
        for step in self.steps(until):
            step()


class Spread(Travel):
    def share(self, ref):
        remote(ref, ref, self.send_sem(1), self.recv_sem(5), self.twin()).start()

    def pass_on(self, kind, level, came, before):
        def pieces(k):
            for side, by in ((0, -1), (1, 1)):
                piece = came(k, by).at[pl.ds(2 * side, 2)]
                yield piece, piece, self.neighbour(k, level, -by)

        self.depart(kind, pieces, before)

    def send_block(self, kind, level, sides, block, before):
        def pieces(k):
            mine = block(k)
            return [(mine, mine, self.neighbour(k, level, by)) for by in sides]

        self.depart(kind, pieces, before)

    def step(self, number):
        own, turn = self.own, self.turn
        plane = lambda k, by=0: own(k).at[turn(k, 0, by)]
        line = lambda k, by=0: own(k).at[turn(k, 0), turn(k, 1, by)]
        cell = lambda k: own(k).at[turn(k, 0), turn(k, 1), turn(k, 2)]
        if number == 0:
            self.send_block(0, 2, (1, -1, 2), cell, None)
        elif number == 1:
            self.arrive(0, self.cells(3))
            sides = (1, -1) if self.ring else (1, -1, 2)
            self.send_block(1, 1, sides, line, self.cells(3))
        elif number == 2 and self.ring:
            self.arrive(1, self.lines(2))
            self.pass_on(2, 1, line, self.lines(2))
        elif number == 3:
            if self.ring:
                self.arrive(2, self.lines(1))
            else:
                self.arrive(1, self.lines(3))
            self.send_block(3, 0, (1, -1), plane, self.lines(1 if self.ring else 3))
            self.each(lambda k: self.share(plane(k)))
        elif number == 4:
            self.arrive(3, self.planes(2))
            self.pass_on(4, 0, plane, self.planes(2))

            def share(k):
                for by in (1, -1):
                    self.share(plane(k, by))

            self.each(share)
        elif number == 5:
            self.arrive(4, self.planes(1))
            self.each(lambda k: self.share(plane(k, 2)))
        elif number == 6:
            self.arrive(5, self.blocks.at[:, 0])

    def finish(self):
        self.departed(self.planes(1))
        self.crossed()


class Reduce(Travel):
    def __init__(self, number, blocks, buffers, result, at, sems, ring, credits, row_credits):
        super().__init__(number, blocks, at, sems, ring)
        self.pair, self.half, self.full, self.row, self.cell = buffers
        self.result, self.traded = result, 0
        self.credits, self.row_credits = credits, row_credits

    def trade(self, k):
        for kind, by in ((0, 2), (1, 1), (1, -1), (1, 0)):
            plane = self.turn(k, 0, by)
            src, dst = self.gone(k).at[plane], self.pair.at[k, plane]
            remote(src, dst, self.send_sem(1), self.recv_sem(kind), self.twin()).start()

    def meet(self, k, by):
        plane, own = self.turn(k, 0, by), self.own(k)
        own[plane] = own[plane] + self.pair[k, plane]

    def start_ring(self, kind, level, opposite, halves, before):
        def pieces(k):
            for side, by in ((0, 1), (1, -1)):
                piece = opposite(k).at[pl.ds(2 * side, 2)]
                yield piece, halves(k, side), self.neighbour(k, level, by)

        self.depart(kind, pieces, before)

    def step(self, number):
        own, turn = self.own, self.turn
        if number == 0:
            if self.credits is not None:
                self.credits()
            self.each(self.trade)
        elif number == 1:
            self.arrive(0, self.planes(1))
            self.each(lambda k: self.meet(k, 2))
            opposite = lambda k: own(k).at[turn(k, 0, 2)]
            self.start_ring(2, 0, opposite, lambda k, side: self.half.at[k, side], None)
        elif number == 2:
            self.arrive(1, self.planes(3))

            def meet(k):
                for by in (1, -1, 0):
                    self.meet(k, by)

            self.each(meet)
            self.arrive(2, self.planes(1))

            def pieces(k):
                ref = own(k)
                for side, by in ((0, 1), (1, -1)):
                    plane, rows = turn(k, 0, by), pl.ds(2 * side, 2)
                    ref[plane, rows] = ref[plane, rows] + self.half[k, side]
                    yield ref.at[plane], self.full.at[k, side], self.neighbour(k, 0, by)

            self.depart(3, pieces, self.planes(1))
        elif number == 3:
            self.arrive(3, self.planes(2))

            def settle(k):
                c, ref = turn(k, 0), own(k)
                total = ref[c].astype(F32) + self.full[k, 0].astype(F32)
                ref[c] = (total + self.full[k, 1].astype(F32)).astype(BF16)

            self.each(settle)
            if self.row_credits is not None:
                self.row_credits()
            if self.ring:
                opposite = lambda k: own(k).at[turn(k, 0), turn(k, 1, 2)]
                halves = lambda k, side: self.row.at[k, 2, pl.ds(2 * side, 2)]
                self.start_ring(4, 1, opposite, halves, self.planes(2))
            else:

                def pieces(k):
                    for side, by in enumerate((1, -1, 2)):
                        line = own(k).at[turn(k, 0), turn(k, 1, by)]
                        yield line, self.row.at[k, side], self.neighbour(k, 1, by)

                self.depart(5, pieces, self.planes(2))
        elif number == 4 and self.ring:
            self.arrive(4, self.lines(1))

            def pieces(k):
                c, ref = turn(k, 0), own(k)
                for side, by in ((0, 1), (1, -1)):
                    line, cells = turn(k, 1, by), pl.ds(2 * side, 2)
                    ref[c, line, cells] = ref[c, line, cells] + self.row[k, 2, cells]
                    yield ref.at[c, line], self.row.at[k, side], self.neighbour(k, 1, by)

            self.depart(5, pieces, self.lines(1))
        elif number == 5:
            count = 2 if self.ring else 3
            self.arrive(5, self.lines(count))

            def pieces(k):
                c, b, ref = turn(k, 0), turn(k, 1), own(k)
                total = ref[c, b].astype(F32)
                for side in range(count):
                    total += self.row[k, side].astype(F32)
                ref[c, b] = total.astype(BF16)
                for side, by in enumerate((1, -1, 2)):
                    yield ref.at[c, b, turn(k, 2, by)], self.cell.at[k, side], self.neighbour(k, 2, by)

            self.depart(6, pieces, self.lines(count))
        elif number == 6:
            self.arrive(6, self.cells(3))

            def settle(k):
                total = own(k)[turn(k, 0), turn(k, 1), turn(k, 2)].astype(F32)
                for side in range(3):
                    total += self.cell[k, side].astype(F32)
                self.result(k, total)

            self.each(settle)

    def finish(self):
        self.departed(self.cells(3))


def place(k, core, x, y, z):
    at = {"x": x, "y": y, "z": z}
    return (core,) + tuple(at[name] for name in AXES[k])


def read_tile(weights, part, k, inner, groups=GROUPS):
    y_lo, x_lo = inner // 2, inner % 2
    return jnp.concatenate(
        [
            jnp.concatenate(
                [
                    weights[(part, k) + place(k, core, 2 * x_hi + x_lo, 2 * y_hi + y_lo, z)]
                    for x_hi, z, y_hi in groups
                ],
                axis=0,
            )
            for core in range(2)
        ],
        axis=1,
    )


def write_tile(grads, part, k, inner, values):
    y_lo, x_lo = inner // 2, inner % 2
    low = values.astype(BF16)
    for at, (x_hi, z, y_hi) in enumerate(GROUPS):
        for core in range(2):
            grads[(part, k) + place(k, core, 2 * x_hi + x_lo, 2 * y_hi + y_lo, z)] = low[
                48 * at : 48 * at + 48, 128 * core : 128 * core + 128
            ]


def read_rows(weights, step, chunks=range(6)):
    x_hi, z = step // 4, step % 4
    return jnp.concatenate(
        [
            jnp.concatenate(
                [
                    weights[(2, chunk % 3) + place(chunk % 3, chunk // 3, 2 * x_hi + x_lo, y, z)]
                    for y in range(4)
                    for x_lo in range(2)
                ],
                axis=0,
            )
            for chunk in chunks
        ],
        axis=1,
    )


def write_rows(grads, step, values):
    x_hi, z = step // 4, step % 4
    low = values.astype(BF16)
    for y in range(4):
        for x_lo in range(2):
            at = 48 * (2 * y + x_lo)
            for core in range(2):
                for k in range(3):
                    column = 128 * (3 * core + k)
                    grads[(2, k) + place(k, core, 2 * x_hi + x_lo, y, z)] = low[
                        at : at + 48, column : column + 128
                    ]


def chunks_of(ref, first, count):
    return jnp.concatenate([ref[first + at] for at in range(count)], axis=1)


def by_rows(step):
    for first in range(0, 256, 64):
        step(pl.ds(first, 64))


def normalize(values):
    center = values - jnp.mean(values, axis=-1, keepdims=True)
    scale = lax.rsqrt(jnp.mean(center * center, axis=-1, keepdims=True) + EPS)
    return center * scale, scale


def normalize_back(grad, gain, normal, scale):
    grad_normal = grad * gain
    mean_one = jnp.mean(grad_normal, axis=-1, keepdims=True)
    mean_two = jnp.mean(grad_normal * normal, axis=-1, keepdims=True)
    return scale * (grad_normal - mean_one - normal * mean_two)


def half_masks():
    lane = lax.broadcasted_iota(jnp.int32, (1, 128), 1)
    first = jnp.where(lane < 64, 1.0, 0.0)
    return first.astype(BF16), (1.0 - first).astype(BF16)


class Kept:
    shapes = (
        ("proj", (18, 256, 128), BF16),
        ("soft", (12, 256, 256), BF16),
        ("mixed", (6, 256, 128), BF16),
        ("normal1", (256, 768), BF16),
        ("first_low", (256, 768), BF16),
        ("act", (24, 256, 128), BF16),
        ("slope", (24, 256, 128), BF16),
        ("normal2", (256, 768), F32),
        ("scales", (256, 2), F32),
    )

    def __init__(self, refs, layer):
        for (name, _, _), ref in zip(self.shapes, refs):
            setattr(self, name, ref.at[layer])


def forward_layer(enter_state, norms, bias, shut, weights, kept, acc, tick):
    def enter(state, rows):
        values = state(rows)
        acc[rows, :] = values
        kept.first_low[rows, :] = values.astype(BF16)

    enter_state(lambda state: by_rows(partial(enter, state)))
    tick("qkv")
    for k in range(3):
        for inner in range(TILES[k]):
            out = dot(kept.first_low[...], read_tile(weights, 0, k, inner)).astype(BF16)
            chunk = 8 * k + 2 * inner
            kept.proj[chunk] = out[:, :128]
            kept.proj[chunk + 1] = out[:, 128:]
        tick(1 + k)

    low_half = lax.broadcasted_iota(jnp.int32, (256, 128), 1) < 64
    halves = half_masks()
    closed = jnp.concatenate([shut[...], shut[...]], axis=1)
    for pair in range(6):
        queries = kept.proj[pair] * jnp.asarray(0.125, BF16)
        keys = kept.proj[6 + pair]
        values = kept.proj[12 + pair]
        outs = []
        for side in range(2):
            scores = dot(keys, queries * halves[side], NT) + closed
            top = jnp.max(scores, axis=0, keepdims=True)
            exps = jnp.exp(scores - top)
            low = (exps * (1.0 / jnp.sum(exps, axis=0, keepdims=True))).astype(BF16)
            kept.soft[2 * pair + side] = low
            outs.append(dot(low, values, TN))
        kept.mixed[pair] = jnp.where(low_half, outs[0], outs[1]).astype(BF16)
        if pair % 3 == 2:
            tick(4 + pair // 3)

    mixed_all = chunks_of(kept.mixed, 0, 6)
    for tile in range(3):
        columns = pl.ds(256 * tile, 256)
        acc[:, columns] += dot(mixed_all, read_tile(weights, 0, 2, 1 + tile))

    def first_norm(rows):
        normal, scale = normalize(acc[rows, :])
        kept.normal1[rows, :] = normal.astype(BF16)
        kept.scales[rows, 0:1] = scale
        first = normal * norms[0:1, :] + norms[1:2, :]
        acc[rows, :] = first
        kept.first_low[rows, :] = first.astype(BF16)

    by_rows(first_norm)
    tick(6)
    tick("feed")

    for k in range(3):
        for tile in range(4 * k, 4 * k + 4):
            columns = slice(256 * tile, 256 * tile + 256)
            pre = dot(kept.first_low[...], read_tile(weights, 1, k, tile % 4)) + bias[0:1, columns]
            cdf = 0.5 * (1.0 + lax.erf(pre * math.sqrt(0.5)))
            out = (pre * cdf).astype(BF16)
            bell = jnp.exp(-0.5 * pre * pre) * (1.0 / math.sqrt(2 * math.pi))
            grad = (cdf + pre * bell).astype(BF16)
            kept.act[2 * tile] = out[:, :128]
            kept.act[2 * tile + 1] = out[:, 128:]
            kept.slope[2 * tile] = grad[:, :128]
            kept.slope[2 * tile + 1] = grad[:, 128:]
        tick(7 + k)
    tick("unfeed")
    for side in range(2):
        for tile in range(3):
            columns = slice(256 * tile, 256 * tile + 256)
            pair = (2 * tile, 2 * tile + 1)
            rows = [read_rows(weights, 4 * side + step, pair) for step in range(4)]
            acc[:, columns] += dot(
                chunks_of(kept.act, 12 * side, 12), jnp.concatenate(rows, axis=0)
            )
        tick(10 + side)

    def second_norm(rows):
        normal, scale = normalize(acc[rows, :])
        kept.normal2[rows, :] = normal
        kept.scales[rows, 1:2] = scale

    by_rows(second_norm)


def backward_layer(
    turn_state, norms, weights, kept, acc, low, turned, grad_norms, grad_bias, tick
):
    def norm_back(which, normal_of, grad_of):
        sums = [jnp.zeros((1, 768), F32), jnp.zeros((1, 768), F32)]

        def step(rows):
            grad, normal = grad_of(rows), normal_of(rows)
            sums[0] += jnp.sum(grad * normal, axis=0, keepdims=True)
            sums[1] += jnp.sum(grad, axis=0, keepdims=True)
            scale = kept.scales[rows, which : which + 1]
            out = normalize_back(grad, norms[2 * which : 2 * which + 1, :], normal, scale)
            acc[rows, :] = out
            low[rows, :] = out.astype(BF16)

        by_rows(step)
        grad_norms[2 * which] = sums[0]
        grad_norms[2 * which + 1] = sums[1]

    norm_back(1, lambda rows: kept.normal2[rows, :], lambda rows: acc[rows, :])
    for step in range(8):
        branch = low[...]
        grad_act = dot(branch, read_rows(weights, step), NT)
        pre_low = (grad_act * chunks_of(kept.slope, 3 * step, 3).astype(F32)).astype(BF16)
        for at in range(3):
            kept.slope[3 * step + at] = pre_low[:, 128 * at : 128 * at + 128]
        grad_bias[step] = jnp.sum(pre_low.astype(F32), axis=0, keepdims=True)
        write_rows(weights, step, dot(chunks_of(kept.act, 3 * step, 3), branch, TN))
        if step % 2:
            tick(1 + step // 2)
    turned[...] = kept.first_low[...].T
    for k in range(3):
        for inner in range(4):
            pre_low = chunks_of(kept.slope, 8 * k + 2 * inner, 2)
            acc[...] += dot(pre_low, read_tile(weights, 1, k, inner), NT)
            write_tile(weights, 1, k, inner, dot(turned[...], pre_low))
        tick(5 + k)

    norm_back(0, lambda rows: kept.normal1[rows, :].astype(F32), lambda rows: acc[rows, :])
    turned[...] = chunks_of(kept.mixed, 0, 6).T
    for side in range(2):
        groups = GROUPS[8 * side : 8 * side + 8]
        tiles = [read_tile(weights, 0, 2, 1 + tile, groups) for tile in range(3)]
        total = dot(low[...], jnp.concatenate(tiles, axis=1), NT)
        for chunk in range(3):
            columns = slice(128 * chunk, 128 * chunk + 128)
            kept.mixed[3 * side + chunk] = total[:, columns].astype(BF16)
    for tile in range(3):
        part_low = low[:, 256 * tile : 256 * tile + 256]
        write_tile(weights, 0, 2, 1 + tile, dot(turned[...], part_low))
    tick(8)

    low_half = lax.broadcasted_iota(jnp.int32, (256, 128), 1) < 64
    halves = half_masks()
    for pair in range(6):
        queries, keys, values = kept.proj[pair], kept.proj[6 + pair], kept.proj[12 + pair]
        back = kept.mixed[pair]
        scores, grads_k, grads_v = [], [], []
        for side in range(2):
            soft = kept.soft[2 * pair + side]
            weight = soft.astype(F32)
            grad_soft = dot(values, back * (halves[side] * jnp.asarray(0.125, BF16)), NT)
            inner = jnp.sum(weight * grad_soft, axis=0, keepdims=True)
            grad_score = (weight * (grad_soft - inner)).astype(BF16)
            scores.append(grad_score)
            grads_k.append(dot(grad_score, queries))
            grads_v.append(dot(soft, back))
        both_keys = jnp.concatenate([keys * halves[0], keys * halves[1]], axis=0)
        kept.proj[pair] = dot(jnp.concatenate(scores, axis=0), both_keys, TN).astype(BF16)
        for first, both in ((6, grads_k), (12, grads_v)):
            kept.proj[first + pair] = jnp.where(low_half, both[0], both[1]).astype(BF16)
        if pair % 3 == 2:
            tick(9 + pair // 3)

    def turn(state):
        for first in (0, 128):
            rows = pl.ds(first, 128)
            turned[:, rows] = state(rows).astype(BF16).T

    turn_state(turn)
    for k in range(3):
        for inner in range(TILES[k]):
            pair = chunks_of(kept.proj, 8 * k + 2 * inner, 2)
            acc[...] += dot(pair, read_tile(weights, 0, k, inner), NT)
            write_tile(weights, 0, k, inner, dot(turned[...], pair))
        tick(11 + k)


def member_rows(extra, who):
    y_lo, x_lo, core = who // 4, who // 2 % 2, who % 2
    return jnp.concatenate(
        [
            extra[(k,) + place(k, core, 2 * x_hi + x_lo, 2 * y_hi + y_lo, z)]
            for x_hi, z, y_hi in GROUPS
            for k in range(2)
        ],
        axis=0,
    )


def write_member_rows(extra, who, values):
    y_lo, x_lo, core = who // 4, who // 2 % 2, who % 2
    for at, (x_hi, z, y_hi) in enumerate(GROUPS):
        for k in range(2):
            first = 32 * at + 16 * k
            into = (k,) + place(k, core, 2 * x_hi + x_lo, 2 * y_hi + y_lo, z)
            extra[into] = values[first : first + 16].astype(BF16)


def pick_rows(rows, columns, width):
    row = lax.broadcasted_iota(jnp.int32, (rows, columns), 0)
    column = lax.broadcasted_iota(jnp.int32, (rows, columns), 1)
    from_first = column - width * lax.shift_right_logical(row, 2)
    inside = jnp.logical_and(from_first >= 0, from_first < width)
    return jnp.where(inside, 1.0, 0.0).astype(BF16)


def pick_lanes(rows, columns, width):
    row = lax.broadcasted_iota(jnp.int32, (rows, columns), 0).astype(F32)
    column = lax.broadcasted_iota(jnp.int32, (rows, columns), 1).astype(F32)
    remainder = column - width * jnp.floor((column + 0.5) * (1.0 / width))
    return jnp.where(remainder == row, 1.0, 0.0)


def read_time_bias(extra):
    small = member_rows(extra, 7)
    pick, lanes = pick_rows(128, 128, 4), pick_lanes(8, 128, 4)
    return jnp.concatenate(
        [
            jnp.sum(dot(small[128 * at : 128 * at + 128], pick, TN)[:8] * lanes, axis=0, keepdims=True)
            for at in range(4)
        ],
        axis=1,
    )


def read_vectors(extra, norms, bias):
    small = member_rows(extra, 7)
    pick, lanes = pick_rows(256, 384, 6), pick_lanes(8, 384, 6)
    for at in range(2):
        spread = dot(small[256 * at : 256 * at + 256], pick, TN)
        for vector in range(8):
            value = jnp.sum(spread[8 + 8 * vector : 16 + 8 * vector] * lanes, axis=0, keepdims=True)
            norms[vector // 4, vector % 4 : vector % 4 + 1, 384 * at : 384 * at + 384] = value
    pick, lanes = pick_rows(64, 384, 24), pick_lanes(24, 384, 24)
    for at in range(8):
        spread = dot(small[64 * at : 64 * at + 64], pick, TN)
        for layer in range(2):
            value = spread[72 + 24 * layer : 96 + 24 * layer] * lanes
            bias[layer, :, 384 * at : 384 * at + 384] = jnp.sum(value, axis=0, keepdims=True)


def time_weights(extra):
    return jnp.concatenate([member_rows(extra, who) for who in range(6)], axis=1)


def time_forward(extra, emb, time_bias, time_pre, time_act, temb):
    by_chunk = dot(emb[...], member_rows(extra, 6))
    pre = jnp.concatenate([by_chunk[at : at + 1] for at in range(4)], axis=1) + time_bias
    act = (pre * lax.logistic(pre)).astype(BF16)
    time_pre[...] = pre
    time_act[...] = act.astype(F32)
    temb[...] = dot(jnp.broadcast_to(act, (8, 512)), time_weights(extra))[0:1]


def high_low(values):
    high = values.astype(BF16).astype(F32)
    return high, values - high


def time_backward(extra, emb, time_pre, time_act, grad, grad_norms, grad_bias):
    zero = lambda rows, columns: jnp.zeros((rows, columns), F32)
    total = jnp.sum(grad, axis=0, keepdims=True)
    both = jnp.concatenate(high_low(total) + (zero(6, 768),), axis=0).astype(BF16)
    grad_act = jnp.sum(dot(both, time_weights(extra), NT), axis=0, keepdims=True)
    pre = time_pre[...]
    gate = lax.logistic(pre)
    grad_pre = grad_act * gate * (1.0 + pre * (1.0 - gate))
    act = time_act[...]
    acts = jnp.concatenate([act, act, zero(6, 512)], axis=0).astype(BF16)
    for who in range(6):
        write_member_rows(extra, who, dot(acts, both[:, 128 * who : 128 * who + 128], TN))
    high, low = high_low(grad_pre)
    by_chunk = [side[:, 128 * at : 128 * at + 128] for side in (high, low) for at in range(4)]
    write_member_rows(extra, 6, dot(emb[...], jnp.concatenate(by_chunk, axis=0).astype(BF16), TN))

    pieces = []
    pick, lanes = pick_rows(64, 384, 24), pick_lanes(24, 384, 24)
    for at in range(8):
        rows = [zero(72, 384)] + [lanes * grad_bias[layer, at] for layer in range(2)] + [zero(8, 384)]
        pieces.append(dot(pick, jnp.concatenate(rows, axis=0).astype(BF16), NT))
    small = jnp.concatenate(pieces, axis=0)
    pick, lanes, pieces = pick_rows(256, 384, 6), pick_lanes(8, 384, 6), []
    for at in range(2):
        rows = [zero(8, 384)]
        for layer in range(2):
            for vector in range(4):
                rows.append(lanes * grad_norms[layer, vector, :, 384 * at : 384 * at + 384])
        rows.append(zero(56, 384))
        pieces.append(dot(pick, jnp.concatenate(rows, axis=0).astype(BF16), NT))
    small += jnp.concatenate(pieces, axis=0)
    pick, lanes, pieces = pick_rows(128, 128, 4), pick_lanes(8, 128, 4), []
    for at in range(4):
        rows = [lanes * grad_pre[:, 128 * at : 128 * at + 128], zero(120, 128)]
        pieces.append(dot(pick, jnp.concatenate(rows, axis=0).astype(BF16), NT))
    write_member_rows(extra, 7, small + jnp.concatenate(pieces, axis=0))


class Stop:
    def __init__(self, run):
        self.run, self.done, self.result = run, False, None

    def once(self):
        self.result = self.run()

    def steps(self, until):
        first, self.done = self.done, True
        return [] if first else [self.once]

    def advance(self, until):
        for step in self.steps(until):
            step()


class Clock:
    def __init__(self, plans):
        self.plans = [
            {
                stop: [step for travel, until in events for step in travel.steps(until)]
                for stop, events in plan.items()
            }
            for plan in plans
        ]

    def tick(self, index, stop):
        for at, plan in enumerate(self.plans):
            if plan.get(stop):

                @pl.when(index == at)
                def _(steps=plan[stop]):
                    for step in steps:
                        step()


def either(index, run, choices):
    for at, choice in enumerate(choices):

        @pl.when(index == at)
        def _(choice=choice):
            run(choice)


def whole_kernel(*refs):
    refs = list(refs)
    take = lambda count: [refs.pop(0) for _ in range(count)]
    src_len, total_len = take(2)
    step_of, frequencies = take(2)
    qkv, out_w, ffn_in, ffn_out, time_in, time_out, time_bias, ffn_bias = take(8)
    norm_parts = take(4)
    tokens, cotangent = take(2)
    got_a, got_b, kept_b, output_part, grad_part = take(5)
    (all_weights,) = take(1)
    weights = [all_weights.at[layer] for layer in range(2)]
    kept_refs = take(len(Kept.shapes))
    kept = [Kept(kept_refs, layer) for layer in range(2)]
    acc, turned, shut, norms, bias, grad_norms, grad_bias = take(7)
    extra, emb, time_pre, time_act, temb = take(5)
    tokens_all, cotangent_all, leaving = take(3)
    send_a, send_b, rows, rows_b = take(4)
    pair, half, full = take(3)
    buffers_x = take(5)
    spread_sems, reduce_sems = take(2), take(2)
    first_sems, last_sems, move_sems = take(3)
    pair_free, ring_free, gone_free = take(3)

    at = here()
    mine, core = member(at), at["core"]
    my_stream = stream_of(at)
    partners = greet(at)

    def pack(layer):
        for to in range(8):
            for k in range(6):
                chunk = to + 8 * (k % 3)
                source, column = (qkv, chunk) if chunk < 18 else (out_w, chunk - 18)
                if k >= 3:
                    source, column = ffn_in, chunk
                piece = source[:, layer, 128 * column : 128 * column + 128]
                send_a[layer, to, k, 0:6, :] = piece.astype(F32)
        for k in range(3):
            column = pl.multiple_of(128 * (3 * (1 - core) + k), 128)
            send_b[layer, k] = ffn_out[layer, :, pl.ds(column, 128)].astype(F32)

    class Trade:
        def __init__(self, layer, sems, first_slot, slots, kinds=(0, 1), pair=True):
            self.sems = lambda kind: sems.at[layer, kind]
            self.kinds, self.pair = kinds, pair
            which = pl.ds(first_slot, slots)
            self.all_a, self.all_b = got_a.at[layer, pl.ds(0, 7), which], got_b.at[layer]
            for flip in FLIPS:
                to = flipped(at, *flip)
                src = send_a.at[layer, member(to), which]
                dst = got_a.at[layer, mine, which]
                remote(src, dst, self.sems(kinds[0]), self.sems(kinds[1]), to).start()
            if pair:
                twin = flipped(at, 0, 0, 1)
                remote(send_b.at[layer], got_b.at[layer], self.sems(2), self.sems(3), twin).start()
            got_a[layer, mine, which] = send_a[layer, mine, which]

        def arrived(self):
            wait_bytes(self.all_a, self.sems(self.kinds[1]))
            if self.pair:
                wait_bytes(self.all_b, self.sems(3))

        def left(self):
            wait_bytes(self.all_a, self.sems(self.kinds[0]))
            if self.pair:
                wait_bytes(self.all_b, self.sems(2))

    class Move:
        def __init__(self, number, src, dst, split, later=False):
            self.sems = lambda kind: move_sems.at[number, kind]
            self.what = (src, dst, split)
            if not later:
                self.start()

        def start(self):
            src, dst, split = self.what
            rows_of = lambda who: pl.ds(pl.multiple_of(64 * who, 64), 64)
            own_src = src.at[rows_of(my_stream)] if split else src.at[my_stream]
            own_dst = dst.at[my_stream] if split else dst.at[rows_of(my_stream)]
            pltpu.make_async_copy(own_src, own_dst, self.sems(0)).start()
            for flip in range(1, 4):
                to = flipped(at, 0, flip // 2, flip % 2)
                there = src.at[rows_of(stream_of(to))] if split else src.at[stream_of(to)]
                remote(there, own_dst, self.sems(1), self.sems(2), to).start()

        def wait(self):
            wait_bytes(tokens_all.at[pl.ds(0, 64)], self.sems(0))
            for kind in (1, 2):
                wait_bytes(tokens_all.at[pl.ds(0, 192)], self.sems(kind))

    pack(0)
    for to in range(8):
        send_a[0, to, 6] = jnp.zeros((8, 128), F32)
        if to < 6:
            send_a[0, to, 6, 0:4, :] = time_out[:, 128 * to : 128 * to + 128].astype(F32)
        elif to == 6:
            for chunk in range(4):
                columns = slice(128 * chunk, 128 * chunk + 128)
                send_a[0, to, 6, chunk : chunk + 1, :] = time_in[:, columns].astype(F32)
        else:
            send_a[0, to, 6, 0:1, 0:4] = time_bias[...].astype(F32)
            for layer in range(2):
                for vector in range(4):
                    first_lane = 8 + 32 * layer + 8 * vector
                    values = norm_parts[vector][layer : layer + 1, :].astype(F32)
                    send_a[0, to, 6, 0:1, first_lane : first_lane + 6] = values
                first_lane = 72 + 24 * layer
                values = ffn_bias[layer : layer + 1, :].astype(F32)
                send_a[0, to, 6, 0:1, first_lane : first_lane + 24] = values
    pl.semaphore_wait(pltpu.get_barrier_semaphore(), partners)
    first = [Trade(0, first_sems, 0, 3, (4, 5), False), Trade(0, first_sems, 3, 4)]
    pack(1)
    first.append(Trade(1, first_sems, 0, 6))
    bring_tokens = Move(0, tokens, tokens_all, False)

    mine_at = [tuple(at[name] for name in AXES[k]) for k in range(3)]

    def assemble_part(layer, part):
        for k in range(3):
            if part == 2:
                column = pl.multiple_of(128 * (3 * core + k), 128)
                rows_b[core] = ffn_out[layer, :, pl.ds(column, 128)].astype(F32)
                rows_b[1 - core] = got_b[layer, k]
                unit = rows_b[...].reshape(48, 128)
            else:
                for frm in range(8):
                    rows[6 * frm : 6 * frm + 6, :] = got_a[layer, frm, 3 * part + k, 0:6, :]
                unit = rows[...]
            weights[layer][(part, k, core) + mine_at[k]] = unit.astype(BF16)

    spread = {}
    for layer in range(2):
        for part in range(3):
            blocks = weights[layer].at[part]
            ring = layer + part > 0
            spread[layer, part] = Spread(3 * layer + part, blocks, at, spread_sems, ring)
    spread_x = Spread(6, extra, at, spread_sems, False)

    def advance(*steps):
        for layer, part, until in steps:
            spread[layer, part].advance(until)

    angles = step_of[my_stream] * frequencies[...]
    column = lax.broadcasted_iota(jnp.int32, (1, 512), 1)
    features = jnp.where(column < 256, jnp.sin(angles), jnp.cos(angles))
    column = lax.broadcasted_iota(jnp.int32, (8, 512), 1)
    row = lax.broadcasted_iota(jnp.int32, (8, 512), 0)
    same = lax.bitwise_and(column, 3) == lax.bitwise_and(row, 3)
    emb[...] = jnp.where(same, jnp.broadcast_to(features, (8, 512)), 0.0).astype(BF16)

    first[0].arrived()
    assemble_part(0, 0)
    advance((0, 0, 1))
    first[1].arrived()
    for frm in range(8):
        rows[4 * frm : 4 * frm + 4, :] = got_a[0, frm, 6, 0:4, :]
    for k in range(2):
        extra[(k, core) + mine_at[k]] = rows[16 * k : 16 * k + 16, :].astype(BF16)
    spread_x.advance(1)
    for part in (1, 2):
        assemble_part(0, part)
        advance((0, part, 1))
    advance((0, 0, 2))
    spread_x.advance(2)
    advance((0, 1, 2), (0, 2, 2))
    first[2].arrived()
    for part in range(3):
        assemble_part(1, part)
        advance((1, part, 1))
    advance((0, 0, 4))
    spread_x.advance(4)
    advance((0, 1, 3), (0, 2, 3), (1, 0, 2), (1, 1, 2), (1, 2, 2), (0, 0, 5))
    spread_x.advance(5)
    advance((0, 1, 4), (0, 2, 4), (1, 0, 3), (1, 1, 3), (1, 2, 3), (0, 0, 6))
    spread_x.advance(7)
    time_forward(extra, emb, read_time_bias(extra), time_pre, time_act, temb)
    advance((0, 1, 5), (0, 0, 7))
    read_vectors(extra, norms, bias)
    lens = (src_len[my_stream], total_len[my_stream])
    key_at = lax.broadcasted_iota(jnp.int32, (256, 128), 0)
    bound = jnp.where(key_at < 128, lens[0], 128 + lens[1] - lens[0])
    shut[...] = jnp.where(key_at < bound, 0.0, -1e30)
    bring_tokens.wait()

    first_plan = {
        1: [(0, 2, 5), (1, 0, 4), (1, 1, 4)],
        4: [(0, 1, 6)],
        6: [(0, 1, 7), (0, 2, 6)],
        "unfeed": [(0, 2, 7)],
        10: [(1, 0, 5), (1, 2, 4)],
        11: [(1, 1, 5), (1, 0, 6)],
    }
    second_plan = {
        "qkv": [(1, 0, 7)],
        3: [(1, 2, 5)],
        5: [(1, 1, 6)],
        "feed": [(1, 1, 7)],
        7: [(1, 2, 6)],
        "unfeed": [(1, 2, 7)],
    }
    for plan in (first_plan, second_plan):
        for stops in plan.values():
            stops[:] = [(spread[layer, part], until) for layer, part, until in stops]
    bring_cotangent = Move(1, cotangent, cotangent_all, False, later=True)
    second_plan[3].append((Stop(bring_cotangent.start), 0))
    clock = Clock([first_plan, second_plan])
    states = [
        lambda rows: tokens_all[rows, :].astype(F32) + temb[...],
        lambda rows: kept[0].normal2[rows, :] * norms[0, 2:3, :] + norms[0, 3:4, :],
    ]

    def forward(layer, carry):
        forward_layer(
            lambda run: either(layer, run, states),
            norms.at[layer],
            bias.at[layer],
            shut,
            all_weights.at[layer],
            Kept(kept_refs, layer),
            acc,
            partial(clock.tick, layer),
        )
        return carry

    lax.fori_loop(0, 2, forward, 0)

    def leave(rows):
        final = kept[1].normal2[rows, :] * norms[1, 2:3, :] + norms[1, 3:4, :]
        leaving[rows, :] = final.astype(BF16)

    by_rows(leave)
    give_output = Move(2, leaving, output_part, True)
    for travel in list(spread.values()) + [spread_x]:
        travel.finish()
    for trade in first:
        trade.left()
    bring_cotangent.wait()
    by_rows(lambda rows: acc.__setitem__((rows, slice(None)), cotangent_all[rows, :].astype(F32)))

    there = pl.ds(pl.multiple_of(24 * (1 - core), 8), 24)
    near = pl.ds(pl.multiple_of(24 * core, 8), 24)

    def deliver(layer, part, k, total):
        rows[...] = total
        if part == 2:
            send_b[layer, k] = rows[there, :]
            kept_b[layer, k] = rows[near, :]
            return
        for to in range(8):
            send_a[layer, to, 3 * part + k, 0:6, :] = rows[6 * to : 6 * to + 6, :]

    def deliver_extra(k, total):
        rows[0:16, :] = total
        for to in range(4):
            send_a[0, 4 * k + to, 6, 0:4, :] = rows[4 * to : 4 * to + 4, :]

    around = [moved(at, axis, by) for axis in "xyz" for by in (1, -1, 2)]
    reduce = {}

    near_by = [moved(at, axis, by) for axis in "xyz" for by in (1, -1)]

    def gone(part):
        reduce[1, part].crossed()
        for to in around:
            signal(gone_free.at[part], to)

    def wait_gone(part):
        pl.semaphore_wait(gone_free.at[part], len(around))

    def free(part):
        signal(pair_free.at[part], flipped(at, 0, 0, 1))
        for to in near_by:
            signal(ring_free.at[part], to)

    def freed(part):
        pl.semaphore_wait(pair_free.at[part], 1)
        pl.semaphore_wait(ring_free.at[part], len(near_by))

    for layer in range(2):
        for part in range(3):
            spare = weights[1].at[part, :, 1 - core, layer]
            small_buffers = [spare.at[:, pl.ds(0, 3)], spare.at[:, 3, pl.ds(0, 3)]]
            reduce[layer, part] = Reduce(
                3 * layer + part,
                weights[layer].at[part],
                [pair.at[part], half.at[part], full.at[part]] + small_buffers,
                partial(deliver, layer, part),
                at,
                reduce_sems,
                layer + part > 0,
                None if layer else partial(freed, part),
                partial(wait_gone, part) if layer else None,
            )
    reduce_x = Reduce(6, extra, buffers_x, deliver_extra, at, reduce_sems, False, None, None)

    frees = [Stop(partial(free, part)) for part in range(3)]
    gones = [Stop(partial(gone, part)) for part in range(3)]
    second = lambda part, until: (reduce[1, part], until)
    early = lambda part, until: (reduce[0, part], until)
    give = lambda part, k: (Stop(partial(reduce[1, part].trade, k)), 0)
    for part in range(3):
        reduce[1, part].done = 1
    second_plan = {
        4: [give(2, 0), give(2, 1), give(2, 2)],
        5: [give(1, 0)],
        6: [give(1, 1), second(2, 2)],
        7: [give(1, 2)],
        9: [second(1, 2), second(2, 3), (gones[2], 0)],
        11: [give(0, 0)],
        12: [give(0, 1)],
        13: [give(0, 2), second(1, 3), (gones[1], 0)],
    }
    first_plan = {
        2: [second(0, 2)],
        4: [second(2, 4), (frees[2], 0)],
        6: [early(2, 1)],
        8: [early(2, 2), second(1, 4), (frees[1], 0)],
        9: [early(1, 1), second(0, 3), (gones[0], 0), second(2, 5)],
        10: [early(1, 2), early(2, 3), second(1, 5)],
    }
    clock = Clock([second_plan, first_plan])

    def backward(index, carry):
        layer = 1 - index
        backward_layer(
            lambda run: either(layer, run, states),
            norms.at[layer],
            all_weights.at[layer],
            Kept(kept_refs, layer),
            acc,
            cotangent_all,
            turned,
            grad_norms.at[layer],
            grad_bias.at[layer],
            partial(clock.tick, index),
        )
        return carry

    lax.fori_loop(0, 2, backward, 0)

    give_output.wait()
    by_rows(lambda rows: leaving.__setitem__((rows, slice(None)), acc[rows, :].astype(BF16)))
    time_backward(extra, emb, time_pre, time_act, acc[...], grad_norms, grad_bias)
    give_grad = Stop(lambda: Move(3, leaving, grad_part, True))
    give_rows = [Stop(partial(Trade, layer, last_sems, 0, 7 - layer)) for layer in range(2)]
    rest = [
        second(0, 4), (frees[0], 0), second(2, 6), (reduce_x, 1), early(0, 1), (reduce_x, 2), early(1, 3), early(0, 2),
        early(2, 4), second(1, 6), second(0, 5), second(2, 7), (reduce_x, 3), early(1, 4), early(0, 3),
        early(2, 5), second(1, 7), second(0, 6), (reduce_x, 4), early(1, 5), (reduce_x, 5), early(0, 5),
        early(2, 6), second(0, 7), (give_rows[1], 0), (reduce_x, 6), early(1, 6), early(0, 6), (give_grad, 0),
        early(2, 7), (reduce_x, 7), early(1, 7), early(0, 7), (give_rows[0], 0),
    ]
    for travel, until in rest:
        travel.advance(until)
    for (layer, part), travel in reduce.items():
        travel.finish()
        if layer == 0:
            travel.crossed()
    reduce_x.finish()
    reduce_x.crossed()
    for give in give_rows:
        give.result.arrived()
        give.result.left()
    give_grad.result.wait()


def whole(*operands):
    vmem, anywhere = pl.BlockSpec(memory_space=pltpu.VMEM), pl.BlockSpec(memory_space=pl.ANY)
    smem = pl.BlockSpec(memory_space=pltpu.SMEM)
    dma, regular = pltpu.SemaphoreType.DMA, pltpu.SemaphoreType.REGULAR
    buffers = lambda lead, unit: [
        pltpu.VMEM(lead + shape + unit, BF16)
        for shape in ((4, 4, 4), (2, 2, 4), (2, 4, 4), (3, 4), (3,))
    ]
    scratch = [pltpu.VMEM((2, 3, 3, 2, 4, 4, 4) + UNIT, BF16)]
    scratch += [pltpu.VMEM((2,) + shape, kind) for _, shape, kind in Kept.shapes]
    scratch += [
        pltpu.VMEM((256, 768), F32),
        pltpu.VMEM((768, 256), BF16),
        pltpu.VMEM((256, 128), F32),
        pltpu.VMEM((2, 8, 768), F32),
        pltpu.VMEM((2, 1, 3072), F32),
        pltpu.VMEM((2, 4, 1, 768), F32),
        pltpu.VMEM((2, 8, 1, 384), F32),
        pltpu.VMEM((2, 2, 4, 4, 4) + EXTRA, BF16),
        pltpu.VMEM((8, 512), BF16),
        pltpu.VMEM((1, 512), F32),
        pltpu.VMEM((1, 512), F32),
        pltpu.VMEM((1, 768), F32),
        pltpu.VMEM((256, 768), BF16),
        pltpu.VMEM((256, 768), BF16),
        pltpu.VMEM((256, 768), BF16),
        pltpu.VMEM((2, 8, 7, 8, 128), F32),
        pltpu.VMEM((2, 3, 24, 128), F32),
        pltpu.VMEM((48, 128), F32),
        pltpu.VMEM((2, 24, 128), F32),
    ]
    scratch += buffers((3, 3), UNIT)[:3] + buffers((2,), EXTRA)
    scratch += [
        dma((7, SPREAD_SEMS)),
        dma((7, 2)),
        dma((7, REDUCE_SEMS)),
        dma((7, 2)),
        dma((2, 6)),
        dma((2, 4)),
        dma((4, 3)),
        regular((3,)),
        regular((3,)),
        regular((3,)),
    ]
    return pl.pallas_call(
        whole_kernel,
        out_shape=[
            jax.ShapeDtypeStruct((2, 8, 7, 8, 128), F32),
            jax.ShapeDtypeStruct((2, 3, 24, 128), F32),
            jax.ShapeDtypeStruct((2, 3, 24, 128), F32),
            jax.ShapeDtypeStruct((4, 64, 768), BF16),
            jax.ShapeDtypeStruct((4, 64, 768), BF16),
        ],
        in_specs=[smem] * 3 + [vmem] * 13 + [anywhere] * 2,
        out_specs=[vmem] * 3 + [anywhere] * 2,
        scratch_shapes=scratch,
        compiler_params=pltpu.CompilerParams(
            collective_id=1, has_side_effects=True, vmem_limit_bytes=VMEM_BYTES
        ),
        name="whole",
    )(*operands)


def finish_kernel(got_a, got_b, kept_b, output, grad, *results):
    out, grad_x, g_tin, g_bias, g_tout, g_qkv, g_out = results[:7]
    norm1_gain, norm1_bias, g_in, g_ffn_bias, g_ffn, norm2_gain, norm2_bias = results[7:]
    core = lax.rem(lax.axis_index("stream"), 2)
    out[...] = output[...]
    grad_x[...] = grad[...].astype(F32)
    for frm in range(8):
        for layer in range(2):
            for k in range(6):
                chunk = frm + 8 * (k % 3)
                into, column = (g_qkv, chunk) if chunk < 18 else (g_out, chunk - 18)
                if k >= 3:
                    into, column = g_in, chunk
                into[:, layer, 128 * column : 128 * column + 128] = got_a[layer, frm, k, 0:6, :]
        if frm < 6:
            g_tout[:, 128 * frm : 128 * frm + 128] = got_a[0, frm, 6, 0:4, :]
        elif frm == 6:
            for chunk in range(4):
                g_tin[:, 128 * chunk : 128 * chunk + 128] = got_a[0, frm, 6, chunk : chunk + 1, :]
        else:
            g_bias[...] = got_a[0, frm, 6, 0:1, 0:4]
            vectors = (norm1_gain, norm1_bias, norm2_gain, norm2_bias)
            for layer in range(2):
                here_at = slice(layer, layer + 1)
                for at, vector in enumerate(vectors):
                    lane = 8 + 32 * layer + 8 * at
                    vector[here_at, :] = got_a[0, frm, 6, 0:1, lane : lane + 6]
                lane = 72 + 24 * layer
                g_ffn_bias[here_at, :] = got_a[0, frm, 6, 0:1, lane : lane + 24]
    for layer in range(2):
        for k in range(3):
            near = pl.ds(pl.multiple_of(128 * (3 * core + k), 128), 128)
            there = pl.ds(pl.multiple_of(128 * (3 * (1 - core) + k), 128), 128)
            g_ffn[layer, :, near] = kept_b[layer, k]
            g_ffn[layer, :, there] = got_b[layer, k]


def finish(got_a, got_b, kept_b, output, grad):
    shapes = [
        (4, 64, 768),
        (4, 64, 768),
        (1, 512),
        (1, 4),
        (4, 768),
        (6, 2, 2304),
        (6, 2, 768),
        (2, 6),
        (2, 6),
        (6, 2, 3072),
        (2, 24),
        (2, 24, 768),
        (2, 6),
        (2, 6),
    ]
    vmem = pl.BlockSpec(memory_space=pltpu.VMEM)
    return pl.pallas_call(
        finish_kernel,
        out_shape=[
            jax.ShapeDtypeStruct(shape, F32 if at else BF16) for at, shape in enumerate(shapes)
        ],
        in_specs=[vmem] * 5,
        out_specs=[vmem] * len(shapes),
        compiler_params=pltpu.CompilerParams(vmem_limit_bytes=VMEM_BYTES),
        name="lay_out_results",
    )(got_a, got_b, kept_b, output, grad)


def per_device(
    tokens,
    timestep,
    src_len,
    total_len,
    time_in,
    time_bias,
    time_out,
    qkv_weight,
    out_weight,
    norm1_gain,
    norm1_bias,
    ffn_in,
    ffn_bias,
    ffn_out,
    norm2_gain,
    norm2_bias,
    cotangent,
):
    frequencies = np.exp(-math.log(10000.0) * np.arange(64) / 64)
    by_layer = lambda weight: weight.transpose(1, 0, 2)
    got = whole(
        src_len,
        total_len,
        timestep,
        jnp.asarray(np.repeat(np.tile(frequencies, 2), 4)[None, :], F32),
        by_layer(qkv_weight),
        by_layer(out_weight),
        by_layer(ffn_in),
        ffn_out,
        time_in,
        time_out,
        time_bias[None, :],
        ffn_bias,
        norm1_gain,
        norm1_bias,
        norm2_gain,
        norm2_bias,
        tokens,
        cotangent,
    )
    results = list(finish(*got))
    results[3] = results[3][0]
    for at in (5, 6, 9):
        results[at] = by_layer(results[at])
    return tuple(results)


def solution(mesh):
    in_specs = (
        P("batch", "stream", None),
        P("batch"),
        P("batch"),
        P("batch"),
        P(("batch", "stream"), None),
        P(("batch", "stream")),
        P(("batch", "stream"), None),
        P(None, ("batch", "stream"), None),
        P(None, ("batch", "stream"), None),
        P(None, ("batch", "stream")),
        P(None, ("batch", "stream")),
        P(None, ("batch", "stream"), None),
        P(None, ("batch", "stream")),
        P(None, ("batch", "stream"), None),
        P(None, ("batch", "stream")),
        P(None, ("batch", "stream")),
        P("batch", "stream", None),
    )
    out_specs = (
        P("batch", "stream", None),
        P("batch", "stream", None),
        P(("batch", "stream"), None),
        P(("batch", "stream")),
        P(("batch", "stream"), None),
        P(None, ("batch", "stream"), None),
        P(None, ("batch", "stream"), None),
        P(None, ("batch", "stream")),
        P(None, ("batch", "stream")),
        P(None, ("batch", "stream"), None),
        P(None, ("batch", "stream")),
        P(None, ("batch", "stream"), None),
        P(None, ("batch", "stream")),
        P(None, ("batch", "stream")),
    )
    return jax.shard_map(
        per_device, mesh=mesh, in_specs=in_specs, out_specs=out_specs, check_vma=False
    )
```
